32 devices in a mesh: dp: 8 (over z, x), blk: 4 (over y, core).
Axes of the slice: x: 2, y: 2, z: 4, core: 2. Of those that a mesh axis runs over, the one named last changes fastest.
Arguments:
- tokens: bfloat16 [64, 512, 1024], P('dp', 'blk'), may hold values from -6 to 6
- lengths: int32 [64], P('dp'), may hold values from 128 to 512, as said below
- teacher: bfloat16 [64, 512, 1024], P('dp', 'blk'), may hold values from -18 to 18
- out_grad: bfloat16 [64, 512, 1024], P('dp', 'blk'), may hold values from -6 to 6
- w_query: bfloat16 [1024, 1024], P(('dp', 'blk')), may hold values from -0.1875 to 0.1875
- w_key: bfloat16 [1024, 1024], P(('dp', 'blk')), may hold values from -0.1875 to 0.1875
- w_value: bfloat16 [1024, 1024], P(('dp', 'blk')), may hold values from -0.1875 to 0.1875
- w_output: bfloat16 [1024, 1024], P(('dp', 'blk')), may hold values from -1.5 to 1.5
- gain_one: bfloat16 [1024], P(('dp', 'blk')), may hold values from 0.099609375 to 1.8984375
- shift_one: bfloat16 [1024], P(('dp', 'blk')), may hold values from -3 to 3
- w_inner: bfloat16 [1024, 4096], P(('dp', 'blk')), may hold values from -0.1875 to 0.1875
- bias_inner: bfloat16 [4096], P(('dp', 'blk')), may hold values from -3 to 3
- w_outer: bfloat16 [4096, 1024], P(('dp', 'blk')), may hold values from -0.09375 to 0.09375
- bias_outer: bfloat16 [1024], P(('dp', 'blk')), may hold values from -3 to 3
- gain_two: bfloat16 [1024], P(('dp', 'blk')), may hold values from 0.099609375 to 1.8984375
- shift_two: bfloat16 [1024], P(('dp', 'blk')), may hold values from -3 to 3
Outputs:
- mse_loss: float32 [], replicated
- layer_out: bfloat16 [64, 512, 1024], P('dp', 'blk')
- grad_tokens: float32 [64, 512, 1024], P('dp', 'blk')
- grad_query: float32 [1024, 1024], P(('dp', 'blk'))
- grad_key: float32 [1024, 1024], P(('dp', 'blk'))
- grad_value: float32 [1024, 1024], P(('dp', 'blk'))
- grad_output: float32 [1024, 1024], P(('dp', 'blk'))
- grad_gain_one: float32 [1024], P(('dp', 'blk'))
- grad_shift_one: float32 [1024], P(('dp', 'blk'))
- grad_inner: float32 [1024, 4096], P(('dp', 'blk'))
- grad_bias_inner: float32 [4096], P(('dp', 'blk'))
- grad_outer: float32 [4096, 1024], P(('dp', 'blk'))
- grad_bias_outer: float32 [1024], P(('dp', 'blk'))
- grad_gain_two: float32 [1024], P(('dp', 'blk'))
- grad_shift_two: float32 [1024], P(('dp', 'blk'))
The draws below stay inside these ranges and needn't reach their ends.
Inputs may be any that keep to these rules, and one draw needn't show every extreme that they name: `lengths`: each aligned block of 8 sequences, those of one index of dp, holds one sequence of full length 512, which one drawn from the seed.
All inputs are finite; a program needn't handle non-finite values.
Results may differ from the reference program's by a relative error of at most 0.019.
Values may be sent and summed in bfloat16 or wider, within the bound.
A program may use at most 320 MiB of HBM per device.

```python
import math
import jax
import jax.numpy as jnp
from jax import lax

D = 1024
H = 16
DH = 64
FF = 4096
SEQ_DEV = 8
SEQS = 64
SLOT = 512


def draw_lengths(key, part):
    key = jax.random.fold_in(key, 7)
    key_base, key_chosen = jax.random.split(key)
    drawn = jax.random.randint(key_base, (SEQS,), SLOT // 4, SLOT // 4 + SLOT // 2)
    groups = SEQS // SEQ_DEV
    chosen = jax.random.randint(key_chosen, (groups,), 0, SEQ_DEV)
    is_full = jnp.arange(SEQS) % SEQ_DEV == jnp.repeat(chosen, SEQ_DEV)
    return jnp.where(is_full, SLOT, drawn).astype(jnp.int32)


def draw_teacher(key, part):
    key = jax.random.fold_in(key, 11)
    fraction = jnp.arange(SEQS, dtype=jnp.float32) / max(SEQS - 1, 1)
    ramp = 1.0 + 2.0 * fraction
    values = jnp.clip(jax.random.normal(key, (SEQS, SLOT, D), jnp.float32), -6.0, 6.0)
    return (values * ramp[:, None, None]).astype(jnp.bfloat16)


def shard_levels(key, dims, pieces, low, largest):
    gain, own = 1.0, jax.random.fold_in(key, 6)
    for axis_at, blocks in pieces:
        heights = jnp.exp(jax.random.uniform(jax.random.fold_in(own, axis_at), (blocks,), jnp.float32, low / len(pieces), largest / len(pieces)))
        gain = gain * jnp.repeat(heights, dims[axis_at] // blocks).reshape([-1 if axis == axis_at else 1 for axis in range(len(dims))])
    return gain


def normal_values(key, dims, width, bound, cuts=(), kind=jnp.bfloat16):
    factor_of = shard_levels(key, dims, cuts, -0.22, 0.18) if cuts else 1.0
    values = jax.random.normal(key, dims, jnp.float32) * width * factor_of
    return jnp.minimum(jnp.maximum(values, -bound), bound).astype(kind)


def setup_inputs(seed: int = 0) -> dict:
    key_of = jax.random.split(jax.random.key(seed), 17)
    tokens = normal_values(key_of[0], (SEQS, SLOT, D), 1.0, 6.0, ((0, 8), (1, 4)))
    lengths = draw_lengths(jax.random.fold_in(key_of[16], 71), 0)
    teacher = draw_teacher(jax.random.fold_in(key_of[16], 71), 0)
    out_grad = normal_values(key_of[3], (SEQS, SLOT, D), 1.0, 6.0, ((0, 8), (1, 4)))
    w_query = normal_values(key_of[4], (D, D), D ** -0.5, 0.1875, ((0, 32),))
    w_key = normal_values(key_of[5], (D, D), D ** -0.5, 0.1875, ((0, 32),))
    w_value = normal_values(key_of[6], (D, D), D ** -0.5, 0.1875, ((0, 32),))
    w_output = normal_values(key_of[7], (D, D), (D // 64) ** -0.5, 1.5, ((0, 32),))
    gain_one = jnp.clip(1.0 + 0.18 * jax.random.normal(key_of[8], (D,), jnp.float32), 0.099609375, 1.8984375).astype(jnp.bfloat16)
    shift_one = normal_values(key_of[9], (D,), 0.5, 3.0, ((0, 32),))
    w_inner = normal_values(key_of[10], (D, FF), D ** -0.5, 0.1875, ((0, 32),))
    bias_inner = normal_values(key_of[11], (FF,), 0.5, 3.0, ((0, 32),))
    w_outer = normal_values(key_of[12], (FF, D), FF ** -0.5, 0.09375, ((0, 32),))
    bias_outer = normal_values(key_of[13], (D,), 0.5, 3.0, ((0, 32),))
    gain_two = jnp.clip(1.0 + 0.18 * jax.random.normal(key_of[14], (D,), jnp.float32), 0.099609375, 1.8984375).astype(jnp.bfloat16)
    shift_two = normal_values(key_of[15], (D,), 0.5, 3.0, ((0, 32),))
    return dict(tokens=tokens, lengths=lengths, teacher=teacher, out_grad=out_grad, w_query=w_query, w_key=w_key, w_value=w_value, w_output=w_output, gain_one=gain_one, shift_one=shift_one, w_inner=w_inner, bias_inner=bias_inner, w_outer=w_outer, bias_outer=bias_outer, gain_two=gain_two, shift_two=shift_two)


@jax.custom_vjp
def low(v):
    return lax.optimization_barrier(v.astype(jnp.bfloat16)).astype(jnp.float32)

@jax.custom_vjp
def low_back(v):
    return v

def low_keep(v):
    return (low(v), None)

def low_pass(kept, grad):
    return (grad,)

def back_keep(v):
    return (v, None)

def back_low(kept, grad):
    return (low(grad),)
low.defvjp(low_keep, low_pass)
low_back.defvjp(back_keep, back_low)
highest = lax.Precision.HIGHEST

def matmul(left, right):
    return jnp.dot(left, right, precision=highest)

def layer_norm(values, gain_vec, shift_vec):
    row_mean = lax.optimization_barrier(jnp.mean(values, axis=-1, keepdims=True))
    centred = values - row_mean
    spread = lax.optimization_barrier(jnp.mean(centred * centred, axis=-1, keepdims=True))
    return centred * lax.rsqrt(spread + 1e-12) * gain_vec + shift_vec

def attend_one(queries, key_rows, values, length):
    scaling = 1.0 / math.sqrt(DH)
    query_heads = queries.reshape(SLOT, H, DH)
    key_heads = key_rows.reshape(SLOT, H, DH)
    value_heads = values.reshape(SLOT, H, DH)
    scores = jnp.einsum('qhd,khd->hqk', query_heads, key_heads, precision=highest) * scaling
    valid_keys = jnp.arange(SLOT) < length
    scores = low_back(jnp.where(valid_keys[None, None, :], scores, -1000000000.0))
    probability = low(jax.nn.softmax(scores, axis=-1))
    mixed = jnp.einsum('hqk,khd->qhd', probability, value_heads, precision=highest)
    return mixed.reshape(SLOT, D)

def forward(params, inputs, group_lengths, targets, inv_count):
    w_query, w_key, w_value, w_output, gain_one, shift_one, w_inner, bias_inner, w_outer, bias_outer, gain_two, shift_two = params
    token_rows = inputs.reshape(-1, D)
    queries = low_back(low(matmul(token_rows, w_query)))
    key_rows = low_back(low(matmul(token_rows, w_key)))
    value_rows = low_back(low(matmul(token_rows, w_value)))
    attend_block = jax.checkpoint(attend_one)

    def one_sequence(packed):
        return attend_block(packed[0], packed[1], packed[2], packed[3])
    attended = lax.map(one_sequence, (queries.reshape(-1, SLOT, D), key_rows.reshape(-1, SLOT, D), value_rows.reshape(-1, SLOT, D), group_lengths))
    mixed = low_back(low(attended.reshape(-1, D)))
    branch = low_back(matmul(mixed, w_output))
    normed = layer_norm(token_rows + branch, gain_one, shift_one)
    inner = low_back(matmul(low(normed), w_inner) + bias_inner)
    active = jax.nn.gelu(inner, approximate=False)
    outer = low_back(matmul(low(active), w_outer) + bias_outer)
    result = layer_norm(normed + outer, gain_two, shift_two)
    valid_rows = (jnp.arange(SLOT)[None, :] < group_lengths[:, None]).astype(result.dtype).reshape(-1, 1)
    deviation = result - targets.reshape(-1, D)
    loss_value = jnp.sum(deviation * deviation * valid_rows) * inv_count
    return (result, loss_value)

def add_up(earlier, later):
    return earlier + later

def reference(tokens, lengths, teacher, out_grad, w_query, w_key, w_value, w_output, gain_one, shift_one, w_inner, bias_inner, w_outer, bias_outer, gain_two, shift_two):
    params = tuple((weight.astype(jnp.float32) for weight in (w_query, w_key, w_value, w_output, gain_one, shift_one, w_inner, bias_inner, w_outer, bias_outer, gain_two, shift_two)))
    valid_count = jnp.sum(lengths).astype(jnp.float32)
    inv_count = 1.0 / (valid_count * D)
    groups = SEQS // SEQ_DEV

    def group_step(state_carry, group_block):
        grads, loss_sum = state_carry
        inputs, group_lengths, targets, cotangent = group_block
        inputs = inputs.astype(jnp.float32)
        targets = targets.astype(jnp.float32)

        def local(param_set, token_block):
            return forward(param_set, token_block, group_lengths, targets, inv_count)
        (result, loss_value), pullback = jax.vjp(local, params, inputs)
        valid_rows = (jnp.arange(SLOT)[None, :] < group_lengths[:, None]).astype(result.dtype).reshape(-1, 1)
        seed_rows = cotangent.astype(jnp.float32).reshape(-1, D) * valid_rows
        param_grads, input_grads = pullback((seed_rows, jnp.ones_like(loss_value)))
        grads = jax.tree.map(add_up, grads, param_grads)
        outputs = result.reshape(SEQ_DEV, SLOT, D).astype(jnp.bfloat16)
        return ((grads, loss_sum + loss_value), (outputs, input_grads.reshape(SEQ_DEV, SLOT, D)))
    blocks = (tokens.reshape(groups, SEQ_DEV, SLOT, D), lengths.reshape(groups, SEQ_DEV), teacher.reshape(groups, SEQ_DEV, SLOT, D), out_grad.reshape(groups, SEQ_DEV, SLOT, D))
    initial = jax.tree.map(jnp.zeros_like, params)
    (grads, loss_sum), (outputs, input_grads) = lax.scan(group_step, (initial, jnp.float32(0.0)), blocks)
    return (loss_sum, outputs.reshape(SEQS, SLOT, D), input_grads.reshape(SEQS, SLOT, D), grads[0], grads[1], grads[2], grads[3], grads[4], grads[5], grads[6], grads[7], grads[8], grads[9], grads[10], grads[11])
```

```python
import math

import jax
import jax.numpy as jnp
from jax import lax
from jax.experimental import pallas as pl
from jax.experimental.pallas import tpu as pltpu
from jax.sharding import PartitionSpec as P

ANY = pl.BlockSpec(memory_space=pl.ANY)
MESH = pl.DeviceIdType.MESH
f32 = jnp.float32
bf16 = jnp.bfloat16


class Layout:
    def __init__(self, mesh):
        dp, blk = mesh.shape["dp"], mesh.shape["blk"]
        if dp == 8 and blk == 4:
            dims = [("z", "dp", 2, 4), ("x", "dp", 1, 2), ("y", "blk", 2, 2), ("c", "blk", 1, 2)]
        else:
            dims = [("z", "dp", dp // 4, 4), ("x", "dp", 2, dp // 8), ("c", "dp", 1, 2), ("y", "blk", 1, blk)]
        self.order = [d[0] for d in dims]
        self.axis = {d[0]: d[1] for d in dims}
        self.stride = {d[0]: d[2] for d in dims}
        self.size = {d[0]: d[3] for d in dims}
        self.dims = tuple(d[3] for d in dims)
        self.blk = blk
        self.devices = dp * blk
        self.slot = {}
        count = 0
        for name in self.order:
            self.slot[name] = count
            count += self.size[name] - 1
        self.slots = count

    def here(self):
        return {
            name: lax.rem(lax.axis_index(self.axis[name]) // self.stride[name], self.size[name])
            for name in self.order
        }

    def step_to(self, here, name, distance):
        there = lax.rem(here[name] + distance, self.size[name])
        index = lax.axis_index(self.axis[name]) + (there - here[name]) * self.stride[name]
        return there, {self.axis[name]: index}

    def at(self, here, whole, changed=(), names=None):
        changed = dict(changed)
        return tuple(
            slice(None) if name in whole else changed.get(name, here[name])
            for name in (names or self.order)
        )

    def greet(self, here):
        barrier = pltpu.get_barrier_semaphore()
        count = 0
        for name in self.order:
            if self.axis[name] == "blk":
                continue
            for distance in range(1, self.size[name]):
                _, device = self.step_to(here, name, distance)
                pl.semaphore_signal(barrier, inc=1, device_id=device, device_id_type=MESH)
                count += 1
        me = lax.axis_index("blk")
        for distance in range(1, self.blk):
            pl.semaphore_signal(
                barrier, inc=1, device_id={"blk": lax.rem(me + distance, self.blk)}, device_id_type=MESH
            )
            count += 1
        pl.semaphore_wait(barrier, count)


def by_core(here, orders, make):
    if orders[0] == orders[1]:
        make(orders[0])
        return
    for core in range(2):
        @pl.when(here["c"] == core)
        def _():
            make(orders[core])


class Gather:
    stages = 5

    def __init__(self, lay, here, src, full, rows, send, recv, own, orders):
        self.lay, self.here = lay, here
        self.rows = (pl.ds(*rows),)
        self.src, self.full = src.at[self.rows], full
        self.send, self.recv, self.own = send, recv, own
        self.orders = orders

    def line(self, name, whole):
        copies = []
        place = self.full.at[self.lay.at(self.here, whole) + self.rows]
        source = self.src if not whole else place
        for distance in range(1, self.lay.size[name]):
            _, device = self.lay.step_to(self.here, name, distance)
            slot = self.lay.slot[name] + distance - 1
            copies.append(
                pltpu.make_async_remote_copy(
                    src_ref=source, dst_ref=place, send_sem=self.send.at[slot], recv_sem=self.recv.at[slot],
                    device_id=device, device_id_type=MESH,
                )
            )
        return copies

    def local(self):
        return pltpu.make_async_copy(self.src, self.full.at[self.lay.at(self.here, ()) + self.rows], self.own)

    def stage(self, k):
        if k == 1:
            self.local().wait()

        def make(order):
            lines = tuple(order) + ("c",)
            if k > 0:
                for c in self.line(lines[k - 1], lines[: k - 1]):
                    c.wait_recv()
            if k < 4:
                for c in self.line(lines[k], lines[:k]):
                    c.start()

        if k == 0:
            self.local().start()
        by_core(self.here, self.orders, make)

    def drain(self):
        def make(order):
            lines = tuple(order) + ("c",)
            for k in range(4):
                for c in self.line(lines[k], lines[:k]):
                    c.wait_send()
        by_core(self.here, self.orders, make)


class Resplit:
    def __init__(self, lay, src, dst, send, recv, own, back=False):
        self.lay, self.src, self.dst = lay, src, dst
        self.send, self.recv, self.own = send, recv, own
        self.me = lax.axis_index("blk")
        self.back = back
        self.seqs = (src if back else dst).shape[0]
        self.span = (dst if back else src).shape[1]

    def ends(self, there):
        if self.back:
            return (self.src.at[:, pl.ds(there * self.span, self.span)],
                    self.dst.at[pl.ds(self.me * self.seqs, self.seqs)])
        return (self.src.at[pl.ds(there * self.seqs, self.seqs)],
                self.dst.at[:, pl.ds(self.me * self.span, self.span)])

    def copies(self):
        out = []
        for distance in range(1, self.lay.blk):
            there = lax.rem(self.me + distance, self.lay.blk)
            src, dst = self.ends(there)
            out.append(
                pltpu.make_async_remote_copy(
                    src_ref=src, dst_ref=dst,
                    send_sem=self.send.at[distance - 1], recv_sem=self.recv.at[distance - 1],
                    device_id={"blk": there}, device_id_type=MESH,
                )
            )
        return out

    def local(self):
        src, dst = self.ends(self.me)
        return pltpu.make_async_copy(src, dst, self.own)

    def start(self):
        self.local().start()
        for c in self.copies():
            c.start()

    def finish(self):
        self.local().wait()
        for c in self.copies():
            c.wait()


class Scatter:
    stages = 5

    def __init__(self, lay, here, grad, out, rows, bufs, send, recv, own, orders):
        self.lay, self.here, self.grad = lay, here, grad
        self.rows = (pl.ds(*rows),)
        self.out = out.at[self.rows]
        self.held, self.recvs = bufs[0], bufs[1:]
        self.send, self.recv, self.own = send, recv, own
        self.orders = orders
        self.names = [n for n in lay.order if n != "c"]

    @staticmethod
    def buffers(lay, shard, orders):
        shape, dtype = tuple(shard.shape), shard.dtype
        names = [n for n in lay.order if n != "c"]
        out = [pltpu.VMEM(tuple(lay.size[n] for n in names) + shape, dtype)]
        out.append(pltpu.VMEM(tuple(lay.size[n] for n in names) + shape, dtype))
        for k in range(3):
            lines = orders[0][k + 1 :]
            left = tuple(lay.size[n] for n in names if n in lines)
            out.append(pltpu.VMEM((lay.size[orders[0][k]] - 1,) + left + shape, dtype))
        return out

    def local(self):
        return pltpu.make_async_copy(
            self.grad.at[self.lay.at(self.here, self.names) + self.rows], self.held, self.own)

    def core(self):
        there, device = self.lay.step_to(self.here, "c", 1)
        slot = self.lay.slot["c"]
        return pltpu.make_async_remote_copy(
            src_ref=self.grad.at[self.lay.at(self.here, self.names, {"c": there}) + self.rows], dst_ref=self.recvs[0],
            send_sem=self.send.at[slot], recv_sem=self.recv.at[slot], device_id=device, device_id_type=MESH)

    def line(self, order, k):
        name, left = order[k], order[k + 1 :]
        copies = []
        for distance in range(1, self.lay.size[name]):
            there, device = self.lay.step_to(self.here, name, distance)
            slot = self.lay.slot[name] + distance - 1
            copies.append(
                pltpu.make_async_remote_copy(
                    src_ref=self.held.at[self.lay.at(self.here, left, {name: there}, self.names)],
                    dst_ref=self.recvs[k + 1].at[distance - 1],
                    send_sem=self.send.at[slot], recv_sem=self.recv.at[slot],
                    device_id=device, device_id_type=MESH,
                )
            )
        return copies

    def add(self, order, k):
        left = [n for n in self.names if k < 0 or n in order[k + 1 :]]
        sizes = [self.lay.size[n] for n in left]
        total = 1
        for s in sizes:
            total *= s
        buf = self.recvs[k + 1]
        many = 1 if k < 0 else self.lay.size[order[k]] - 1

        def one(i, carry):
            index, rest = {}, i
            for n, s in reversed(list(zip(left, sizes))):
                index[n] = lax.rem(rest, s)
                rest = rest // s
            mine = tuple(index.get(n, self.here[n]) for n in self.names)
            theirs = tuple(index[n] for n in left)
            value = self.held[mine].astype(f32)
            for d in range(many):
                at = theirs if k < 0 else (d,) + theirs
                value = value + buf[at].astype(f32)
            if k == 2:
                self.out[...] = value
            else:
                self.held[mine] = value.astype(self.held.dtype)
            return carry

        lax.fori_loop(0, total, one, 0)

    def stage(self, k):
        if k == 0:
            self.core().start()
            self.local().start()
            return
        if k == 1:
            self.local().wait()
            self.core().wait_recv()
            self.add(None, -1)

        def make(order):
            if k > 1:
                for c in self.line(order, k - 2):
                    c.wait_recv()
                self.add(order, k - 2)
            if k < 4:
                for c in self.line(order, k - 1):
                    c.start()

        by_core(self.here, self.orders, make)

    def drain(self):
        self.core().wait_send()

        def make(order):
            for k in range(3):
                for c in self.line(order, k):
                    c.wait_send()

        by_core(self.here, self.orders, make)


def skewed(parts, stages=5):
    for t in range(len(parts) + stages - 1):
        for i, part in enumerate(parts):
            if 0 <= t - i < stages:
                part.stage(t - i)
    for part in parts:
        part.drain()


def sems(lay, n, m):
    dma = pltpu.SemaphoreType.DMA
    n, m = max(n, 1), max(m, 1)
    return [dma((n, lay.slots)), dma((n, lay.slots)), dma((n,)), dma((m, lay.blk - 1)), dma((m, lay.blk - 1)), dma((m,))]


def gather_call(lay, shards, parts, rows, cid):
    n, m, p = len(shards), len(rows), len(parts)

    def kernel(*refs):
        ins, refs = refs[: n + m], refs[n + m :]
        outs, refs = refs[: n + m], refs[n + m :]
        send, recv, own, rsend, rrecv, rown = refs
        here = lay.here()
        lay.greet(here)
        gathers = [
            Gather(lay, here, ins[a], outs[a], (r, c), send.at[i], recv.at[i], own.at[i], orders)
            for i, (a, r, c, orders) in enumerate(parts)
        ]
        splits = [Resplit(lay, ins[n + i], outs[n + i], rsend.at[i], rrecv.at[i], rown.at[i]) for i in range(m)]
        for s in splits:
            s.start()
        skewed(gathers)
        for s in splits:
            s.finish()

    outs = [jax.ShapeDtypeStruct(lay.dims + s.shape, s.dtype) for s in shards]
    outs += [
        jax.ShapeDtypeStruct((r.shape[0] // lay.blk, r.shape[1] * lay.blk, r.shape[2]), r.dtype) for r in rows
    ]
    return pl.pallas_call(
        kernel, out_shape=outs, in_specs=[ANY] * (n + m), out_specs=[ANY] * (n + m),
        scratch_shapes=sems(lay, p, m),
        compiler_params=pltpu.CompilerParams(collective_id=cid, has_side_effects=True),
        name=f"gather_{cid}",
    )(*shards, *rows)


def scatter_call(lay, grads, parts, rows, cid):
    n, m, p = len(grads), len(rows), len(parts)
    bufs = [
        Scatter.buffers(lay, jax.ShapeDtypeStruct((c,) + grads[a].shape[2:], grads[a].dtype), orders)
        for a, r, c, orders in parts
    ]

    def kernel(*refs):
        ins, refs = refs[: n + m], refs[n + m :]
        outs, refs = refs[: n + m], refs[n + m :]
        own_bufs = []
        for _ in parts:
            own_bufs.append(refs[:5])
            refs = refs[5:]
        send, recv, own, rsend, rrecv, rown = refs
        here = lay.here()
        lay.greet(here)
        sums = [
            Scatter(lay, here, ins[a], outs[a], (r, c), own_bufs[i], send.at[i], recv.at[i], own.at[i], orders)
            for i, (a, r, c, orders) in enumerate(parts)
        ]
        splits = [
            Resplit(lay, ins[n + i], outs[n + i], rsend.at[i], rrecv.at[i], rown.at[i], True) for i in range(m)
        ]
        for s in splits:
            s.start()
        skewed(sums)
        for s in splits:
            s.finish()

    outs = [jax.ShapeDtypeStruct(g.shape[1:], f32) for g in grads]
    outs += [
        jax.ShapeDtypeStruct((r.shape[0] * lay.blk, r.shape[1] // lay.blk, r.shape[2]), r.dtype) for r in rows
    ]
    grads = [g.reshape(lay.dims + g.shape[1:]) for g in grads]
    return pl.pallas_call(
        kernel, out_shape=outs, in_specs=[ANY] * (n + m),
        out_specs=[pl.BlockSpec(memory_space=pltpu.VMEM)] * n + [ANY] * m,
        scratch_shapes=[b for bs in bufs for b in bs] + sems(lay, p, m),
        compiler_params=pltpu.CompilerParams(
            collective_id=cid, has_side_effects=True, vmem_limit_bytes=60 << 20),
        name=f"scatter_{cid}",
    )(*grads, *rows)


DH = 64
LOG2E = math.log2(math.e)
GROUP = 256


def dot(a, b):
    return lax.dot_general(a, b, (((1,), (0,)), ((), ())), preferred_element_type=f32)


def dot_t(a, b):
    return lax.dot_general(a, b, (((1,), (1,)), ((), ())), preferred_element_type=f32)


def once(shape):
    return pl.BlockSpec(shape, lambda *_: (0,) * len(shape), pipeline_mode=pl.Buffered(1))


def attention_forward(x, lengths, wq, wk, wv, wo):
    rows, width = x.shape
    seqs = lengths.shape[0]
    span = rows // seqs
    groups = width // GROUP
    scale = LOG2E / math.sqrt(DH)

    def kernel(len_ref, x_ref, wq_ref, wk_ref, wv_ref, wo_ref, q_ref, k_ref, v_ref, att_ref, lse_ref, h1_ref):
        g = pl.program_id(0)
        xv = x_ref[...]
        q_ref[...] = dot(xv, wq_ref[...]).astype(bf16)
        k_ref[...] = dot(xv, wk_ref[...]).astype(bf16)
        v_ref[...] = dot(xv, wv_ref[...]).astype(bf16)

        def pair_step(i, carry):
            s, pair = i // 2, lax.rem(i, 2)
            at = (pl.ds(pl.multiple_of(s * span, span), span), pl.ds(pl.multiple_of(pair * 128, 128), 128))
            length = len_ref[s]
            qs, ks, vs = q_ref[at], k_ref[at], v_ref[at]
            lane = lax.broadcasted_iota(jnp.int32, (span, 128), 1)
            keep = lax.broadcasted_iota(jnp.int32, (span, 1), 0) < length
            vt = vs.T
            outs, lses = [], []
            for h in range(2):
                km = jnp.where((lane < DH) if h == 0 else (lane >= DH), ks, jnp.zeros_like(ks))
                st = dot_t(km, qs) * scale
                st = jnp.where(keep, st, -1e30)
                top = jnp.max(st, axis=0, keepdims=True)
                p = jnp.exp2(st - top)
                den = jnp.sum(p, axis=0, keepdims=True)
                ot = dot(vt[h * DH : (h + 1) * DH], p.astype(bf16))
                outs.append(ot * (1.0 / den))
                lses.append(top + jnp.log2(den))
            att_ref[at] = jnp.concatenate(outs, axis=0).T.astype(bf16)
            lse_ref[0, pl.ds(i * 2, 1)] = lses[0]
            lse_ref[0, pl.ds(i * 2 + 1, 1)] = lses[1]
            return carry

        lax.fori_loop(0, seqs * GROUP // 128, pair_step, 0)

        @pl.when(g == 0)
        def _():
            h1_ref[...] = x_ref[...].astype(f32)

        h1_ref[...] += dot(att_ref[...], wo_ref[...])

    col = pl.BlockSpec((width, GROUP), lambda g, *_: (0, g))
    act = pl.BlockSpec((rows, GROUP), lambda g, *_: (0, g))
    heads = seqs * GROUP // DH
    return pl.pallas_call(
        kernel,
        grid_spec=pltpu.PrefetchScalarGridSpec(
            num_scalar_prefetch=1,
            grid=(groups,),
            in_specs=[once((rows, width)), col, col, col, pl.BlockSpec((GROUP, width), lambda g, *_: (g, 0))],
            out_specs=[act, act, act, act, pl.BlockSpec((1, heads, span), lambda g, *_: (g, 0, 0)), once((rows, width))],
        ),
        out_shape=[jax.ShapeDtypeStruct((rows, width), bf16)] * 4
        + [jax.ShapeDtypeStruct((groups, heads, span), f32), jax.ShapeDtypeStruct((rows, width), f32)],
        compiler_params=pltpu.CompilerParams(vmem_limit_bytes=60 << 20),
        name="attention_forward",
    )(lengths, x, wq, wk, wv, wo)


def attention_backward(x, lengths, wq, wk, wv, wo, q, k, v, att, lse, d_branch, d_one):
    rows, width = x.shape
    seqs = lengths.shape[0]
    span = rows // seqs
    groups = width // GROUP
    scale = LOG2E / math.sqrt(DH)

    def kernel(
        len_ref, x_ref, wq_ref, wk_ref, wv_ref, wo_ref, q_ref, k_ref, v_ref, att_ref, lse_ref, db_ref, d1_ref,
        gq_ref, gk_ref, gv_ref, go_ref, dx_ref, xt_ref, do_ref, dq_ref, dk_ref, dv_ref, acc_ref,
    ):
        g = pl.program_id(0)

        @pl.when(g == 0)
        def _():
            xt_ref[...] = x_ref[...].T
            acc_ref[...] = d1_ref[...]

        db = db_ref[...]
        do_ref[...] = dot_t(db, wo_ref[...]).astype(bf16)
        go_ref[...] = dot(att_ref[...].T, db).astype(bf16)

        def pair_step(i, carry):
            s, pair = i // 2, lax.rem(i, 2)
            at = (pl.ds(pl.multiple_of(s * span, span), span), pl.ds(pl.multiple_of(pair * 128, 128), 128))
            length = len_ref[s]
            qs, ks, vs, dos = q_ref[at], k_ref[at], v_ref[at], do_ref[at]
            lane = lax.broadcasted_iota(jnp.int32, (span, 128), 1)
            keep = lax.broadcasted_iota(jnp.int32, (span, 1), 0) < length
            kt = ks.T
            dqs, dks, dvs = [], [], []
            for h in range(2):
                mine = (lane < DH) if h == 0 else (lane >= DH)
                zero = jnp.zeros_like(ks)
                st = dot_t(jnp.where(mine, ks, zero), qs) * scale
                p = jnp.where(keep, jnp.exp2(st - lse_ref[0, pl.ds(i * 2 + h, 1)]), 0.0)
                dp = dot_t(jnp.where(mine, vs, zero), dos)
                delta = jnp.sum(p * dp, axis=0, keepdims=True)
                ds = (p * (dp - delta)).astype(bf16)
                dvs.append(dot(p.astype(bf16), dos))
                dks.append(dot(ds, qs))
                dqs.append(dot(kt[h * DH : (h + 1) * DH], ds))
            first = lane < DH
            unit = 1.0 / math.sqrt(DH)
            dv_ref[at] = jnp.where(first, dvs[0], dvs[1]).astype(bf16)
            dk_ref[at] = (jnp.where(first, dks[0], dks[1]) * unit).astype(bf16)
            dq_ref[at] = (jnp.concatenate(dqs, axis=0).T * unit).astype(bf16)
            return carry

        lax.fori_loop(0, seqs * GROUP // 128, pair_step, 0)
        xt = xt_ref[...]
        gq_ref[...] = dot(xt, dq_ref[...]).astype(bf16)
        gk_ref[...] = dot(xt, dk_ref[...]).astype(bf16)
        gv_ref[...] = dot(xt, dv_ref[...]).astype(bf16)

        acc_ref[...] += (
            dot_t(dq_ref[...], wq_ref[...]) + dot_t(dk_ref[...], wk_ref[...]) + dot_t(dv_ref[...], wv_ref[...])
        )

        @pl.when(g == groups - 1)
        def _():
            dx_ref[...] = acc_ref[...].astype(bf16)

    col = pl.BlockSpec((width, GROUP), lambda g, *_: (0, g))
    row = pl.BlockSpec((GROUP, width), lambda g, *_: (g, 0))
    act = pl.BlockSpec((rows, GROUP), lambda g, *_: (0, g))
    heads = seqs * GROUP // DH
    full = once((rows, width))
    return pl.pallas_call(
        kernel,
        grid_spec=pltpu.PrefetchScalarGridSpec(
            num_scalar_prefetch=1,
            grid=(groups,),
            in_specs=[full, col, col, col, row, act, act, act, act,
                      pl.BlockSpec((1, heads, span), lambda g, *_: (g, 0, 0)), full, full],
            out_specs=[col, col, col, row, full],
            scratch_shapes=[pltpu.VMEM((width, rows), bf16)] + [pltpu.VMEM((rows, GROUP), bf16)] * 4
            + [pltpu.VMEM((rows, width), f32)],
        ),
        out_shape=[jax.ShapeDtypeStruct((width, width), bf16)] * 4 + [jax.ShapeDtypeStruct((rows, width), bf16)],
        compiler_params=pltpu.CompilerParams(vmem_limit_bytes=60 << 20),
        name="attention_backward",
    )(lengths, x, wq, wk, wv, wo, q, k, v, att, lse, d_branch, d_one)


TILE = 512
CHUNK = 256


def feed_forward(h1, teacher, out_grad, lengths, inv_count, vecs, bias_inner, w1, w2, devices):
    rows, width = h1.shape
    hidden = w1.shape[1]
    seqs = lengths.shape[0]
    span = rows // seqs
    tiles = hidden // TILE
    share = hidden // devices
    per_tile = TILE // share
    wide = share % 128 == 0

    def kernel(
        len_ref, inv_ref, h1_ref, teach_ref, og_ref, vec_ref, b1_ref, w1_ref, w2_ref,
        out_ref, d1_ref, db_ref, gw1_ref, gw2_ref, sums_ref, gb1_ref,
        low_ref, lowt_ref, act_ref, slope_ref, acc_ref, do_ref, dot_ref, inv1_ref, di_ref,
    ):
        t = pl.program_id(0)
        gain1, shift1 = vec_ref[0:1], vec_ref[1:2]
        bias2, gain2, shift2 = vec_ref[2:3], vec_ref[3:4], vec_ref[4:5]

        @pl.when(t == 0)
        def _():
            sums_ref[...] = jnp.zeros_like(sums_ref)

            def norm(i, carry):
                at = pl.ds(pl.multiple_of(i * 128, 128), 128)
                h = h1_ref[at]
                centred = h - jnp.mean(h, axis=-1, keepdims=True)
                inverse = lax.rsqrt(jnp.mean(centred * centred, axis=-1, keepdims=True) + 1e-12)
                normal = centred * inverse
                d1_ref[at] = normal
                inv1_ref[at] = inverse
                low = (normal * gain1 + shift1).astype(bf16)
                low_ref[at] = low
                lowt_ref[:, at] = low.T
                return carry

            lax.fori_loop(0, rows // 128, norm, 0)
            acc_ref[...] = jnp.zeros_like(acc_ref)

        @pl.when(t < tiles)
        def _():
            for i in range(rows // CHUNK):
                at = slice(i * CHUNK, (i + 1) * CHUNK)
                inner = dot(low_ref[at], w1_ref[...]) + b1_ref[...]
                cum = 0.5 * (1.0 + lax.erf(inner * (1.0 / math.sqrt(2.0))))
                density = jnp.exp(-0.5 * inner * inner) * (1.0 / math.sqrt(2.0 * math.pi))
                active = (inner * cum).astype(bf16)
                act_ref[t, at] = active
                slope_ref[t, at] = (cum + inner * density).astype(bf16)
                acc_ref[at] += dot(active, w2_ref[...])

        @pl.when(t == tiles)
        def _():
            inv = inv_ref[0]

            def middle(i, carry):
                at = pl.ds(pl.multiple_of(i * 128, 128), 128)
                normed = d1_ref[at] * gain1 + shift1
                h2 = normed + acc_ref[at] + bias2
                centred = h2 - jnp.mean(h2, axis=-1, keepdims=True)
                inverse = lax.rsqrt(jnp.mean(centred * centred, axis=-1, keepdims=True) + 1e-12)
                normal = centred * inverse
                result = normal * gain2 + shift2
                out_ref[at] = result.astype(bf16)
                seq = (i * 128) // span
                pos = i * 128 - seq * span + lax.broadcasted_iota(jnp.int32, (128, 1), 0)
                valid = (pos < len_ref[seq]).astype(f32)
                deviation = (result - teach_ref[at].astype(f32)) * valid
                grad = og_ref[at].astype(f32) * valid + (2.0 * inv) * deviation
                sums_ref[0:1] += jnp.sum(deviation * deviation, axis=0, keepdims=True)
                sums_ref[1:2] += jnp.sum(grad * normal, axis=0, keepdims=True)
                sums_ref[2:3] += jnp.sum(grad, axis=0, keepdims=True)
                scaled = grad * gain2
                mean = jnp.mean(scaled, axis=-1, keepdims=True)
                along = jnp.mean(scaled * normal, axis=-1, keepdims=True)
                d_two = inverse * (scaled - mean - normal * along)
                acc_ref[at] = d_two
                low = d_two.astype(bf16)
                sums_ref[3:4] += jnp.sum(low.astype(f32), axis=0, keepdims=True)
                do_ref[at] = low
                dot_ref[:, at] = low.T
                return carry

            lax.fori_loop(0, rows // 128, middle, 0)

        @pl.when(t > tiles)
        def _():
            j = t - tiles - 1
            total = jnp.zeros((1, TILE), f32)
            for i in range(rows // CHUNK):
                at = slice(i * CHUNK, (i + 1) * CHUNK)
                d_act = dot_t(do_ref[at], w2_ref[...])
                d_in = (d_act * slope_ref[j, at].astype(f32)).astype(bf16)
                total += jnp.sum(d_in.astype(f32), axis=0, keepdims=True)
                di_ref[at] = d_in
                acc_ref[at] += dot_t(d_in, w1_ref[...])
            gb1_ref[...] = total
            gw1_ref[...] = dot(lowt_ref[...], di_ref[...]).astype(bf16)
            gw2 = dot(dot_ref[...], act_ref[j]).astype(bf16)
            if wide:
                for d in range(per_tile):
                    gw2_ref[d] = gw2[:, d * share : (d + 1) * share]
            else:
                gw2_ref[...] = gw2

        @pl.when(t == 2 * tiles)
        def _():
            def back(i, carry):
                at = pl.ds(pl.multiple_of(i * 128, 128), 128)
                grad, normal = acc_ref[at], d1_ref[at]
                sums_ref[4:5] += jnp.sum(grad * normal, axis=0, keepdims=True)
                sums_ref[5:6] += jnp.sum(grad, axis=0, keepdims=True)
                scaled = grad * gain1
                mean = jnp.mean(scaled, axis=-1, keepdims=True)
                along = jnp.mean(scaled * normal, axis=-1, keepdims=True)
                d_one = inv1_ref[at] * (scaled - mean - normal * along)
                d1_ref[at] = d_one
                db_ref[at] = d_one.astype(bf16)
                return carry

            lax.fori_loop(0, rows // 128, back, 0)

    def tile(t, *_):
        return jnp.where(t < tiles, t, jnp.maximum(t - tiles - 1, 0))

    def back_tile(t, *_):
        return jnp.maximum(t - tiles - 1, 0)

    full = once((rows, width))
    vec = pl.BlockSpec((1, TILE), lambda t, *_: (0, tile(t)))
    return pl.pallas_call(
        kernel,
        grid_spec=pltpu.PrefetchScalarGridSpec(
            num_scalar_prefetch=2,
            grid=(2 * tiles + 1,),
            in_specs=[
                full, full, full, once((8, width)), vec,
                pl.BlockSpec((width, TILE), lambda t, *_: (0, tile(t))),
                pl.BlockSpec((TILE, width), lambda t, *_: (tile(t), 0)),
            ],
            out_specs=[
                full, full, full,
                pl.BlockSpec((width, TILE), lambda t, *_: (0, back_tile(t))),
                pl.BlockSpec((per_tile, width, share), lambda t, *_: (back_tile(t), 0, 0))
                if wide else pl.BlockSpec((width, TILE), lambda t, *_: (0, back_tile(t))),
                once((8, width)),
                pl.BlockSpec((1, TILE), lambda t, *_: (0, back_tile(t))),
            ],
            scratch_shapes=[
                pltpu.VMEM((rows, width), bf16), pltpu.VMEM((width, rows), bf16),
                pltpu.VMEM((tiles, rows, TILE), bf16), pltpu.VMEM((tiles, rows, TILE), bf16),
                pltpu.VMEM((rows, width), f32), pltpu.VMEM((rows, width), bf16), pltpu.VMEM((width, rows), bf16),
                pltpu.VMEM((rows, 1), f32), pltpu.VMEM((rows, TILE), bf16),
            ],
        ),
        out_shape=[
            jax.ShapeDtypeStruct((rows, width), bf16),
            jax.ShapeDtypeStruct((rows, width), f32),
            jax.ShapeDtypeStruct((rows, width), bf16),
            jax.ShapeDtypeStruct((width, hidden), bf16),
            jax.ShapeDtypeStruct((devices, width, share) if wide else (width, hidden), bf16),
            jax.ShapeDtypeStruct((8, width), f32),
            jax.ShapeDtypeStruct((1, hidden), f32),
        ],
        compiler_params=pltpu.CompilerParams(vmem_limit_bytes=63 << 20),
        name="feed_forward",
    )(lengths, inv_count, h1, teacher, out_grad, vecs, bias_inner, w1, w2)


def cut(shape, which, pieces, orders):
    rows = shape[0]
    while pieces > 1 and rows % (pieces * 16):
        pieces -= 1
    step = rows // pieces
    return [(which, i * step, step, orders) for i in range(pieces)]


def shards(
    lay, tokens, lengths, teacher, out_grad, w_query, w_key, w_value, w_output, gain_one, shift_one,
    w_inner, bias_inner, w_outer, bias_outer, gain_two, shift_two,
):
    width = tokens.shape[2]
    hidden = w_inner.shape[1]
    devices = lay.devices
    there = (("z", "x", "y"), ("z", "y", "x"))
    back = (("y", "x", "z"), ("x", "y", "z"))
    share, deep = gain_one.shape[0], bias_inner.shape[0]

    small = jnp.concatenate(
        [v.astype(f32) for v in (gain_one, shift_one, bias_outer, gain_two, shift_two, bias_inner)]
        + [jnp.sum(lengths).astype(f32)[None]]
    )
    used = 5 * share + deep
    pack = jnp.pad(small, (0, 1024 - small.shape[0])).reshape(8, 128)
    ins = [w_query, w_key, w_value, w_output]
    parts = [(4, 0, 8, there)]
    for i, w in enumerate(ins):
        parts += cut(w.shape, i, 1, there)
    wq, wk, wv, wo, packs, x = gather_call(lay, ins + [pack], parts, [tokens], 1)
    parts = cut(w_inner.shape, 0, 2, there) + cut(w_outer.shape, 1, 2, there)
    w1, w2, teach, given = gather_call(lay, [w_inner, w_outer], parts, [teacher, out_grad], 2)
    wq, wk, wv, wo = (w.reshape(width, width) for w in (wq, wk, wv, wo))
    w1, w2 = w1.reshape(width, hidden), w2.reshape(hidden, width)
    packs = packs.reshape(devices, 1024)
    vecs = packs[:, : 5 * share].reshape(devices, 5, share).transpose(1, 0, 2).reshape(5, width)
    vecs = jnp.pad(vecs, ((0, 3), (0, 0)))
    bias1 = packs[:, 5 * share : used].reshape(1, hidden)
    inv_count = 1.0 / (jnp.sum(packs[:, used]) / lay.blk * width)

    seqs = x.shape[0]
    own = lax.dynamic_slice(lengths, (lax.axis_index("blk") * seqs,), (seqs,))
    x = x.reshape(-1, width)
    q, k, v, att, lse, h1 = attention_forward(x, own, wq, wk, wv, wo)
    out, d_one, d_branch, gw1, gw2, sums, gb1 = feed_forward(
        h1, teach.reshape(-1, width), given.reshape(-1, width), own, inv_count[None], vecs, bias1, w1, w2, devices
    )
    gq, gk, gv, go, dx = attention_backward(x, own, wq, wk, wv, wo, q, k, v, att, lse, d_branch, d_one)

    span = lambda a: a.reshape(seqs, -1, width)
    by_device = lambda a: a.reshape((devices, a.shape[0] // devices) + a.shape[1:])
    gw1 = by_device(gw1)
    turned = gw2.ndim == 3
    if not turned:
        gw2 = by_device(gw2.T)
    parts = cut(gw1.shape[1:], 0, 2, back) + cut(gw2.shape[1:], 1, 2, back)
    g_inner, g_outer, layer_out = scatter_call(lay, [gw1, gw2], parts, [span(out)], 3)
    loss = jnp.broadcast_to(jnp.sum(sums[0])[None, None], (devices, 1))
    vec_sums = sums[1:6].reshape(5, devices, share).transpose(1, 0, 2).reshape(devices, 5 * share)
    small = jnp.concatenate([vec_sums, gb1.reshape(devices, deep), loss], axis=1)
    small = jnp.pad(small, ((0, 0), (0, 1024 - small.shape[1]))).reshape(devices, 8, 128)
    grads = [by_device(g) for g in (gq, gk, gv, go)] + [small]
    parts = [(4, 0, 8, back)]
    for i in range(4):
        parts += cut(grads[i].shape[1:], i, 1, back)
    g_query, g_key, g_value, g_output, small, d_tokens = scatter_call(lay, grads, parts, [span(dx)], 4)
    small = small.reshape(1024)
    vec = lambda i: small[i * share : (i + 1) * share]
    return (
        small[used] * inv_count,
        layer_out,
        d_tokens.astype(f32),
        g_query,
        g_key,
        g_value,
        g_output,
        vec(3),
        vec(4),
        g_inner,
        small[5 * share : used],
        g_outer.T if turned else g_outer,
        vec(2),
        vec(0),
        vec(1),
    )


def solution(mesh):
    lay = Layout(mesh)
    rows = P("dp", "blk", None)
    weight = P(("dp", "blk"), None)
    vector = P(("dp", "blk"))
    return jax.shard_map(
        lambda *args: shards(lay, *args),
        mesh=mesh,
        in_specs=(
            rows, P("dp"), rows, rows, weight, weight, weight, weight, vector, vector,
            weight, vector, weight, vector, vector, vector,
        ),
        out_specs=(
            P(), rows, rows, weight, weight, weight, weight, vector, vector,
            weight, vector, weight, vector, vector, vector,
        ),
        check_vma=False,
    )
```

```python
import math

import jax
import jax.numpy as jnp
from jax import lax
from jax.experimental import pallas as pl
from jax.experimental.pallas import tpu as pltpu
from jax.sharding import PartitionSpec as P

ANY = pl.BlockSpec(memory_space=pl.ANY)
MESH = pl.DeviceIdType.MESH
f32 = jnp.float32
bf16 = jnp.bfloat16


class Layout:
    def __init__(self, mesh):
        dp, blk = mesh.shape["dp"], mesh.shape["blk"]
        if dp == 8 and blk == 4:
            dims = [("z", "dp", 2, 4), ("x", "dp", 1, 2), ("y", "blk", 2, 2), ("c", "blk", 1, 2)]
        else:
            dims = [("z", "dp", dp // 4, 4), ("x", "dp", 2, dp // 8), ("c", "dp", 1, 2), ("y", "blk", 1, blk)]
        self.order = [d[0] for d in dims]
        self.axis = {d[0]: d[1] for d in dims}
        self.stride = {d[0]: d[2] for d in dims}
        self.size = {d[0]: d[3] for d in dims}
        self.dims = tuple(d[3] for d in dims)
        self.blk = blk
        self.devices = dp * blk
        self.slot = {}
        count = 0
        for name in self.order:
            self.slot[name] = count
            count += self.size[name] - 1
        self.slots = count

    def here(self):
        return {
            name: lax.rem(lax.axis_index(self.axis[name]) // self.stride[name], self.size[name])
            for name in self.order
        }

    def step_to(self, here, name, distance):
        there = lax.rem(here[name] + distance, self.size[name])
        index = lax.axis_index(self.axis[name]) + (there - here[name]) * self.stride[name]
        return there, {self.axis[name]: index}

    def at(self, here, whole, changed=(), names=None):
        changed = dict(changed)
        return tuple(
            slice(None) if name in whole else changed.get(name, here[name])
            for name in (names or self.order)
        )

    def place(self, device):
        index = []
        for size in reversed(self.dims):
            index.append(lax.rem(device, size))
            device = device // size
        return tuple(reversed(index))

    def greet(self, here):
        barrier = pltpu.get_barrier_semaphore()
        count = 0
        for name in self.order:
            if self.axis[name] == "blk":
                continue
            for distance in range(1, self.size[name]):
                _, device = self.step_to(here, name, distance)
                pl.semaphore_signal(barrier, inc=1, device_id=device, device_id_type=MESH)
                count += 1
        me = lax.axis_index("blk")
        for distance in range(1, self.blk):
            pl.semaphore_signal(
                barrier, inc=1, device_id={"blk": lax.rem(me + distance, self.blk)}, device_id_type=MESH
            )
            count += 1
        pl.semaphore_wait(barrier, count)


def window(cut):
    if len(cut) == 2:
        return (pl.ds(*cut),)
    return (pl.ds(cut[0], cut[1]), pl.ds(cut[2], cut[3]))


def by_core(here, orders, make):
    if orders[0] == orders[1]:
        make(orders[0])
        return
    for core in range(2):
        @pl.when(here["c"] == core)
        def _():
            make(orders[core])


class Gather:
    stages = 5

    def __init__(self, lay, here, src, full, rows, send, recv, own, orders):
        self.lay, self.here = lay, here
        self.rows = window(rows)
        self.src, self.full = src.at[self.rows], full
        self.send, self.recv, self.own = send, recv, own
        self.orders = orders

    def line(self, name, whole):
        copies = []
        place = self.full.at[self.lay.at(self.here, whole) + self.rows]
        source = self.src if not whole else place
        for distance in range(1, self.lay.size[name]):
            _, device = self.lay.step_to(self.here, name, distance)
            slot = self.lay.slot[name] + distance - 1
            copies.append(
                pltpu.make_async_remote_copy(
                    src_ref=source, dst_ref=place, send_sem=self.send.at[slot], recv_sem=self.recv.at[slot],
                    device_id=device, device_id_type=MESH,
                )
            )
        return copies

    def local(self):
        return pltpu.make_async_copy(self.src, self.full.at[self.lay.at(self.here, ()) + self.rows], self.own)

    def stage(self, k):
        if k == 1:
            self.local().wait()

        def make(order):
            lines = tuple(order) + ("c",)
            if k > 0:
                for c in self.line(lines[k - 1], lines[: k - 1]):
                    c.wait_recv()
            if k < 4:
                for c in self.line(lines[k], lines[:k]):
                    c.start()

        if k == 0:
            self.local().start()
        by_core(self.here, self.orders, make)

    def drain(self):
        def make(order):
            lines = tuple(order) + ("c",)
            for k in range(4):
                for c in self.line(lines[k], lines[:k]):
                    c.wait_send()
        by_core(self.here, self.orders, make)


class Resplit:
    def __init__(self, lay, src, dst, send, recv, own, back=False):
        self.lay, self.src, self.dst = lay, src, dst
        self.send, self.recv, self.own = send, recv, own
        self.me = lax.axis_index("blk")
        self.back = back
        self.seqs = (src if back else dst).shape[0]
        self.span = (dst if back else src).shape[1]

    def ends(self, there):
        if self.back:
            return (self.src.at[:, pl.ds(there * self.span, self.span)],
                    self.dst.at[pl.ds(self.me * self.seqs, self.seqs)])
        return (self.src.at[pl.ds(there * self.seqs, self.seqs)],
                self.dst.at[:, pl.ds(self.me * self.span, self.span)])

    def copies(self):
        out = []
        for distance in range(1, self.lay.blk):
            there = lax.rem(self.me + distance, self.lay.blk)
            src, dst = self.ends(there)
            out.append(
                pltpu.make_async_remote_copy(
                    src_ref=src, dst_ref=dst,
                    send_sem=self.send.at[distance - 1], recv_sem=self.recv.at[distance - 1],
                    device_id={"blk": there}, device_id_type=MESH,
                )
            )
        return out

    def local(self):
        src, dst = self.ends(self.me)
        return pltpu.make_async_copy(src, dst, self.own)

    def start(self):
        self.local().start()
        for c in self.copies():
            c.start()

    def finish(self):
        self.local().wait()
        for c in self.copies():
            c.wait()


class Scatter:
    stages = 5

    def __init__(self, lay, here, grad, out, rows, bufs, send, recv, own, orders):
        self.lay, self.here, self.grad = lay, here, grad
        self.rows = window(rows)
        self.out = out.at[self.rows]
        self.held, self.recvs = bufs[0], bufs[1:]
        self.send, self.recv, self.own = send, recv, own
        self.orders = orders
        self.names = [n for n in lay.order if n != "c"]

    @staticmethod
    def buffers(lay, grad, cut, orders):
        dtype = grad.dtype
        shape = (cut[1], cut[3] if len(cut) == 4 else grad.shape[-1])
        names = [n for n in lay.order if n != "c"]
        out = [pltpu.VMEM(tuple(lay.size[n] for n in names) + shape, dtype)]
        out.append(pltpu.VMEM(tuple(lay.size[n] for n in names) + shape, dtype))
        for k in range(3):
            lines = orders[0][k + 1 :]
            left = tuple(lay.size[n] for n in names if n in lines)
            out.append(pltpu.VMEM((lay.size[orders[0][k]] - 1,) + left + shape, dtype))
        return out

    def local(self):
        return pltpu.make_async_copy(
            self.grad.at[self.lay.at(self.here, self.names) + self.rows], self.held, self.own)

    def core(self):
        there, device = self.lay.step_to(self.here, "c", 1)
        slot = self.lay.slot["c"]
        return pltpu.make_async_remote_copy(
            src_ref=self.grad.at[self.lay.at(self.here, self.names, {"c": there}) + self.rows], dst_ref=self.recvs[0],
            send_sem=self.send.at[slot], recv_sem=self.recv.at[slot], device_id=device, device_id_type=MESH)

    def line(self, order, k):
        name, left = order[k], order[k + 1 :]
        copies = []
        for distance in range(1, self.lay.size[name]):
            there, device = self.lay.step_to(self.here, name, distance)
            slot = self.lay.slot[name] + distance - 1
            copies.append(
                pltpu.make_async_remote_copy(
                    src_ref=self.held.at[self.lay.at(self.here, left, {name: there}, self.names)],
                    dst_ref=self.recvs[k + 1].at[distance - 1],
                    send_sem=self.send.at[slot], recv_sem=self.recv.at[slot],
                    device_id=device, device_id_type=MESH,
                )
            )
        return copies

    def add(self, order, k):
        left = [n for n in self.names if k < 0 or n in order[k + 1 :]]
        sizes = [self.lay.size[n] for n in left]
        total = 1
        for s in sizes:
            total *= s
        buf = self.recvs[k + 1]
        many = 1 if k < 0 else self.lay.size[order[k]] - 1

        def one(i, carry):
            index, rest = {}, i
            for n, s in reversed(list(zip(left, sizes))):
                index[n] = lax.rem(rest, s)
                rest = rest // s
            mine = tuple(index.get(n, self.here[n]) for n in self.names)
            theirs = tuple(index[n] for n in left)
            value = self.held[mine].astype(f32)
            for d in range(many):
                at = theirs if k < 0 else (d,) + theirs
                value = value + buf[at].astype(f32)
            if k == 2:
                self.out[...] = value
            else:
                self.held[mine] = value.astype(self.held.dtype)
            return carry

        lax.fori_loop(0, total, one, 0)

    def stage(self, k):
        if k == 0:
            self.core().start()
            self.local().start()
            return
        if k == 1:
            self.local().wait()
            self.core().wait_recv()
            self.add(None, -1)

        def make(order):
            if k > 1:
                for c in self.line(order, k - 2):
                    c.wait_recv()
                self.add(order, k - 2)
            if k < 4:
                for c in self.line(order, k - 1):
                    c.start()

        by_core(self.here, self.orders, make)

    def drain(self):
        self.core().wait_send()

        def make(order):
            for k in range(3):
                for c in self.line(order, k):
                    c.wait_send()

        by_core(self.here, self.orders, make)


def skewed(parts, lag=1, stages=5):
    events = []
    for t in range(len(parts) + lag * (stages - 1)):
        for i, part in enumerate(parts):
            stage, rest = divmod(t - i, lag)
            if rest == 0 and 0 <= stage < stages:
                events.append((part, stage))
    return events


def run(parts, lag=2):
    for part, stage in skewed(parts, lag):
        part.stage(stage)
    for part in parts:
        part.drain()


class Hooks:
    def __init__(self, events, steps, first=0):
        self.slots = {}
        room = max(steps - first, 1)
        for n, event in enumerate(events):
            self.slots.setdefault(first + n * room // max(len(events), 1), []).append(event)

    def at(self, step):
        for k, events in self.slots.items():
            @pl.when(step == k)
            def _():
                for part, stage in events:
                    part.stage(stage)


def sems(lay, n, m):
    dma = pltpu.SemaphoreType.DMA
    n, m = max(n, 1), max(m, 1)
    return [dma((n, lay.slots)), dma((n, lay.slots)), dma((n,)), dma((m, lay.blk - 1)), dma((m, lay.blk - 1)), dma((m,))]


def scatter_call(lay, grads, parts, rows, cid):
    n, m, p = len(grads), len(rows), len(parts)
    bufs = [
        Scatter.buffers(lay, grads[a], cut, orders)
        for a, cut, orders in parts
    ]

    def kernel(*refs):
        ins, refs = refs[: n + m], refs[n + m :]
        outs, refs = refs[: n + m], refs[n + m :]
        own_bufs = []
        for _ in parts:
            own_bufs.append(refs[:5])
            refs = refs[5:]
        send, recv, own, rsend, rrecv, rown = refs
        here = lay.here()
        lay.greet(here)
        sums = [
            Scatter(lay, here, ins[a], outs[a], cut, own_bufs[i], send.at[i], recv.at[i], own.at[i], orders)
            for i, (a, cut, orders) in enumerate(parts)
        ]
        splits = [
            Resplit(lay, ins[n + i], outs[n + i], rsend.at[i], rrecv.at[i], rown.at[i], True) for i in range(m)
        ]
        for s in splits:
            s.start()
        run(sums)
        for s in splits:
            s.finish()

    outs = [jax.ShapeDtypeStruct(g.shape[1:], f32) for g in grads]
    outs += [
        jax.ShapeDtypeStruct((r.shape[0] * lay.blk, r.shape[1] // lay.blk, r.shape[2]), r.dtype) for r in rows
    ]
    grads = [g.reshape(lay.dims + g.shape[1:]) for g in grads]
    return pl.pallas_call(
        kernel, out_shape=outs, in_specs=[ANY] * (n + m),
        out_specs=[pl.BlockSpec(memory_space=pltpu.VMEM)] * n + [ANY] * m,
        scratch_shapes=[b for bs in bufs for b in bs] + sems(lay, p, m),
        compiler_params=pltpu.CompilerParams(
            collective_id=cid, has_side_effects=True, vmem_limit_bytes=60 << 20),
        name=f"scatter_{cid}",
    )(*grads, *rows)


DH = 64
LOG2E = math.log2(math.e)
GROUP = 256


def dot(a, b):
    return lax.dot_general(a, b, (((1,), (0,)), ((), ())), preferred_element_type=f32)


def dot_t(a, b):
    return lax.dot_general(a, b, (((1,), (1,)), ((), ())), preferred_element_type=f32)


def once(shape):
    return pl.BlockSpec(shape, lambda *_: (0,) * len(shape), pipeline_mode=pl.Buffered(1))


def attention_forward(lay, tokens, lengths, shards, parts, early):
    width = tokens.shape[2]
    seqs, span = tokens.shape[0] // lay.blk, tokens.shape[1] * lay.blk
    rows = seqs * span
    groups = width // GROUP
    scale = LOG2E / math.sqrt(DH)
    heads = seqs * GROUP // DH
    pairs = seqs * GROUP // 128
    n, p = len(shards), len(parts)

    def kernel(len_ref, tok_ref, *refs):
        ins, refs = refs[:n], refs[n:]
        fulls, refs = refs[:n], refs[n:]
        x_out, q_out, k_out, v_out, att_out, lse_ref, h1_out = refs[:7]
        x_ref, wq_ref, wk_ref, wv_ref, wo_ref, q_ref, k_ref, v_ref, att_ref, h1_ref = refs[7:17]
        load, send, recv, own, rsend, rrecv, rown = refs[17:]
        here = lay.here()
        lay.greet(here)
        split = Resplit(lay, tok_ref, x_out, rsend, rrecv, rown)
        split.start()
        gathers = [
            Gather(lay, here, ins[a], fulls[a], cut, send.at[i], recv.at[i], own.at[i], orders)
            for i, (a, cut, orders) in enumerate(parts)
        ]
        events = skewed(gathers, 2)
        last = max(i for i, (part, stage) in enumerate(events) if part in gathers[:early] and stage == 4)
        for part, stage in events[: last + 1]:
            part.stage(stage)
        split.finish()
        loads = [
            pltpu.make_async_copy(src, dst, load.at[i])
            for i, (src, dst) in enumerate(
                zip([x_out] + list(fulls[:4]), [x_ref, wq_ref, wk_ref, wv_ref, wo_ref]))
        ]
        for c in loads:
            c.start()
        for c in loads:
            c.wait()
        hooks = Hooks(events[last + 1 :], groups * pairs)
        base = lax.axis_index("blk") * seqs

        def columns(ref, g):
            block = ref[(slice(None),) * 5 + (pl.ds(pl.multiple_of(g * GROUP, GROUP), GROUP),)]
            return block.reshape(width, GROUP)

        def features(ref, g):
            per = GROUP // ref.shape[-2]
            return jnp.concatenate([ref[lay.place(g * per + j)] for j in range(per)], axis=0)

        def step(i, carry):
            g, r = i // pairs, lax.rem(i, pairs)
            cols = pl.ds(pl.multiple_of(g * GROUP, GROUP), GROUP)

            @pl.when(r == 0)
            def _():
                xv = x_ref[...].reshape(rows, width)
                q_ref[:, cols] = dot(xv, columns(wq_ref, g)).astype(bf16)
                k_ref[:, cols] = dot(xv, columns(wk_ref, g)).astype(bf16)
                v_ref[:, cols] = dot(xv, columns(wv_ref, g)).astype(bf16)

            s, pair = r // (GROUP // 128), lax.rem(r, GROUP // 128)
            at = (pl.ds(pl.multiple_of(s * span, span), span),
                  pl.ds(pl.multiple_of(g * GROUP + pair * 128, 128), 128))
            qs, ks, vs = q_ref[at], k_ref[at], v_ref[at]
            lane = lax.broadcasted_iota(jnp.int32, (span, 128), 1)
            keep = lax.broadcasted_iota(jnp.int32, (span, 1), 0) < len_ref[base + s]
            vt = vs.T
            outs = []
            for h in range(2):
                km = jnp.where((lane < DH) if h == 0 else (lane >= DH), ks, jnp.zeros_like(ks))
                st = dot_t(km, qs) * scale
                st = jnp.where(keep, st, -1e30)
                top = jnp.max(st, axis=0, keepdims=True)
                e = jnp.exp2(st - top)
                den = jnp.sum(e, axis=0, keepdims=True)
                ot = dot(vt[h * DH : (h + 1) * DH], e.astype(bf16))
                outs.append(ot * (1.0 / den))
                lse_ref[g, pl.ds(r * 2 + h, 1)] = top + jnp.log2(den)
            att_ref[at] = jnp.concatenate(outs, axis=0).T.astype(bf16)

            @pl.when(r == pairs - 1)
            def _():
                add = dot(att_ref[:, cols], features(wo_ref, g))

                @pl.when(g == 0)
                def _():
                    h1_ref[...] = x_ref[...].reshape(rows, width).astype(f32) + add

                @pl.when(g > 0)
                def _():
                    h1_ref[...] += add

            hooks.at(i)
            return carry

        lax.fori_loop(0, groups * pairs, step, 0)
        saves = [
            pltpu.make_async_copy(src, dst, load.at[i])
            for i, (src, dst) in enumerate(
                zip([q_ref, k_ref, v_ref, att_ref, h1_ref], [q_out, k_out, v_out, att_out, h1_out]))
        ]
        for c in saves:
            c.start()
        for g in gathers:
            g.drain()
        for c in saves:
            c.wait()

    whole = [jax.ShapeDtypeStruct(lay.dims + s.shape, s.dtype) for s in shards]
    act = jax.ShapeDtypeStruct((rows, width), bf16)
    return pl.pallas_call(
        kernel,
        in_specs=[pl.BlockSpec(memory_space=pltpu.SMEM)] + [ANY] * (n + 1),
        out_specs=[ANY] * (n + 5) + [pl.BlockSpec(memory_space=pltpu.VMEM), ANY],
        out_shape=whole
        + [jax.ShapeDtypeStruct((seqs, span, width), bf16), act, act, act, act,
           jax.ShapeDtypeStruct((groups, heads, span), f32), jax.ShapeDtypeStruct((rows, width), f32)],
        scratch_shapes=[pltpu.VMEM((seqs, span, width), bf16)]
        + [pltpu.VMEM(lay.dims + s.shape, bf16) for s in shards[:4]]
        + [pltpu.VMEM((rows, width), bf16)] * 4
        + [pltpu.VMEM((rows, width), f32), pltpu.SemaphoreType.DMA((5,))]
        + sems(lay, p, 0)[:3]
        + [pltpu.SemaphoreType.DMA((lay.blk - 1,)), pltpu.SemaphoreType.DMA((lay.blk - 1,)),
           pltpu.SemaphoreType.DMA],
        compiler_params=pltpu.CompilerParams(collective_id=1, has_side_effects=True, vmem_limit_bytes=60 << 20),
        name="attention_forward",
    )(lengths, tokens, *shards)


def attention_backward(lay, x, lengths, wq, wk, wv, wo, q, k, v, att, lse, d_branch, d_one, grads, parts):
    rows, width = x.shape
    seqs, heads, span = lse.shape[1] * DH // GROUP, lse.shape[1], lse.shape[2]
    groups = width // GROUP
    pairs = seqs * GROUP // 128
    scale = LOG2E / math.sqrt(DH)
    bufs = [Scatter.buffers(lay, grads[a], cut, orders) for a, cut, orders in parts]
    n = len(grads)
    grads = [g.reshape(lay.dims + g.shape[1:]) for g in grads]

    def kernel(*refs):
        ins, refs = refs[13 : 13 + n], refs[:13] + refs[13 + n :]
        outs, refs = refs[18 : 18 + n], refs[:18] + refs[18 + n :]
        *own_bufs, send, recv, own, d1_sem = refs[24:]
        body(ins, outs, own_bufs, send, recv, own, d1_sem, *refs[:24])

    def body(
        ins, outs, own_bufs, send, recv, own, d1_sem, len_ref, x_ref, wq_ref, wk_ref, wv_ref, wo_ref, q_ref, k_ref, v_ref, att_ref, lse_ref, db_ref, d1_ref,
        gq_ref, gk_ref, gv_ref, go_ref, dx_ref, xt_ref, do_ref, dq_ref, dk_ref, dv_ref, acc_ref,
    ):
        g = pl.program_id(0)
        here = lay.here()
        sums = [
            Scatter(lay, here, ins[a], outs[a], cut, own_bufs[5 * i : 5 * i + 5], send.at[i], recv.at[i], own.at[i], orders)
            for i, (a, cut, orders) in enumerate(parts)
        ]
        events = skewed(sums, 2)
        hooks = Hooks(events[1:], groups * pairs)
        base = lax.axis_index("blk") * seqs

        @pl.when(g == 0)
        def _():
            lay.greet(here)
            events[0][0].stage(0)
            fetch = pltpu.make_async_copy(d1_ref, acc_ref, d1_sem)
            fetch.start()
            xt_ref[...] = x_ref[...].T
            fetch.wait()

        db = db_ref[...]
        do_ref[...] = dot_t(db, wo_ref[...]).astype(bf16)
        go_ref[...] = dot(att_ref[...].T, db).astype(bf16)

        def pair_step(i, carry):
            s, pair = i // 2, lax.rem(i, 2)
            at = (pl.ds(pl.multiple_of(s * span, span), span), pl.ds(pl.multiple_of(pair * 128, 128), 128))
            length = len_ref[base + s]
            qs, ks, vs, dos = q_ref[at], k_ref[at], v_ref[at], do_ref[at]
            lane = lax.broadcasted_iota(jnp.int32, (span, 128), 1)
            keep = lax.broadcasted_iota(jnp.int32, (span, 1), 0) < length
            kt = ks.T
            dqs, dks, dvs = [], [], []
            for h in range(2):
                mine = (lane < DH) if h == 0 else (lane >= DH)
                zero = jnp.zeros_like(ks)
                st = dot_t(jnp.where(mine, ks, zero), qs) * scale
                p = jnp.where(keep, jnp.exp2(st - lse_ref[0, pl.ds(i * 2 + h, 1)]), 0.0)
                dp = dot_t(jnp.where(mine, vs, zero), dos)
                delta = jnp.sum(p * dp, axis=0, keepdims=True)
                ds = (p * (dp - delta)).astype(bf16)
                dvs.append(dot(p.astype(bf16), dos))
                dks.append(dot(ds, qs))
                dqs.append(dot(kt[h * DH : (h + 1) * DH], ds))
            first = lane < DH
            unit = 1.0 / math.sqrt(DH)
            dv_ref[at] = jnp.where(first, dvs[0], dvs[1]).astype(bf16)
            dk_ref[at] = (jnp.where(first, dks[0], dks[1]) * unit).astype(bf16)
            dq_ref[at] = (jnp.concatenate(dqs, axis=0).T * unit).astype(bf16)
            hooks.at(g * pairs + i)
            return carry

        lax.fori_loop(0, pairs, pair_step, 0)
        xt = xt_ref[...]
        gq_ref[...] = dot(xt, dq_ref[...]).astype(bf16)
        gk_ref[...] = dot(xt, dk_ref[...]).astype(bf16)
        gv_ref[...] = dot(xt, dv_ref[...]).astype(bf16)

        acc_ref[...] += (
            dot_t(dq_ref[...], wq_ref[...]) + dot_t(dk_ref[...], wk_ref[...]) + dot_t(dv_ref[...], wv_ref[...])
        )

        @pl.when(g == groups - 1)
        def _():
            dx_ref[...] = acc_ref[...].astype(bf16)
            for part in sums:
                part.drain()

    col = pl.BlockSpec((width, GROUP), lambda g, *_: (0, g))
    row = pl.BlockSpec((GROUP, width), lambda g, *_: (g, 0))
    act = pl.BlockSpec((rows, GROUP), lambda g, *_: (0, g))
    full = once((rows, width))
    return pl.pallas_call(
        kernel,
        grid_spec=pltpu.PrefetchScalarGridSpec(
            num_scalar_prefetch=0,
            grid=(groups,),
            in_specs=[pl.BlockSpec(memory_space=pltpu.SMEM), full, col, col, col, row, act, act, act, act,
                      pl.BlockSpec((1, heads, span), lambda g, *_: (g, 0, 0)), full, ANY] + [ANY] * n,
            out_specs=[col, col, col, row, full] + [pl.BlockSpec(memory_space=pltpu.VMEM)] * n,
            scratch_shapes=[pltpu.VMEM((width, rows), bf16)] + [pltpu.VMEM((rows, GROUP), bf16)] * 4
            + [pltpu.VMEM((rows, width), f32)]
            + [b for bs in bufs for b in bs] + sems(lay, len(parts), 0)[:3] + [pltpu.SemaphoreType.DMA],
        ),
        out_shape=[jax.ShapeDtypeStruct((width, width), bf16)] * 4 + [jax.ShapeDtypeStruct((rows, width), bf16)]
        + [jax.ShapeDtypeStruct(g.shape[-2:], f32) for g in grads],
        compiler_params=pltpu.CompilerParams(
            collective_id=3, has_side_effects=True, vmem_limit_bytes=63 << 20),
        name="attention_backward",
    )(lengths, x, wq, wk, wv, wo, q, k, v, att, lse, d_branch, d_one, *grads)


TILE = 512
CHUNK = 256


def feed_forward(lay, h1, teacher, out_grad, lengths, inv_count, vecs, bias_inner, w1, w2):
    rows, width = h1.shape
    hidden = w1.shape[1]
    seqs = teacher.shape[0] // lay.blk
    span = rows // seqs
    devices = lay.devices
    tiles = hidden // TILE
    share = hidden // devices
    per_tile = TILE // share
    wide = share % 128 == 0

    def kernel(
        len_ref, inv_ref, h1_ref, teach_in, og_in, vec_ref, b1_ref, w1_ref, w2_ref,
        layer_out, d1_ref, db_ref, gw1_ref, gw2_ref, sums_ref, gb1_ref,
        low_ref, lowt_ref, act_ref, slope_ref, acc_ref, do_ref, dot_ref, inv1_ref, di_ref,
        teach_ref, og_ref, out_ref, send, recv, own,
    ):
        t = pl.program_id(0)
        base = lax.axis_index("blk") * seqs
        splits = [
            Resplit(lay, src, dst, send.at[i], recv.at[i], own.at[i], i == 2)
            for i, (src, dst) in enumerate(((teach_in, teach_ref), (og_in, og_ref), (out_ref, layer_out)))
        ]
        gain1, shift1 = vec_ref[0:1], vec_ref[1:2]
        bias2, gain2, shift2 = vec_ref[2:3], vec_ref[3:4], vec_ref[4:5]

        @pl.when(t == 0)
        def _():
            lay.greet(lay.here())
            splits[0].start()
            splits[1].start()
            sums_ref[...] = jnp.zeros_like(sums_ref)

            def norm(i, carry):
                at = pl.ds(pl.multiple_of(i * 128, 128), 128)
                h = h1_ref[at]
                centred = h - jnp.mean(h, axis=-1, keepdims=True)
                inverse = lax.rsqrt(jnp.mean(centred * centred, axis=-1, keepdims=True) + 1e-12)
                normal = centred * inverse
                d1_ref[at] = normal
                inv1_ref[at] = inverse
                low = (normal * gain1 + shift1).astype(bf16)
                low_ref[at] = low
                lowt_ref[:, at] = low.T
                return carry

            lax.fori_loop(0, rows // 128, norm, 0)
            acc_ref[...] = jnp.zeros_like(acc_ref)

        @pl.when(t < tiles)
        def _():
            for i in range(rows // CHUNK):
                at = slice(i * CHUNK, (i + 1) * CHUNK)
                inner = dot(low_ref[at], w1_ref[...]) + b1_ref[...]
                cum = 0.5 * (1.0 + lax.erf(inner * (1.0 / math.sqrt(2.0))))
                density = jnp.exp(-0.5 * inner * inner) * (1.0 / math.sqrt(2.0 * math.pi))
                active = (inner * cum).astype(bf16)
                act_ref[t, at] = active
                slope_ref[t, at] = (cum + inner * density).astype(bf16)
                acc_ref[at] += dot(active, w2_ref[...])

        @pl.when(t == tiles)
        def _():
            inv = inv_ref[0]
            splits[0].finish()
            splits[1].finish()

            def middle(i, carry):
                at = pl.ds(pl.multiple_of(i * 128, 128), 128)
                normed = d1_ref[at] * gain1 + shift1
                h2 = normed + acc_ref[at] + bias2
                centred = h2 - jnp.mean(h2, axis=-1, keepdims=True)
                inverse = lax.rsqrt(jnp.mean(centred * centred, axis=-1, keepdims=True) + 1e-12)
                normal = centred * inverse
                result = normal * gain2 + shift2
                seq = (i * 128) // span
                first = i * 128 - seq * span
                there = (seq, pl.ds(pl.multiple_of(first, 128), 128))
                out_ref[there] = result.astype(bf16)
                pos = first + lax.broadcasted_iota(jnp.int32, (128, 1), 0)
                valid = (pos < len_ref[base + seq]).astype(f32)
                deviation = (result - teach_ref[there].astype(f32)) * valid
                grad = og_ref[there].astype(f32) * valid + (2.0 * inv) * deviation
                sums_ref[0:1] += jnp.sum(deviation * deviation, axis=0, keepdims=True)
                sums_ref[1:2] += jnp.sum(grad * normal, axis=0, keepdims=True)
                sums_ref[2:3] += jnp.sum(grad, axis=0, keepdims=True)
                scaled = grad * gain2
                mean = jnp.mean(scaled, axis=-1, keepdims=True)
                along = jnp.mean(scaled * normal, axis=-1, keepdims=True)
                d_two = inverse * (scaled - mean - normal * along)
                acc_ref[at] = d_two
                low = d_two.astype(bf16)
                sums_ref[3:4] += jnp.sum(low.astype(f32), axis=0, keepdims=True)
                do_ref[at] = low
                dot_ref[:, at] = low.T
                return carry

            lax.fori_loop(0, rows // 128, middle, 0)
            splits[2].start()

        @pl.when(t > tiles)
        def _():
            j = t - tiles - 1
            total = jnp.zeros((1, TILE), f32)
            for i in range(rows // CHUNK):
                at = slice(i * CHUNK, (i + 1) * CHUNK)
                d_act = dot_t(do_ref[at], w2_ref[...])
                d_in = (d_act * slope_ref[j, at].astype(f32)).astype(bf16)
                total += jnp.sum(d_in.astype(f32), axis=0, keepdims=True)
                di_ref[at] = d_in
                acc_ref[at] += dot_t(d_in, w1_ref[...])
            gb1_ref[...] = total
            gw1_ref[...] = dot(lowt_ref[...], di_ref[...]).astype(bf16)
            gw2 = dot(dot_ref[...], act_ref[j]).astype(bf16)
            if wide:
                for d in range(per_tile):
                    gw2_ref[d] = gw2[:, d * share : (d + 1) * share]
            else:
                gw2_ref[...] = gw2

        @pl.when(t == 2 * tiles)
        def _():
            def back(i, carry):
                at = pl.ds(pl.multiple_of(i * 128, 128), 128)
                grad, normal = acc_ref[at], d1_ref[at]
                sums_ref[4:5] += jnp.sum(grad * normal, axis=0, keepdims=True)
                sums_ref[5:6] += jnp.sum(grad, axis=0, keepdims=True)
                scaled = grad * gain1
                mean = jnp.mean(scaled, axis=-1, keepdims=True)
                along = jnp.mean(scaled * normal, axis=-1, keepdims=True)
                d_one = inv1_ref[at] * (scaled - mean - normal * along)
                d1_ref[at] = d_one
                db_ref[at] = d_one.astype(bf16)
                return carry

            lax.fori_loop(0, rows // 128, back, 0)
            splits[2].finish()

    def tile(t, *_):
        return jnp.where(t < tiles, t, jnp.maximum(t - tiles - 1, 0))

    def back_tile(t, *_):
        return jnp.maximum(t - tiles - 1, 0)

    full = once((rows, width))
    vec = pl.BlockSpec((1, TILE), lambda t, *_: (0, tile(t)))
    return pl.pallas_call(
        kernel,
        grid_spec=pltpu.PrefetchScalarGridSpec(
            num_scalar_prefetch=0,
            grid=(2 * tiles + 1,),
            in_specs=[
                pl.BlockSpec(memory_space=pltpu.SMEM), pl.BlockSpec(memory_space=pltpu.SMEM),
                full, ANY, ANY, once((8, width)), vec,
                pl.BlockSpec((width, TILE), lambda t, *_: (0, tile(t))),
                pl.BlockSpec((TILE, width), lambda t, *_: (tile(t), 0)),
            ],
            out_specs=[
                ANY, full, full,
                pl.BlockSpec((width, TILE), lambda t, *_: (0, back_tile(t))),
                pl.BlockSpec((per_tile, width, share), lambda t, *_: (back_tile(t), 0, 0))
                if wide else pl.BlockSpec((width, TILE), lambda t, *_: (0, back_tile(t))),
                once((8, width)),
                pl.BlockSpec((1, TILE), lambda t, *_: (0, back_tile(t))),
            ],
            scratch_shapes=[
                pltpu.VMEM((rows, width), bf16), pltpu.VMEM((width, rows), bf16),
                pltpu.VMEM((tiles, rows, TILE), bf16), pltpu.VMEM((tiles, rows, TILE), bf16),
                pltpu.VMEM((rows, width), f32), pltpu.VMEM((rows, width), bf16), pltpu.VMEM((width, rows), bf16),
                pltpu.VMEM((rows, 1), f32), pltpu.VMEM((rows, TILE), bf16),
            ]
            + [pltpu.VMEM((seqs, span, width), bf16)] * 3
            + sems(lay, 0, 3)[3:],
        ),
        out_shape=[
            jax.ShapeDtypeStruct(teacher.shape, bf16),
            jax.ShapeDtypeStruct((rows, width), f32),
            jax.ShapeDtypeStruct((rows, width), bf16),
            jax.ShapeDtypeStruct((width, hidden), bf16),
            jax.ShapeDtypeStruct((devices, width, share) if wide else (width, hidden), bf16),
            jax.ShapeDtypeStruct((8, width), f32),
            jax.ShapeDtypeStruct((1, hidden), f32),
        ],
        compiler_params=pltpu.CompilerParams(
            collective_id=2, has_side_effects=True, vmem_limit_bytes=63 << 20),
        name="feed_forward",
    )(lengths, inv_count, h1, teacher, out_grad, vecs, bias_inner, w1, w2)

def cut(shape, which, pieces, orders, columns=False):
    rows, wide = shape
    if columns:
        step = wide // pieces
        return [(which, (0, rows, i * step, step), orders) for i in range(pieces)]
    while pieces > 1 and rows % (pieces * 16):
        pieces -= 1
    step = rows // pieces
    return [(which, (i * step, step), orders) for i in range(pieces)]


def shards(
    lay, tokens, lengths, teacher, out_grad, w_query, w_key, w_value, w_output, gain_one, shift_one,
    w_inner, bias_inner, w_outer, bias_outer, gain_two, shift_two,
):
    width = tokens.shape[2]
    hidden = w_inner.shape[1]
    devices = lay.devices
    there = (("z", "x", "y"), ("z", "y", "x"))
    back = (("y", "x", "z"), ("x", "y", "z"))
    share, deep = gain_one.shape[0], bias_inner.shape[0]

    small = jnp.concatenate(
        [v.astype(f32) for v in (gain_one, shift_one, bias_outer, gain_two, shift_two, bias_inner)]
        + [jnp.sum(lengths).astype(f32)[None]]
    )
    used = 5 * share + deep
    pack = jnp.pad(small, (0, 1024 - small.shape[0])).reshape(8, 128)
    ins = [w_query, w_key, w_value, w_output, pack, w_inner, w_outer]
    parts = [(4, (0, 8), there)]
    for i in range(4):
        parts += cut(ins[i].shape, i, 1, there)
    early = len(parts)
    parts += cut(w_inner.shape, 5, 4, there, True) + cut(w_outer.shape, 6, 4, there)
    wq, wk, wv, wo, packs, w1, w2, x, q, k, v, att, lse, h1 = attention_forward(
        lay, tokens, lengths, ins, parts, early
    )
    wq, wk, wv, wo = (w.reshape(width, width) for w in (wq, wk, wv, wo))
    w1, w2 = w1.reshape(width, hidden), w2.reshape(hidden, width)
    packs = packs.reshape(devices, 1024)
    vecs = packs[:, : 5 * share].reshape(devices, 5, share).transpose(1, 0, 2).reshape(5, width)
    vecs = jnp.pad(vecs, ((0, 3), (0, 0)))
    bias1 = packs[:, 5 * share : used].reshape(1, hidden)
    inv_count = 1.0 / (jnp.sum(packs[:, used]) / lay.blk * width)

    seqs = x.shape[0]
    x = x.reshape(-1, width)
    layer_out, d_one, d_branch, gw1, gw2, sums, gb1 = feed_forward(
        lay, h1, teacher, out_grad, lengths, inv_count[None], vecs, bias1, w1, w2
    )
    by_device = lambda a: a.reshape((devices, a.shape[0] // devices) + a.shape[1:])
    gw1 = by_device(gw1)
    turned = gw2.ndim == 3
    if not turned:
        gw2 = by_device(gw2.T)
    parts = cut(gw1.shape[1:], 0, 4, back, True) + cut(gw2.shape[1:], 1, 4, back)
    gq, gk, gv, go, dx, g_inner, g_outer = attention_backward(
        lay, x, lengths, wq, wk, wv, wo, q, k, v, att, lse, d_branch, d_one, [gw1, gw2], parts
    )
    loss = jnp.broadcast_to(jnp.sum(sums[0])[None, None], (devices, 1))
    vec_sums = sums[1:6].reshape(5, devices, share).transpose(1, 0, 2).reshape(devices, 5 * share)
    small = jnp.concatenate([vec_sums, gb1.reshape(devices, deep), loss], axis=1)
    small = jnp.pad(small, ((0, 0), (0, 1024 - small.shape[1]))).reshape(devices, 8, 128)
    grads = [by_device(g) for g in (gq, gk, gv, go)] + [small]
    parts = [(4, (0, 8), back)]
    for i in range(4):
        parts += cut(grads[i].shape[1:], i, 1, back)
    g_query, g_key, g_value, g_output, small, d_tokens = scatter_call(lay, grads, parts, [dx.reshape(seqs, -1, width)], 4)
    small = small.reshape(1024)
    vec = lambda i: small[i * share : (i + 1) * share]
    return (
        small[used] * inv_count,
        layer_out,
        d_tokens.astype(f32),
        g_query,
        g_key,
        g_value,
        g_output,
        vec(3),
        vec(4),
        g_inner,
        small[5 * share : used],
        g_outer.T if turned else g_outer,
        vec(2),
        vec(0),
        vec(1),
    )


def solution(mesh):
    lay = Layout(mesh)
    rows = P("dp", "blk", None)
    weight = P(("dp", "blk"), None)
    vector = P(("dp", "blk"))
    return jax.shard_map(
        lambda *args: shards(lay, *args),
        mesh=mesh,
        in_specs=(
            rows, P("dp"), rows, rows, weight, weight, weight, weight, vector, vector,
            weight, vector, weight, vector, vector, vector,
        ),
        out_specs=(
            P(), rows, rows, weight, weight, weight, weight, vector, vector,
            weight, vector, weight, vector, vector, vector,
        ),
        check_vma=False,
    )
```

```python
import math

import jax
import jax.numpy as jnp
from jax import lax
from jax.experimental import pallas as pl
from jax.experimental.pallas import tpu as pltpu
from jax.sharding import PartitionSpec as P

ANY = pl.BlockSpec(memory_space=pl.ANY)
MESH = pl.DeviceIdType.MESH
f32 = jnp.float32
bf16 = jnp.bfloat16


class Layout:
    def __init__(self, mesh):
        dp, blk = mesh.shape["dp"], mesh.shape["blk"]
        if dp == 8 and blk == 4:
            dims = [("z", "dp", 2, 4), ("x", "dp", 1, 2), ("y", "blk", 2, 2), ("c", "blk", 1, 2)]
        else:
            dims = [("z", "dp", dp // 4, 4), ("x", "dp", 2, dp // 8), ("c", "dp", 1, 2), ("y", "blk", 1, blk)]
        self.order = [d[0] for d in dims]
        self.axis = {d[0]: d[1] for d in dims}
        self.stride = {d[0]: d[2] for d in dims}
        self.size = {d[0]: d[3] for d in dims}
        self.dims = tuple(d[3] for d in dims)
        self.blk = blk
        self.devices = dp * blk
        self.slot = {}
        count = 0
        for name in self.order:
            self.slot[name] = count
            count += self.size[name] - 1
        self.slots = count

    def here(self):
        return {
            name: lax.rem(lax.axis_index(self.axis[name]) // self.stride[name], self.size[name])
            for name in self.order
        }

    def step_to(self, here, name, distance):
        there = lax.rem(here[name] + distance, self.size[name])
        index = lax.axis_index(self.axis[name]) + (there - here[name]) * self.stride[name]
        return there, {self.axis[name]: index}

    def at(self, here, whole, changed=(), names=None):
        changed = dict(changed)
        return tuple(
            slice(None) if name in whole else changed.get(name, here[name])
            for name in (names or self.order)
        )

    def place(self, device):
        index = []
        for size in reversed(self.dims):
            index.append(lax.rem(device, size))
            device = device // size
        return tuple(reversed(index))

    def greet(self, here):
        barrier = pltpu.get_barrier_semaphore()
        count = 0
        for name in self.order:
            if self.axis[name] == "blk":
                continue
            for distance in range(1, self.size[name]):
                _, device = self.step_to(here, name, distance)
                pl.semaphore_signal(barrier, inc=1, device_id=device, device_id_type=MESH)
                count += 1
        me = lax.axis_index("blk")
        for distance in range(1, self.blk):
            pl.semaphore_signal(
                barrier, inc=1, device_id={"blk": lax.rem(me + distance, self.blk)}, device_id_type=MESH
            )
            count += 1
        pl.semaphore_wait(barrier, count)


def window(cut):
    if len(cut) == 2:
        return (pl.ds(*cut),)
    return (pl.ds(cut[0], cut[1]), pl.ds(cut[2], cut[3]))


def by_core(here, orders, make):
    if orders[0] == orders[1]:
        make(orders[0])
        return
    for core in range(2):
        @pl.when(here["c"] == core)
        def _():
            make(orders[core])


class Gather:
    stages = 5

    def __init__(self, lay, here, src, full, rows, send, recv, own, orders):
        self.lay, self.here = lay, here
        self.rows = window(rows)
        self.src, self.full = src.at[self.rows], full
        self.send, self.recv, self.own = send, recv, own
        self.orders = orders

    def line(self, name, whole):
        copies = []
        place = self.full.at[self.lay.at(self.here, whole) + self.rows]
        source = self.src if not whole else place
        for distance in range(1, self.lay.size[name]):
            _, device = self.lay.step_to(self.here, name, distance)
            slot = self.lay.slot[name] + distance - 1
            copies.append(
                pltpu.make_async_remote_copy(
                    src_ref=source, dst_ref=place, send_sem=self.send.at[slot], recv_sem=self.recv.at[slot],
                    device_id=device, device_id_type=MESH,
                )
            )
        return copies

    def local(self):
        return pltpu.make_async_copy(self.src, self.full.at[self.lay.at(self.here, ()) + self.rows], self.own)

    def stage(self, k):
        if k == 1:
            self.local().wait()

        def make(order):
            lines = tuple(order) + ("c",)
            if k > 0:
                for c in self.line(lines[k - 1], lines[: k - 1]):
                    c.wait_recv()
            if k < 4:
                for c in self.line(lines[k], lines[:k]):
                    c.start()

        if k == 0:
            self.local().start()
        by_core(self.here, self.orders, make)

    def drain(self):
        def make(order):
            lines = tuple(order) + ("c",)
            for k in range(4):
                for c in self.line(lines[k], lines[:k]):
                    c.wait_send()
        by_core(self.here, self.orders, make)


class Resplit:
    def __init__(self, lay, src, dst, send, recv, own, back=False, first=0):
        self.lay, self.src, self.dst = lay, src, dst
        self.first = first
        self.send, self.recv, self.own = send, recv, own
        self.me = lax.axis_index("blk")
        self.back = back
        self.seqs = (src if back else dst).shape[0]
        self.span = (dst if back else src).shape[1]

    def ends(self, there):
        if self.back:
            return (self.src.at[:, pl.ds(there * self.span, self.span)],
                    self.dst.at[pl.ds(self.me * (self.dst.shape[0] // self.lay.blk) + self.first, self.seqs)])
        return (self.src.at[pl.ds(there * self.seqs, self.seqs)],
                self.dst.at[:, pl.ds(self.me * self.span, self.span)])

    def copies(self):
        out = []
        for distance in range(1, self.lay.blk):
            there = lax.rem(self.me + distance, self.lay.blk)
            src, dst = self.ends(there)
            out.append(
                pltpu.make_async_remote_copy(
                    src_ref=src, dst_ref=dst,
                    send_sem=self.send.at[distance - 1], recv_sem=self.recv.at[distance - 1],
                    device_id={"blk": there}, device_id_type=MESH,
                )
            )
        return out

    def local(self):
        src, dst = self.ends(self.me)
        return pltpu.make_async_copy(src, dst, self.own)

    def start(self):
        self.local().start()
        for c in self.copies():
            c.start()

    def finish(self):
        self.local().wait()
        for c in self.copies():
            c.wait()


class Scatter:
    stages = 5

    def __init__(self, lay, here, grad, cut, out, bufs, send, recv, own, orders, staged=None, turn=False):
        self.turn = turn
        self.lay, self.here, self.grad, self.cut = lay, here, grad, window(cut)
        self.out, self.held, self.recvs, self.staged = out, bufs[0], bufs[1:], staged
        self.send, self.recv, self.own = send, recv, own
        self.orders = orders
        self.names = [n for n in lay.order if n != "c"]

    @staticmethod
    def buffers(lay, cut, dtype, orders):
        shape = (cut[1], cut[3])
        names = [n for n in lay.order if n != "c"]
        out = [pltpu.VMEM(tuple(lay.size[n] for n in names) + shape, dtype)]
        for k in range(3):
            lines = orders[0][k + 1 :]
            left = tuple(lay.size[n] for n in names if n in lines)
            out.append(pltpu.VMEM((lay.size[orders[0][k]] - 1,) + left + shape, dtype))
        return out

    def local(self):
        return pltpu.make_async_copy(
            self.grad.at[self.lay.at(self.here, self.names) + self.cut], self.staged, self.own)

    def core(self):
        there, device = self.lay.step_to(self.here, "c", 1)
        slot = self.lay.slot["c"]
        return pltpu.make_async_remote_copy(
            src_ref=self.grad.at[self.lay.at(self.here, self.names, {"c": there}) + self.cut], dst_ref=self.held,
            send_sem=self.send.at[slot], recv_sem=self.recv.at[slot], device_id=device, device_id_type=MESH)

    def line(self, order, k):
        name, left = order[k], order[k + 1 :]
        copies = []
        for distance in range(1, self.lay.size[name]):
            there, device = self.lay.step_to(self.here, name, distance)
            slot = self.lay.slot[name] + distance - 1
            copies.append(
                pltpu.make_async_remote_copy(
                    src_ref=self.held.at[self.lay.at(self.here, left, {name: there}, self.names)],
                    dst_ref=self.recvs[k].at[distance - 1],
                    send_sem=self.send.at[slot], recv_sem=self.recv.at[slot],
                    device_id=device, device_id_type=MESH,
                )
            )
        return copies

    def add(self, order, k):
        left = [n for n in self.names if k < 0 or n in order[k + 1 :]]
        steps = self.lay.size[left[0]] if left else 1

        def one(i, carry):
            index = {n: slice(None) for n in left}
            if left:
                index[left[0]] = i
            mine = tuple(index.get(n, self.here[n]) for n in self.names)
            value = self.held[mine].astype(f32)
            if k >= 0:
                theirs = tuple(index[n] for n in left)
                for d in range(self.lay.size[order[k]] - 1):
                    value = value + self.recvs[k][(d,) + theirs].astype(f32)
            elif self.staged is not None:
                value = value + self.staged[mine].astype(f32)
            else:
                value = value + self.grad[self.lay.at({**self.here, **index}, ()) + self.cut].astype(f32)
            if k == 2:
                self.out[...] = value.T if self.turn else value
            else:
                self.held[mine] = value.astype(self.held.dtype)
            return carry

        lax.fori_loop(0, steps, one, 0)

    def stage(self, k):
        if k == 0:
            self.core().start()
            if self.staged is not None:
                self.local().start()
            return
        if k == 1:
            if self.staged is not None:
                self.local().wait()
            self.core().wait()
            self.add(None, -1)

        def make(order):
            if k > 1:
                for c in self.line(order, k - 2):
                    c.wait_recv()
                self.add(order, k - 2)
            if k < 4:
                for c in self.line(order, k - 1):
                    c.start()

        by_core(self.here, self.orders, make)

    def drain(self):
        def make(order):
            for k in range(3):
                for c in self.line(order, k):
                    c.wait_send()

        by_core(self.here, self.orders, make)


def skewed(parts, lag=1, stages=5):
    events = []
    for t in range(len(parts) + lag * (stages - 1)):
        for i, part in enumerate(parts):
            stage, rest = divmod(t - i, lag)
            if rest == 0 and 0 <= stage < stages:
                events.append((part, stage))
    return events


class Hooks:
    def __init__(self):
        self.slots = {}

    def put(self, slot, event):
        self.slots.setdefault(slot, []).append(event)

    def spread(self, events, first, last):
        for n, event in enumerate(events):
            self.put(first + n * (last - first) // len(events), event)

    def run(self, slot):
        for part, stage in self.slots.get(slot, ()):
            part.stage(stage)

    def at(self, step, slots):
        for k in slots:
            if k in self.slots:
                pl.when(step == k)(lambda k=k: self.run(k))


def sems(lay, n, m):
    dma = pltpu.SemaphoreType.DMA
    n, m = max(n, 1), max(m, 1)
    return [dma((n, lay.slots)), dma((n, lay.slots)), dma((n,)), dma((m, lay.blk - 1)), dma((m, lay.blk - 1)), dma((m,))]


DH = 64
LOG2E = math.log2(math.e)
GROUP = 256


def dot(a, b):
    return lax.dot_general(a, b, (((1,), (0,)), ((), ())), preferred_element_type=f32)


def dot_t(a, b):
    return lax.dot_general(a, b, (((1,), (1,)), ((), ())), preferred_element_type=f32)


def once(shape):
    return pl.BlockSpec(shape, lambda *_: (0,) * len(shape), pipeline_mode=pl.Buffered(1))


def attention_forward(lay, tokens, lengths, vectors, shards, parts, early):
    width = tokens.shape[2]
    seqs, span = tokens.shape[0] // lay.blk, tokens.shape[1] * lay.blk
    rows = seqs * span
    groups = width // GROUP
    scale = LOG2E / math.sqrt(DH)
    heads = seqs * GROUP // DH
    pairs = seqs * GROUP // 128
    n, p, m = len(shards), len(parts), len(vectors)
    share, deep = vectors[0].shape[0], vectors[-1].shape[0]
    slots = pairs + 3

    def kernel(len_ref, *refs):
        vecs, refs = refs[:m], refs[m:]
        tok_ref, refs = refs[0], refs[1:]
        ins, refs = refs[:n], refs[n:]
        fulls, refs = refs[:n], refs[n:]
        x_out, q_out, k_out, v_out, att_out, lse_ref, h1_out, vec_out, bias_out = refs[:9]
        x_ref, wq_ref, wk_ref, wv_ref, wo_ref, q_ref, k_ref, v_ref, att_ref, h1_ref, pack_ref, packs_ref = refs[9:21]
        load, send, recv, own, rsend, rrecv, rown = refs[21:]
        ins, fulls = list(ins) + [pack_ref], list(fulls) + [packs_ref]
        here = lay.here()
        pack_ref[...] = jnp.zeros_like(pack_ref)
        for i, vec in enumerate(vecs):
            pack_ref[i : i + 1, : vec.shape[0]] = vec[...].astype(f32).reshape(1, vec.shape[0])
        tokens_here = len_ref[0]
        for i in range(1, lengths.shape[0]):
            tokens_here = tokens_here + len_ref[i]
        pack_ref[m : m + 1] = jnp.full((1, 128), tokens_here.astype(f32))
        lay.greet(here)
        split = Resplit(lay, tok_ref, x_out, rsend, rrecv, rown)
        split.start()
        gathers = [
            Gather(lay, here, ins[a], fulls[a], cut, send.at[i], recv.at[i], own.at[i], orders)
            for i, (a, cut, orders) in enumerate(parts)
        ]
        events = skewed(gathers, 2)
        last = max(i for i, (part, stage) in enumerate(events) if part in gathers[:early] and stage == 4)
        for part, stage in events[: last + 1]:
            part.stage(stage)
        split.finish()
        loads = [
            pltpu.make_async_copy(src, dst, load.at[i])
            for i, (src, dst) in enumerate(
                zip([x_out] + list(fulls[:4]), [x_ref, wq_ref, wk_ref, wv_ref, wo_ref]))
        ]
        for c in loads:
            c.start()
        for c in loads:
            c.wait()
        hooks = Hooks()
        hooks.spread(events[last + 1 :], 0, groups * slots)
        base = lax.axis_index("blk") * seqs

        def columns(ref, g):
            block = ref[(slice(None),) * 5 + (pl.ds(pl.multiple_of(g * GROUP, GROUP), GROUP),)]
            return block.reshape(width, GROUP)

        def features(ref, g):
            per = GROUP // ref.shape[-2]
            return jnp.concatenate([ref[lay.place(g * per + j)] for j in range(per)], axis=0)

        def step(i, carry):
            g, r = i // pairs, lax.rem(i, pairs)
            cols = pl.ds(pl.multiple_of(g * GROUP, GROUP), GROUP)

            @pl.when(r == 0)
            def _():
                xv = x_ref[...].reshape(rows, width)
                for j, (low, weight) in enumerate(((q_ref, wq_ref), (k_ref, wk_ref), (v_ref, wv_ref))):
                    low[:, cols] = dot(xv, columns(weight, g)).astype(bf16)
                    hooks.at(g * slots + j, range(j, groups * slots, slots))

            @pl.when(i == groups * pairs // 2)
            def _():
                total = jnp.zeros((1, 128), f32)
                for d in range(lay.devices):
                    tile = packs_ref[lay.place(d)]
                    vec_out[0 : m - 1, d * share : (d + 1) * share] = tile[0 : m - 1, :share]
                    bias_out[:, d * deep : (d + 1) * deep] = tile[m - 1 : m, :deep]
                    total = total + tile[m : m + 1]
                inverse = 1.0 / (total / lay.blk * width)
                for d in range(width // 128):
                    vec_out[m - 1 : m, d * 128 : (d + 1) * 128] = inverse

            s, pair = r // (GROUP // 128), lax.rem(r, GROUP // 128)
            at = (pl.ds(pl.multiple_of(s * span, span), span),
                  pl.ds(pl.multiple_of(g * GROUP + pair * 128, 128), 128))
            qs, ks, vs = q_ref[at], k_ref[at], v_ref[at]
            lane = lax.broadcasted_iota(jnp.int32, (span, 128), 1)
            keep = lax.broadcasted_iota(jnp.int32, (span, 1), 0) < len_ref[base + s]
            vt = vs.T
            outs = []
            for h in range(2):
                km = jnp.where((lane < DH) if h == 0 else (lane >= DH), ks, jnp.zeros_like(ks))
                st = dot_t(km, qs) * scale
                st = jnp.where(keep, st, -1e30)
                top = jnp.max(st, axis=0, keepdims=True)
                e = jnp.exp2(st - top)
                den = jnp.sum(e, axis=0, keepdims=True)
                ot = dot(vt[h * DH : (h + 1) * DH], e.astype(bf16))
                outs.append(ot * (1.0 / den))
                lse_ref[g, pl.ds(r * 2 + h, 1)] = top + jnp.log2(den)
            att_ref[at] = jnp.concatenate(outs, axis=0).T.astype(bf16)

            @pl.when(r == pairs - 1)
            def _():
                add = dot(att_ref[:, cols], features(wo_ref, g))

                @pl.when(g == 0)
                def _():
                    h1_ref[...] = x_ref[...].reshape(rows, width).astype(f32) + add

                @pl.when(g > 0)
                def _():
                    h1_ref[...] += add

            hooks.at(g * slots + 3 + r, [k for k in range(groups * slots) if k % slots >= 3])
            return carry

        lax.fori_loop(0, groups * pairs, step, 0)
        saves = [
            pltpu.make_async_copy(src, dst, load.at[i])
            for i, (src, dst) in enumerate(
                zip([q_ref, k_ref, v_ref, att_ref, h1_ref], [q_out, k_out, v_out, att_out, h1_out]))
        ]
        for c in saves:
            c.start()
        for g in gathers:
            g.drain()
        for c in saves:
            c.wait()

    whole = [jax.ShapeDtypeStruct(lay.dims + s.shape, s.dtype) for s in shards]
    vmem = pl.BlockSpec(memory_space=pltpu.VMEM)
    act = jax.ShapeDtypeStruct((rows, width), bf16)
    return pl.pallas_call(
        kernel,
        in_specs=[pl.BlockSpec(memory_space=pltpu.SMEM)] + [vmem] * m + [ANY] * (n + 1),
        out_specs=[ANY] * (n + 5) + [vmem, ANY, vmem, vmem],
        out_shape=whole
        + [jax.ShapeDtypeStruct((seqs, span, width), bf16), act, act, act, act,
           jax.ShapeDtypeStruct((groups, heads, span), f32), jax.ShapeDtypeStruct((rows, width), f32),
           jax.ShapeDtypeStruct((8, width), f32), jax.ShapeDtypeStruct((1, deep * lay.devices), f32)],
        scratch_shapes=[pltpu.VMEM((seqs, span, width), bf16)]
        + [pltpu.VMEM(lay.dims + s.shape, bf16) for s in shards[:4]]
        + [pltpu.VMEM((rows, width), bf16)] * 4
        + [pltpu.VMEM((rows, width), f32), pltpu.VMEM((8, 128), f32), pltpu.VMEM(lay.dims + (8, 128), f32),
           pltpu.SemaphoreType.DMA((5,))]
        + sems(lay, p, 0)[:3]
        + [pltpu.SemaphoreType.DMA((lay.blk - 1,)), pltpu.SemaphoreType.DMA((lay.blk - 1,)),
           pltpu.SemaphoreType.DMA],
        compiler_params=pltpu.CompilerParams(collective_id=1, has_side_effects=True, vmem_limit_bytes=60 << 20),
        name="attention_forward",
    )(lengths, *vectors, tokens, *shards)


def attention_backward(lay, x, lengths, wq, wk, wv, wo, q, k, v, att, lse, d_branch, d_one, outer, small, orders, aside):
    seqs, span, width = x.shape
    rows = seqs * span
    heads = lse.shape[1]
    groups = width // GROUP
    pairs = seqs * GROUP // 128
    steps = pairs + 1
    depth = width // lay.devices
    scale = LOG2E / math.sqrt(DH)
    deep, share = outer.shape[1:]
    pieces, lag = 8, 3
    while deep % (pieces * 16):
        pieces //= 2
    outer_cuts = [(i * deep // pieces, deep // pieces, 0, share) for i in range(pieces)]
    small_cut = (0, 8, 0, 128)
    wo_cuts = [(0, depth, i * width // 2, width // 2) for i in range(2)]
    late_cuts = [((0, depth, c * GROUP, GROUP), c) for c in range(groups)]
    bufs = [Scatter.buffers(lay, small_cut, f32, orders)] + [Scatter.buffers(lay, c, bf16, orders) for c in wo_cuts]
    bufs += [Scatter.buffers(lay, c, bf16, orders) for c in outer_cuts]
    bufs += [Scatter.buffers(lay, c, bf16, aside) for c, _ in late_cuts for _ in range(3)]
    count = len(bufs)
    wide = deep == width
    outer = outer.reshape(lay.dims + outer.shape[1:])

    def kernel(
        len_ref, x_in, wq_ref, wk_ref, wv_ref, wo_ref, q_ref, k_ref, v_ref, att_ref, lse_ref, db_ref, d1_in, outer_in, small_in,
        gq_out, gk_out, gv_out, go_out, outer_out, small_out, dx_out,
        gq_ref, gk_ref, gv_ref, go_ref, xt_ref, do_ref, dq_ref, dk_ref, dv_ref, acc_ref, dx_ref,
        stage_small, stage_ref, send, recv, own, rsend, rrecv, rown, fetch_sem, *held,
    ):
        g = pl.program_id(0)
        here = lay.here()
        base = lax.axis_index("blk") * seqs
        made = []

        def part(grad, cut, out, way, staged=None, turn=False):
            i = len(made)
            made.append(Scatter(
                lay, here, grad, cut, out, held[4 * i : 4 * i + 4], send.at[i], recv.at[i], own.at[i], way, staged, turn))
            return made[-1]

        first = [part(small_in, small_cut, small_out, orders, stage_small)]
        first += [part(go_ref, c, go_out.at[:, pl.ds(c[2], c[3])], orders) for c in wo_cuts]
        first += [
            part(outer_in, c, outer_out.at[:, pl.ds(c[0], c[1])] if wide else outer_out.at[pl.ds(c[0], c[1])], orders,
                 stage_ref.at[i % (lag + 1)], wide)
            for i, c in enumerate(outer_cuts)
        ]
        hooks = Hooks()
        hooks.spread(skewed(first, lag)[1:], 0, groups * steps - 1)
        finals = []
        for c, group in late_cuts:
            parts = [
                part(ref, c, out.at[:, pl.ds(c[2], c[3])], aside)
                for ref, out in ((gq_ref, gq_out), (gk_ref, gk_out), (gv_ref, gv_out))
            ]
            ready = (group + 1) * steps - 1
            for stage in range(5):
                for i, p in enumerate(parts):
                    hooks.put(ready + i + 5 * stage, (p, stage))
        for k in sorted(hooks.slots):
            if k >= groups * steps - 1:
                finals += hooks.slots.pop(k)
        splits = [
            Resplit(lay, dx_ref.at[pl.ds(s, 1)], dx_out, rsend.at[s], rrecv.at[s], rown.at[s], True, s) for s in range(seqs)
        ]

        @pl.when(g == 0)
        def _():
            lay.greet(here)
            first[0].stage(0)
            fetch = [
                pltpu.make_async_copy(x_in, dx_ref, fetch_sem.at[0]),
                pltpu.make_async_copy(d1_in, acc_ref, fetch_sem.at[1]),
            ]
            for c in fetch:
                c.start()
            for c in fetch:
                c.wait()
            for s in range(seqs):
                xt_ref[:, s * span : (s + 1) * span] = dx_ref[s].T

            def output_rows(j, carry):
                cols = pl.ds(pl.multiple_of(j * GROUP, GROUP), GROUP)
                value = dot(att_ref[:, cols].T, db_ref[...].reshape(rows, width)).astype(bf16)
                for d in range(GROUP // depth):
                    go_ref[lay.place(j * (GROUP // depth) + d)] = value[d * depth : (d + 1) * depth]
                return carry

            lax.fori_loop(0, groups, output_rows, 0)

        do_ref[...] = dot_t(db_ref[...].reshape(rows, width), wo_ref[...]).astype(bf16)

        def pair_step(i, carry):
            s, pair = i // (GROUP // 128), lax.rem(i, GROUP // 128)
            at = (pl.ds(pl.multiple_of(s * span, span), span), pl.ds(pl.multiple_of(pair * 128, 128), 128))
            length = len_ref[base + s]
            qs, ks, vs, dos = q_ref[at], k_ref[at], v_ref[at], do_ref[at]
            lane = lax.broadcasted_iota(jnp.int32, (span, 128), 1)
            keep = lax.broadcasted_iota(jnp.int32, (span, 1), 0) < length
            kt = ks.T
            dqs, dks, dvs = [], [], []
            for h in range(2):
                mine = (lane < DH) if h == 0 else (lane >= DH)
                zero = jnp.zeros_like(ks)
                st = dot_t(jnp.where(mine, ks, zero), qs) * scale
                p = jnp.where(keep, jnp.exp2(st - lse_ref[0, pl.ds(i * 2 + h, 1)]), 0.0)
                dp = dot_t(jnp.where(mine, vs, zero), dos)
                delta = jnp.sum(p * dp, axis=0, keepdims=True)
                ds = (p * (dp - delta)).astype(bf16)
                dvs.append(dot(p.astype(bf16), dos))
                dks.append(dot(ds, qs))
                dqs.append(dot(kt[h * DH : (h + 1) * DH], ds))
            low_half = lane < DH
            unit = 1.0 / math.sqrt(DH)
            dv_ref[at] = jnp.where(low_half, dvs[0], dvs[1]).astype(bf16)
            dk_ref[at] = (jnp.where(low_half, dks[0], dks[1]) * unit).astype(bf16)
            dq_ref[at] = (jnp.concatenate(dqs, axis=0).T * unit).astype(bf16)

            @pl.when(pair == GROUP // 128 - 1)
            def _():
                mine = at[0]
                acc_ref[mine] += (
                    dot_t(dq_ref[mine], wq_ref[...]) + dot_t(dk_ref[mine], wk_ref[...]) + dot_t(dv_ref[mine], wv_ref[...])
                )

            for n in range(seqs):
                @pl.when((g == groups - 1) & (i == (n + 1) * (GROUP // 128) - 1))
                def _():
                    dx_ref[n] = acc_ref[n * span : (n + 1) * span].astype(bf16)
                    splits[n].start()

            hooks.at(g * steps + i, [k for k in range(groups * steps) if k % steps < pairs])
            return carry

        lax.fori_loop(0, pairs, pair_step, 0)
        xt = xt_ref[...]
        cols = (slice(None),) * 5 + (pl.ds(pl.multiple_of(g * GROUP, GROUP), GROUP),)
        for grad, low in ((gq_ref, dq_ref), (gk_ref, dk_ref), (gv_ref, dv_ref)):
            grad[cols] = dot(xt, low[...]).astype(bf16).reshape(lay.dims + (depth, GROUP))
        hooks.at(g * steps + pairs, [k for k in range(groups * steps) if k % steps == pairs])

        @pl.when(g == groups - 1)
        def _():
            for p, stage in finals:
                p.stage(stage)
            for p in made:
                p.drain()
            for split in splits:
                split.finish()

    col = pl.BlockSpec((width, GROUP), lambda g, *_: (0, g))
    row = pl.BlockSpec((GROUP, width), lambda g, *_: (g, 0))
    act = pl.BlockSpec((rows, GROUP), lambda g, *_: (0, g))
    vmem = pl.BlockSpec(memory_space=pltpu.VMEM)
    grad = pltpu.VMEM(lay.dims + (depth, width), bf16)
    no_core = tuple(lay.size[n] for n in lay.order if n != "c")
    shard = jax.ShapeDtypeStruct((depth, width), f32)
    return pl.pallas_call(
        kernel,
        grid_spec=pltpu.PrefetchScalarGridSpec(
            num_scalar_prefetch=0,
            grid=(groups,),
            in_specs=[pl.BlockSpec(memory_space=pltpu.SMEM), ANY, col, col, col, row, act, act, act, once((rows, width)),
                      pl.BlockSpec((1, heads, span), lambda g, *_: (g, 0, 0)), once((seqs, span, width)), ANY, ANY, ANY],
            out_specs=[once((depth, width))] * 4 + [once((share, deep) if wide else (deep, share)), once((8, 128)), ANY],
            scratch_shapes=[grad] * 4
            + [pltpu.VMEM((width, rows), bf16)] + [pltpu.VMEM((rows, GROUP), bf16)] * 4
            + [pltpu.VMEM((rows, width), f32), pltpu.VMEM((seqs, span, width), bf16)]
            + [pltpu.VMEM(no_core + (8, 128), f32)] + [pltpu.VMEM((lag + 1,) + no_core + (deep // pieces, share), bf16)]
            + sems(lay, count, 0)[:3]
            + sems(lay, 0, seqs)[3:] + [pltpu.SemaphoreType.DMA((2,))]
            + [b for bs in bufs for b in bs],
        ),
        out_shape=[shard] * 4
        + [jax.ShapeDtypeStruct((share, deep) if wide else (deep, share), f32), jax.ShapeDtypeStruct((8, 128), f32),
           jax.ShapeDtypeStruct((seqs * lay.blk, span // lay.blk, width), bf16)],
        compiler_params=pltpu.CompilerParams(
            collective_id=3, has_side_effects=True, vmem_limit_bytes=63 << 20),
        name="attention_backward",
    )(lengths, x, wq, wk, wv, wo, q, k, v, att, lse, d_branch, d_one, outer, small)


TILE = 512
CHUNK = 512


def feed_forward(lay, h1, teacher, out_grad, lengths, vecs, bias_inner, w1, w2, orders):
    rows, width = h1.shape
    hidden = w1.shape[1]
    seqs = teacher.shape[0] // lay.blk
    span = rows // seqs
    devices = lay.devices
    tiles = hidden // TILE
    share, share1 = hidden // devices, width // devices
    per_tile = TILE // share
    wide = share % 128 == 0
    pieces, depth, lag, kept = tiles, width // devices, 3, 4
    columns = hidden // pieces
    bufs = Scatter.buffers(lay, (0, depth, 0, columns), bf16, orders)

    def kernel(
        len_ref, h1_ref, teach_in, og_in, vec_ref, b1_ref, w1_ref, w2_ref,
        layer_out, d1_ref, db_out, gw1_out, gw2_ref, small_ref,
        low_ref, lowt_ref, act_ref, slope_ref, acc_ref, do_ref, dot_ref, inv1_ref, di_ref, db_ref, gw1_ref, sums_ref, gb1_ref,
        rsend, rrecv, rown, send, recv, own, *held,
    ):
        t = pl.program_id(0)
        here = lay.here()
        base = lax.axis_index("blk") * seqs
        splits = [
            Resplit(lay, src, dst, rsend.at[i], rrecv.at[i], rown.at[i], i == 2)
            for i, (src, dst) in enumerate(((teach_in, do_ref), (og_in, db_ref), (low_ref, layer_out)))
        ]
        sums = [
            Scatter(
                lay, here, gw1_ref.at[i % kept], (0, depth, 0, columns), gw1_out.at[:, pl.ds(i * columns, columns)],
                held[4 * i : 4 * i + 4], send.at[i], recv.at[i], own.at[i], orders)
            for i in range(pieces)
        ]
        hooks = Hooks()
        for slot in range(pieces + 4 * lag):
            for i in range(pieces):
                stage, rest = divmod(slot - i, lag)
                if rest == 0 and 0 <= stage < 5:
                    hooks.put(slot, (sums[i], stage))
        last = max(hooks.slots)
        span_of = lambda row: (row // span, pl.ds(row % span, CHUNK))
        gain1, shift1 = vec_ref[0:1], vec_ref[1:2]
        bias2, gain2, shift2 = vec_ref[2:3], vec_ref[3:4], vec_ref[4:5]

        @pl.when(t == 0)
        def _():
            lay.greet(here)
            splits[0].start()
            splits[1].start()
            fetch = pltpu.make_async_copy(h1_ref, d1_ref, own.at[pieces])
            fetch.start()
            fetch.wait()
            sums_ref[...] = jnp.zeros_like(sums_ref)

            def norm(i, carry):
                at = pl.ds(pl.multiple_of(i * 128, 128), 128)
                seq = (i * 128) // span
                there = (seq, pl.ds(pl.multiple_of(i * 128 - seq * span, 128), 128))
                h = d1_ref[at]
                centred = h - jnp.mean(h, axis=-1, keepdims=True)
                inverse = lax.rsqrt(jnp.mean(centred * centred, axis=-1, keepdims=True) + 1e-12)
                normal = centred * inverse
                d1_ref[at] = normal
                inv1_ref[at] = inverse
                low = (normal * gain1 + shift1).astype(bf16)
                low_ref[there] = low
                lowt_ref[:, at] = low.T
                return carry

            lax.fori_loop(0, rows // 128, norm, 0)
            acc_ref[...] = jnp.zeros_like(acc_ref)

        @pl.when(t < tiles)
        def _():
            for i in range(rows // CHUNK):
                at = slice(i * CHUNK, (i + 1) * CHUNK)
                inner = dot(low_ref[span_of(i * CHUNK)], w1_ref[...]) + b1_ref[...]
                cum = 0.5 * (1.0 + lax.erf(inner * (1.0 / math.sqrt(2.0))))
                density = jnp.exp(-0.5 * inner * inner) * (1.0 / math.sqrt(2.0 * math.pi))
                active = (inner * cum).astype(bf16)
                act_ref[t, at] = active
                slope_ref[t, at] = (cum + inner * density).astype(bf16)
                acc_ref[at] += dot(active, w2_ref[...])

        @pl.when(t == tiles)
        def _():
            inv = vec_ref[5:6]
            splits[0].finish()
            splits[1].finish()

            def middle(i, carry):
                at = pl.ds(pl.multiple_of(i * 128, 128), 128)
                normed = d1_ref[at] * gain1 + shift1
                h2 = normed + acc_ref[at] + bias2
                centred = h2 - jnp.mean(h2, axis=-1, keepdims=True)
                inverse = lax.rsqrt(jnp.mean(centred * centred, axis=-1, keepdims=True) + 1e-12)
                normal = centred * inverse
                result = normal * gain2 + shift2
                seq = (i * 128) // span
                first = i * 128 - seq * span
                there = (seq, pl.ds(pl.multiple_of(first, 128), 128))
                low_ref[there] = result.astype(bf16)
                pos = first + lax.broadcasted_iota(jnp.int32, (128, 1), 0)
                valid = (pos < len_ref[base + seq]).astype(f32)
                deviation = (result - do_ref[there].astype(f32)) * valid
                grad = db_ref[there].astype(f32) * valid + (2.0 * inv) * deviation
                sums_ref[0:1] += jnp.sum(deviation * deviation, axis=0, keepdims=True)
                sums_ref[1:2] += jnp.sum(grad * normal, axis=0, keepdims=True)
                sums_ref[2:3] += jnp.sum(grad, axis=0, keepdims=True)
                scaled = grad * gain2
                mean = jnp.mean(scaled, axis=-1, keepdims=True)
                along = jnp.mean(scaled * normal, axis=-1, keepdims=True)
                d_two = inverse * (scaled - mean - normal * along)
                acc_ref[at] = d_two
                low = d_two.astype(bf16)
                sums_ref[3:4] += jnp.sum(low.astype(f32), axis=0, keepdims=True)
                do_ref[there] = low
                dot_ref[:, at] = low.T
                return carry

            lax.fori_loop(0, rows // 128, middle, 0)
            splits[2].start()

        @pl.when((t > tiles) & (t <= 2 * tiles))
        def _():
            j = t - tiles - 1
            total = jnp.zeros((1, TILE), f32)
            for i in range(rows // CHUNK):
                at = slice(i * CHUNK, (i + 1) * CHUNK)
                d_act = dot_t(do_ref[span_of(i * CHUNK)], w2_ref[...])
                d_in = (d_act * slope_ref[j, at].astype(f32)).astype(bf16)
                total += jnp.sum(d_in.astype(f32), axis=0, keepdims=True)
                di_ref[at] = d_in
                acc_ref[at] += dot_t(d_in, w1_ref[...])
            gb1_ref[:, pl.ds(pl.multiple_of(j * TILE, TILE), TILE)] = total
            value = dot(lowt_ref[...], di_ref[...]).astype(bf16)
            gw1_ref[lax.rem(j, kept)] = value.reshape(lay.dims + (depth, TILE))
            hooks.at(j, range(tiles))

        @pl.when(t == 2 * tiles)
        def _():
            def back(i, carry):
                at = pl.ds(pl.multiple_of(i * 128, 128), 128)
                seq = (i * 128) // span
                there = (seq, pl.ds(pl.multiple_of(i * 128 - seq * span, 128), 128))
                grad, normal = acc_ref[at], d1_ref[at]
                sums_ref[4:5] += jnp.sum(grad * normal, axis=0, keepdims=True)
                sums_ref[5:6] += jnp.sum(grad, axis=0, keepdims=True)
                scaled = grad * gain1
                mean = jnp.mean(scaled, axis=-1, keepdims=True)
                along = jnp.mean(scaled * normal, axis=-1, keepdims=True)
                d_one = inv1_ref[at] * (scaled - mean - normal * along)
                d1_ref[at] = d_one
                db_ref[there] = d_one.astype(bf16)
                return carry

            lax.fori_loop(0, rows // 128, back, 0)

        @pl.when(t > 2 * tiles)
        def _():
            j = t - 2 * tiles - 1
            gw2 = dot(dot_ref[...], act_ref[j]).astype(bf16)
            if wide:
                for d in range(per_tile):
                    gw2_ref[d] = gw2[:, d * share : (d + 1) * share]
            else:
                gw2_ref[...] = gw2
            hooks.at(t - tiles - 1, range(tiles, 2 * tiles))

        @pl.when(t == 2 * tiles + 1)
        def _():
            small_ref[...] = jnp.zeros_like(small_ref)
            loss = jnp.broadcast_to(jnp.sum(sums_ref[0:1], axis=-1, keepdims=True), (1, 128))
            for d in range(devices):
                at = lay.place(d)
                small_ref[at + (slice(0, 5), slice(0, share1))] = sums_ref[1:6, d * share1 : (d + 1) * share1]
                small_ref[at + (slice(5, 6), slice(0, share))] = gb1_ref[:, d * share : (d + 1) * share]
                small_ref[at + (slice(6, 7),)] = loss

        @pl.when(t == 3 * tiles)
        def _():
            save = pltpu.make_async_copy(db_ref, db_out, own.at[pieces])
            save.start()
            for k in range(2 * tiles, last + 1):
                hooks.run(k)
            for part in sums:
                part.drain()
            splits[2].finish()
            save.wait()

    def tile(t, *_):
        return jnp.where(t < tiles, t, jnp.clip(t - tiles - 1, 0, tiles - 1))

    def outer_tile(t, *_):
        return jnp.maximum(t - 2 * tiles - 1, 0)

    full = once((rows, width))
    vec = pl.BlockSpec((1, TILE), lambda t, *_: (0, tile(t)))
    low = pltpu.VMEM((seqs, span, width), bf16)
    return pl.pallas_call(
        kernel,
        grid_spec=pltpu.PrefetchScalarGridSpec(
            num_scalar_prefetch=0,
            grid=(3 * tiles + 1,),
            in_specs=[
                pl.BlockSpec(memory_space=pltpu.SMEM), ANY, ANY, ANY, once((8, width)), vec,
                pl.BlockSpec((width, TILE), lambda t, *_: (0, tile(t))),
                pl.BlockSpec((TILE, width), lambda t, *_: (tile(t), 0)),
            ],
            out_specs=[
                ANY, full, ANY, once((depth, hidden)),
                pl.BlockSpec((per_tile, width, share), lambda t, *_: (outer_tile(t), 0, 0))
                if wide else pl.BlockSpec((width, TILE), lambda t, *_: (0, outer_tile(t))),
                once(lay.dims + (8, 128)),
            ],
            scratch_shapes=[
                low, pltpu.VMEM((width, rows), bf16),
                pltpu.VMEM((tiles, rows, TILE), bf16), pltpu.VMEM((tiles, rows, TILE), bf16),
                pltpu.VMEM((rows, width), f32), low, pltpu.VMEM((width, rows), bf16),
                pltpu.VMEM((rows, 1), f32), pltpu.VMEM((rows, TILE), bf16), low,
                pltpu.VMEM((kept,) + lay.dims + (depth, columns), bf16),
                pltpu.VMEM((8, width), f32), pltpu.VMEM((1, hidden), f32),
            ]
            + sems(lay, 0, 3)[3:]
            + sems(lay, pieces + 1, 0)[:3]
            + bufs * pieces,
        ),
        out_shape=[
            jax.ShapeDtypeStruct(teacher.shape, bf16),
            jax.ShapeDtypeStruct((rows, width), f32),
            jax.ShapeDtypeStruct((seqs, span, width), bf16),
            jax.ShapeDtypeStruct((depth, hidden), f32),
            jax.ShapeDtypeStruct((devices, width, share) if wide else (width, hidden), bf16),
            jax.ShapeDtypeStruct(lay.dims + (8, 128), f32),
        ],
        compiler_params=pltpu.CompilerParams(
            collective_id=2, has_side_effects=True, vmem_limit_bytes=63 << 20),
        name="feed_forward",
    )(lengths, h1, teacher, out_grad, vecs, bias_inner, w1, w2)


def cut(shape, which, pieces, orders, columns=False):
    rows, wide = shape
    if columns:
        step = wide // pieces
        return [(which, (0, rows, i * step, step), orders) for i in range(pieces)]
    while pieces > 1 and rows % (pieces * 16):
        pieces -= 1
    step = rows // pieces
    return [(which, (i * step, step), orders) for i in range(pieces)]


def shards(
    lay, tokens, lengths, teacher, out_grad, w_query, w_key, w_value, w_output, gain_one, shift_one,
    w_inner, bias_inner, w_outer, bias_outer, gain_two, shift_two,
):
    width = tokens.shape[2]
    hidden = w_inner.shape[1]
    devices = lay.devices
    there = (("z", "x", "y"), ("z", "y", "x"))
    back = (("y", "x", "z"), ("x", "y", "z"))
    aside = (("x", "y", "z"),) * 2
    share, deep = gain_one.shape[0], bias_inner.shape[0]
    ins = [w_query, w_key, w_value, w_output, w_inner, w_outer]
    parts = [(6, (0, 8), there)]
    for i in range(4):
        parts += cut(ins[i].shape, i, 1, there)
    early = len(parts)
    parts += cut(w_inner.shape, 4, 8, there, True) + cut(w_outer.shape, 5, 8, there)
    vectors = [gain_one, shift_one, bias_outer, gain_two, shift_two, bias_inner]
    wq, wk, wv, wo, w1, w2, x, q, k, v, att, lse, h1, vecs, bias1 = attention_forward(
        lay, tokens, lengths, vectors, ins, parts, early
    )
    wq, wk, wv, wo = (w.reshape(width, width) for w in (wq, wk, wv, wo))
    w1, w2 = w1.reshape(width, hidden), w2.reshape(hidden, width)
    layer_out, d_one, d_branch, g_inner, gw2, small = feed_forward(
        lay, h1, teacher, out_grad, lengths, vecs, bias1, w1, w2, aside
    )
    if gw2.ndim == 2:
        gw2 = gw2.T.reshape(devices, hidden // devices, width)
    g_query, g_key, g_value, g_output, g_outer, small, d_tokens = attention_backward(
        lay, x, lengths, wq, wk, wv, wo, q, k, v, att, lse, d_branch, d_one, gw2, small, back, aside
    )
    vec = lambda i: small[i, :share]
    return (
        small[6, 0] * vecs[5, 0],
        layer_out,
        d_tokens.astype(f32),
        g_query,
        g_key,
        g_value,
        g_output,
        vec(3),
        vec(4),
        g_inner,
        small[5, :deep],
        g_outer,
        vec(2),
        vec(0),
        vec(1),
    )


def solution(mesh):
    lay = Layout(mesh)
    rows = P("dp", "blk", None)
    weight = P(("dp", "blk"), None)
    vector = P(("dp", "blk"))
    return jax.shard_map(
        lambda *args: shards(lay, *args),
        mesh=mesh,
        in_specs=(
            rows, P("dp"), rows, rows, weight, weight, weight, weight, vector, vector,
            weight, vector, weight, vector, vector, vector,
        ),
        out_specs=(
            P(), rows, rows, weight, weight, weight, weight, vector, vector,
            weight, vector, weight, vector, vector, vector,
        ),
        check_vma=False,
    )
```

```python
import math

import jax
import jax.numpy as jnp
from jax import lax
from jax.experimental import pallas as pl
from jax.experimental.pallas import tpu as pltpu
from jax.sharding import PartitionSpec as P

ANY = pl.BlockSpec(memory_space=pl.ANY)
MESH = pl.DeviceIdType.MESH
f32 = jnp.float32
bf16 = jnp.bfloat16


class Layout:
    def __init__(self, mesh):
        dp, blk = mesh.shape["dp"], mesh.shape["blk"]
        if dp == 8 and blk == 4:
            dims = [("z", "dp", 2, 4), ("x", "dp", 1, 2), ("y", "blk", 2, 2), ("c", "blk", 1, 2)]
        else:
            dims = [("z", "dp", dp // 4, 4), ("x", "dp", 2, dp // 8), ("c", "dp", 1, 2), ("y", "blk", 1, blk)]
        self.order = [d[0] for d in dims]
        self.axis = {d[0]: d[1] for d in dims}
        self.stride = {d[0]: d[2] for d in dims}
        self.size = {d[0]: d[3] for d in dims}
        self.dims = tuple(d[3] for d in dims)
        self.blk = blk
        self.devices = dp * blk
        self.slot = {}
        count = 0
        for name in self.order:
            self.slot[name] = count
            count += self.size[name] - 1
        self.slots = count

    def here(self):
        return {
            name: lax.rem(lax.axis_index(self.axis[name]) // self.stride[name], self.size[name])
            for name in self.order
        }

    def step_to(self, here, name, distance):
        there = lax.rem(here[name] + distance, self.size[name])
        index = lax.axis_index(self.axis[name]) + (there - here[name]) * self.stride[name]
        return there, {self.axis[name]: index}

    def at(self, here, whole, changed=(), names=None):
        changed = dict(changed)
        return tuple(
            slice(None) if name in whole else changed.get(name, here[name])
            for name in (names or self.order)
        )

    def place(self, device):
        index = []
        for size in reversed(self.dims):
            index.append(lax.rem(device, size))
            device = device // size
        return tuple(reversed(index))

    def greet(self, here):
        barrier = pltpu.get_barrier_semaphore()
        count = 0
        for name in self.order:
            if self.axis[name] == "blk":
                continue
            for distance in range(1, self.size[name]):
                _, device = self.step_to(here, name, distance)
                pl.semaphore_signal(barrier, inc=1, device_id=device, device_id_type=MESH)
                count += 1
        me = lax.axis_index("blk")
        for distance in range(1, self.blk):
            pl.semaphore_signal(
                barrier, inc=1, device_id={"blk": lax.rem(me + distance, self.blk)}, device_id_type=MESH
            )
            count += 1
        pl.semaphore_wait(barrier, count)


def window(cut):
    if len(cut) == 2:
        return (pl.ds(*cut),)
    return (pl.ds(cut[0], cut[1]), pl.ds(cut[2], cut[3]))


def by_core(here, orders, make):
    if orders[0] == orders[1]:
        make(orders[0])
        return
    for core in range(2):
        @pl.when(here["c"] == core)
        def _():
            make(orders[core])


class Gather:
    stages = 5

    def __init__(self, lay, here, src, full, rows, send, recv, own, orders):
        self.lay, self.here = lay, here
        self.rows = window(rows)
        self.src, self.full = src.at[self.rows], full
        self.send, self.recv, self.own = send, recv, own
        self.orders = orders

    def line(self, name, whole):
        copies = []
        place = self.full.at[self.lay.at(self.here, whole) + self.rows]
        source = self.src if not whole else place
        for distance in range(1, self.lay.size[name]):
            _, device = self.lay.step_to(self.here, name, distance)
            slot = self.lay.slot[name] + distance - 1
            copies.append(
                pltpu.make_async_remote_copy(
                    src_ref=source, dst_ref=place, send_sem=self.send.at[slot], recv_sem=self.recv.at[slot],
                    device_id=device, device_id_type=MESH,
                )
            )
        return copies

    def local(self):
        return pltpu.make_async_copy(self.src, self.full.at[self.lay.at(self.here, ()) + self.rows], self.own)

    def stage(self, k):
        if k == 1:
            self.local().wait()

        def make(order):
            lines = tuple(order) + ("c",)
            if k > 0:
                for c in self.line(lines[k - 1], lines[: k - 1]):
                    c.wait_recv()
            if k < 4:
                for c in self.line(lines[k], lines[:k]):
                    c.start()

        if k == 0:
            self.local().start()
        by_core(self.here, self.orders, make)

    def drain(self):
        def make(order):
            lines = tuple(order) + ("c",)
            for k in range(4):
                for c in self.line(lines[k], lines[:k]):
                    c.wait_send()
        by_core(self.here, self.orders, make)


class Resplit:
    def __init__(self, lay, src, dst, send, recv, own, back=False, first=0):
        self.lay, self.src, self.dst = lay, src, dst
        self.first = first
        self.send, self.recv, self.own = send, recv, own
        self.me = lax.axis_index("blk")
        self.back = back
        self.seqs = (src if back else dst).shape[0]
        self.total = (dst if back else src).shape[0] // lay.blk
        self.span = (dst if back else src).shape[1]

    def ends(self, there):
        if self.back:
            return (self.src.at[:, pl.ds(there * self.span, self.span)],
                    self.dst.at[pl.ds(self.me * self.total + self.first, self.seqs)])
        return (self.src.at[pl.ds(there * self.total + self.first, self.seqs)],
                self.dst.at[:, pl.ds(self.me * self.span, self.span)])

    def copies(self):
        out = []
        for distance in range(1, self.lay.blk):
            there = lax.rem(self.me + distance, self.lay.blk)
            src, dst = self.ends(there)
            out.append(
                pltpu.make_async_remote_copy(
                    src_ref=src, dst_ref=dst,
                    send_sem=self.send.at[distance - 1], recv_sem=self.recv.at[distance - 1],
                    device_id={"blk": there}, device_id_type=MESH,
                )
            )
        return out

    def local(self):
        src, dst = self.ends(self.me)
        return pltpu.make_async_copy(src, dst, self.own)

    def start(self):
        self.local().start()
        for c in self.copies():
            c.start()

    def finish(self):
        self.local().wait()
        for c in self.copies():
            c.wait()


class Scatter:
    stages = 5

    def __init__(self, lay, here, grad, cut, out, bufs, send, recv, own, orders, staged=None, turn=False):
        self.turn = turn
        self.lay, self.here, self.grad, self.cut = lay, here, grad, window(cut)
        self.out, self.held, self.recvs, self.staged = out, bufs[0], bufs[1:], staged
        self.send, self.recv, self.own = send, recv, own
        self.orders = orders
        self.names = [n for n in lay.order if n != "c"]

    @staticmethod
    def buffers(lay, cut, dtype, orders):
        shape = (cut[1], cut[3])
        names = [n for n in lay.order if n != "c"]
        out = [pltpu.VMEM(tuple(lay.size[n] for n in names) + shape, dtype)]
        for k in range(3):
            lines = orders[0][k + 1 :]
            left = tuple(lay.size[n] for n in names if n in lines)
            out.append(pltpu.VMEM((lay.size[orders[0][k]] - 1,) + left + shape, dtype))
        return out

    def local(self):
        return pltpu.make_async_copy(
            self.grad.at[self.lay.at(self.here, self.names) + self.cut], self.staged, self.own)

    def core(self):
        there, device = self.lay.step_to(self.here, "c", 1)
        slot = self.lay.slot["c"]
        return pltpu.make_async_remote_copy(
            src_ref=self.grad.at[self.lay.at(self.here, self.names, {"c": there}) + self.cut], dst_ref=self.held,
            send_sem=self.send.at[slot], recv_sem=self.recv.at[slot], device_id=device, device_id_type=MESH)

    def line(self, order, k):
        name, left = order[k], order[k + 1 :]
        copies = []
        for distance in range(1, self.lay.size[name]):
            there, device = self.lay.step_to(self.here, name, distance)
            slot = self.lay.slot[name] + distance - 1
            copies.append(
                pltpu.make_async_remote_copy(
                    src_ref=self.held.at[self.lay.at(self.here, left, {name: there}, self.names)],
                    dst_ref=self.recvs[k].at[distance - 1],
                    send_sem=self.send.at[slot], recv_sem=self.recv.at[slot],
                    device_id=device, device_id_type=MESH,
                )
            )
        return copies

    def add(self, order, k):
        left = [n for n in self.names if k < 0 or n in order[k + 1 :]]
        steps = self.lay.size[left[0]] if left else 1

        def one(i, carry):
            index = {n: slice(None) for n in left}
            if left:
                index[left[0]] = i
            mine = tuple(index.get(n, self.here[n]) for n in self.names)
            value = self.held[mine].astype(f32)
            if k >= 0:
                theirs = tuple(index[n] for n in left)
                for d in range(self.lay.size[order[k]] - 1):
                    value = value + self.recvs[k][(d,) + theirs].astype(f32)
            elif self.staged is not None:
                value = value + self.staged[mine].astype(f32)
            else:
                value = value + self.grad[self.lay.at({**self.here, **index}, ()) + self.cut].astype(f32)
            if k == 2:
                self.out[...] = value.T if self.turn else value
            else:
                self.held[mine] = value.astype(self.held.dtype)
            return carry

        lax.fori_loop(0, steps, one, 0)

    def stage(self, k):
        if k == 0:
            self.core().start()
            if self.staged is not None:
                self.local().start()
            return
        if k == 1:
            if self.staged is not None:
                self.local().wait()
            self.core().wait()
            self.add(None, -1)

        def make(order):
            if k > 1:
                for c in self.line(order, k - 2):
                    c.wait_recv()
                self.add(order, k - 2)
            if k < 4:
                for c in self.line(order, k - 1):
                    c.start()

        by_core(self.here, self.orders, make)

    def drain(self):
        def make(order):
            for k in range(3):
                for c in self.line(order, k):
                    c.wait_send()

        by_core(self.here, self.orders, make)


def skewed(parts, lag=1, stages=5):
    events = []
    for t in range(len(parts) + lag * (stages - 1)):
        for i, part in enumerate(parts):
            stage, rest = divmod(t - i, lag)
            if rest == 0 and 0 <= stage < stages:
                events.append((part, stage))
    return events


class Hooks:
    def __init__(self):
        self.slots = {}

    def put(self, slot, event):
        self.slots.setdefault(slot, []).append(event)

    def spread(self, events, first, last):
        for n, event in enumerate(events):
            self.put(first + n * (last - first) // len(events), event)

    def run(self, slot):
        for part, stage in self.slots.get(slot, ()):
            part.stage(stage)

    def at(self, step, slots):
        for k in slots:
            if k in self.slots:
                pl.when(step == k)(lambda k=k: self.run(k))


def sems(lay, n, m):
    dma = pltpu.SemaphoreType.DMA
    n, m = max(n, 1), max(m, 1)
    return [dma((n, lay.slots)), dma((n, lay.slots)), dma((n,)), dma((m, lay.blk - 1)), dma((m, lay.blk - 1)), dma((m,))]


DH = 64
LOG2E = math.log2(math.e)
GROUP = 256


def dot(a, b):
    return lax.dot_general(a, b, (((1,), (0,)), ((), ())), preferred_element_type=f32)


def dot_t(a, b):
    return lax.dot_general(a, b, (((1,), (1,)), ((), ())), preferred_element_type=f32)


def once(shape):
    return pl.BlockSpec(shape, lambda *_: (0,) * len(shape), pipeline_mode=pl.Buffered(1))


def attention_forward(lay, tokens, lengths, vectors, shards, parts, early):
    width = tokens.shape[2]
    seqs, span = tokens.shape[0] // lay.blk, tokens.shape[1] * lay.blk
    rows = seqs * span
    groups = width // GROUP
    scale = LOG2E / math.sqrt(DH)
    heads = seqs * GROUP // DH
    pairs = seqs * GROUP // 128
    n, p, m = len(shards), len(parts), len(vectors)
    share, deep = vectors[0].shape[0], vectors[-1].shape[0]
    slots = pairs + 3

    def kernel(len_ref, *refs):
        vecs, refs = refs[:m], refs[m:]
        tok_ref, refs = refs[0], refs[1:]
        ins, refs = refs[:n], refs[n:]
        fulls, refs = refs[:n], refs[n:]
        x_out, q_out, k_out, v_out, att_out, lse_ref, h1_out, vec_out, bias_out = refs[:9]
        x_ref, wq_ref, wk_ref, wv_ref, wo_ref, q_ref, k_ref, v_ref, att_ref, h1_ref, pack_ref, packs_ref = refs[9:21]
        load, send, recv, own, rsend, rrecv, rown = refs[21:]
        ins, fulls = list(ins) + [pack_ref], list(fulls) + [packs_ref]
        here = lay.here()
        pack_ref[...] = jnp.zeros_like(pack_ref)
        for i, vec in enumerate(vecs):
            pack_ref[i : i + 1, : vec.shape[0]] = vec[...].astype(f32).reshape(1, vec.shape[0])
        tokens_here = len_ref[0]
        for i in range(1, lengths.shape[0]):
            tokens_here = tokens_here + len_ref[i]
        pack_ref[m : m + 1] = jnp.full((1, 128), tokens_here.astype(f32))
        lay.greet(here)
        split = Resplit(lay, tok_ref, x_ref, rsend, rrecv, rown)
        split.start()
        gathers = [
            Gather(lay, here, ins[a], fulls[a], cut, send.at[i], recv.at[i], own.at[i], orders)
            for i, (a, cut, orders) in enumerate(parts)
        ]
        events = skewed(gathers, 2)
        last = max(i for i, (part, stage) in enumerate(events) if part in gathers[:early] and stage == 4)
        for part, stage in events[: last + 1]:
            part.stage(stage)
        split.finish()
        loads = [
            pltpu.make_async_copy(src, dst, load.at[i])
            for i, (src, dst) in enumerate(
                zip(fulls[:4], [wq_ref, wk_ref, wv_ref, wo_ref]))
        ]
        for c in loads:
            c.start()
        for c in loads:
            c.wait()
        hooks = Hooks()
        hooks.spread(events[last + 1 :], 0, groups * slots * 4 // 3)
        base = lax.axis_index("blk") * seqs

        def columns(ref, g):
            block = ref[(slice(None),) * 5 + (pl.ds(pl.multiple_of(g * GROUP, GROUP), GROUP),)]
            return block.reshape(width, GROUP)

        def features(ref, g):
            per = GROUP // ref.shape[-2]
            return jnp.concatenate([ref[lay.place(g * per + j)] for j in range(per)], axis=0)

        def step(i, carry):
            g, r = i // pairs, lax.rem(i, pairs)
            cols = pl.ds(pl.multiple_of(g * GROUP, GROUP), GROUP)

            @pl.when(r == 0)
            def _():
                xv = x_ref[...].reshape(rows, width)
                for j, (low, weight) in enumerate(((q_ref, wq_ref), (k_ref, wk_ref), (v_ref, wv_ref))):
                    low[:, cols] = dot(xv, columns(weight, g)).astype(bf16)
                    hooks.at(g * slots + j, range(j, groups * slots, slots))

            @pl.when(i == groups * pairs // 2)
            def _():
                total = jnp.zeros((1, 128), f32)
                for d in range(lay.devices):
                    tile = packs_ref[lay.place(d)]
                    vec_out[0 : m - 1, d * share : (d + 1) * share] = tile[0 : m - 1, :share]
                    bias_out[:, d * deep : (d + 1) * deep] = tile[m - 1 : m, :deep]
                    total = total + tile[m : m + 1]
                inverse = 1.0 / (total / lay.blk * width)
                for d in range(width // 128):
                    vec_out[m - 1 : m, d * 128 : (d + 1) * 128] = inverse

            s, pair = r // (GROUP // 128), lax.rem(r, GROUP // 128)
            at = (pl.ds(pl.multiple_of(s * span, span), span),
                  pl.ds(pl.multiple_of(g * GROUP + pair * 128, 128), 128))
            qs, ks, vs = q_ref[at], k_ref[at], v_ref[at]
            lane = lax.broadcasted_iota(jnp.int32, (span, 128), 1)
            keep = lax.broadcasted_iota(jnp.int32, (span, 1), 0) < len_ref[base + s]
            vt = vs.T
            outs = []
            for h in range(2):
                km = jnp.where((lane < DH) if h == 0 else (lane >= DH), ks, jnp.zeros_like(ks))
                st = dot_t(km, qs) * scale
                st = jnp.where(keep, st, -1e30)
                top = jnp.max(st, axis=0, keepdims=True)
                e = jnp.exp2(st - top)
                den = jnp.sum(e, axis=0, keepdims=True)
                ot = dot(vt[h * DH : (h + 1) * DH], e.astype(bf16))
                outs.append(ot * (1.0 / den))
                lse_ref[g, pl.ds(r * 2 + h, 1)] = top + jnp.log2(den)
            att_ref[at] = jnp.concatenate(outs, axis=0).T.astype(bf16)

            @pl.when(r == pairs - 1)
            def _():
                add = dot(att_ref[:, cols], features(wo_ref, g))

                @pl.when(g == 0)
                def _():
                    h1_ref[...] = x_ref[...].reshape(rows, width).astype(f32) + add

                @pl.when(g > 0)
                def _():
                    h1_ref[...] += add

            hooks.at(g * slots + 3 + r, [k for k in range(groups * slots) if k % slots >= 3])
            return carry

        lax.fori_loop(0, groups * pairs, step, 0)
        saves = [
            pltpu.make_async_copy(src, dst, load.at[i])
            for i, (src, dst) in enumerate(
                zip([x_ref, q_ref, k_ref, v_ref, att_ref, h1_ref], [x_out, q_out, k_out, v_out, att_out, h1_out]))
        ]
        for c in saves:
            c.start()
        for k in sorted(hooks.slots):
            if k >= groups * slots:
                hooks.run(k)
        for g in gathers:
            g.drain()
        for c in saves:
            c.wait()

    whole = [jax.ShapeDtypeStruct(lay.dims + s.shape, s.dtype) for s in shards]
    vmem = pl.BlockSpec(memory_space=pltpu.VMEM)
    act = jax.ShapeDtypeStruct((rows, width), bf16)
    return pl.pallas_call(
        kernel,
        in_specs=[pl.BlockSpec(memory_space=pltpu.SMEM)] + [vmem] * m + [ANY] + [vmem] * n,
        out_specs=[ANY] * (n + 5) + [vmem, ANY, vmem, vmem],
        out_shape=whole
        + [jax.ShapeDtypeStruct((seqs, span, width), bf16), act, act, act, act,
           jax.ShapeDtypeStruct((groups, heads, span), f32), jax.ShapeDtypeStruct((rows, width), f32),
           jax.ShapeDtypeStruct((8, width), f32), jax.ShapeDtypeStruct((1, deep * lay.devices), f32)],
        scratch_shapes=[pltpu.VMEM((seqs, span, width), bf16)]
        + [pltpu.VMEM(lay.dims + s.shape, bf16) for s in shards[:4]]
        + [pltpu.VMEM((rows, width), bf16)] * 4
        + [pltpu.VMEM((rows, width), f32), pltpu.VMEM((8, 128), f32), pltpu.VMEM(lay.dims + (8, 128), f32),
           pltpu.SemaphoreType.DMA((6,))]
        + sems(lay, p, 0)[:3]
        + [pltpu.SemaphoreType.DMA((lay.blk - 1,)), pltpu.SemaphoreType.DMA((lay.blk - 1,)),
           pltpu.SemaphoreType.DMA],
        compiler_params=pltpu.CompilerParams(collective_id=1, has_side_effects=True, vmem_limit_bytes=60 << 20),
        name="attention_forward",
    )(lengths, *vectors, tokens, *shards)


def attention_backward(lay, x, lengths, wq, wk, wv, wo, q, k, v, att, lse, d_branch, d_one, outer, small, orders, aside):
    seqs, span, width = x.shape
    rows = seqs * span
    heads = lse.shape[1]
    groups = width // GROUP
    pairs = seqs * GROUP // 128
    steps = pairs + 1
    depth = width // lay.devices
    scale = LOG2E / math.sqrt(DH)
    deep, share = outer.shape[1:]
    pieces, lag = 8, 3
    while deep % (pieces * 16):
        pieces //= 2
    outer_cuts = [(i * deep // pieces, deep // pieces, 0, share) for i in range(pieces)]
    small_cut = (0, 8, 0, 128)
    wo_cuts = [(0, depth, i * width // 2, width // 2) for i in range(2)]
    late_cuts = [((0, depth, c * GROUP, GROUP), c) for c in range(groups)]
    bufs = [Scatter.buffers(lay, c, bf16, orders) for c in outer_cuts + wo_cuts]
    bufs += [Scatter.buffers(lay, small_cut, f32, orders)]
    bufs += [Scatter.buffers(lay, c, bf16, aside) for c, _ in late_cuts for _ in range(3)]
    count = len(bufs)
    wide = deep == width
    outer = outer.reshape(lay.dims + outer.shape[1:])

    def kernel(
        len_ref, x_in, wq_ref, wk_ref, wv_ref, wo_ref, q_ref, k_ref, v_ref, att_ref, lse_ref, db_ref, d1_in, outer_in, small_in,
        gq_out, gk_out, gv_out, go_out, outer_out, small_out, dx_out,
        gq_ref, gk_ref, gv_ref, go_ref, xt_ref, do_ref, dq_ref, dk_ref, dv_ref, acc_ref, dx_ref,
        stage_small, stage_ref, send, recv, own, rsend, rrecv, rown, fetch_sem, *held,
    ):
        g = pl.program_id(0)
        here = lay.here()
        base = lax.axis_index("blk") * seqs
        made = []

        def part(grad, cut, out, way, staged=None, turn=False):
            i = len(made)
            made.append(Scatter(
                lay, here, grad, cut, out, held[4 * i : 4 * i + 4], send.at[i], recv.at[i], own.at[i], way, staged, turn))
            return made[-1]

        first = [
            part(outer_in, c, outer_out.at[:, pl.ds(c[0], c[1])] if wide else outer_out.at[pl.ds(c[0], c[1])], orders,
                 stage_ref.at[i % (lag + 1)], wide)
            for i, c in enumerate(outer_cuts)
        ]
        first += [part(go_ref, c, go_out.at[:, pl.ds(c[2], c[3])], orders) for c in wo_cuts]
        first += [part(small_in, small_cut, small_out, orders, stage_small)]
        hooks = Hooks()
        events = skewed(first, lag)
        hooks.spread(events[lag:], 0, groups * steps - 1)
        finals = []
        for c, group in late_cuts:
            parts = [
                part(ref, c, out.at[:, pl.ds(c[2], c[3])], aside)
                for ref, out in ((gq_ref, gq_out), (gk_ref, gk_out), (gv_ref, gv_out))
            ]
            ready = (group + 1) * steps - 1
            for stage in range(5):
                for i, p in enumerate(parts):
                    hooks.put(ready + i + 3 * stage, (p, stage))
        for k in sorted(hooks.slots):
            if k >= groups * steps - 1:
                finals += hooks.slots.pop(k)
        splits = [
            Resplit(lay, dx_ref.at[pl.ds(s, 1)], dx_out, rsend.at[s], rrecv.at[s], rown.at[s], True, s) for s in range(seqs)
        ]

        @pl.when(g == 0)
        def _():
            lay.greet(here)
            for p, stage in events[:lag]:
                p.stage(stage)
            fetch = [
                pltpu.make_async_copy(x_in, dx_ref, fetch_sem.at[0]),
                pltpu.make_async_copy(d1_in, acc_ref, fetch_sem.at[1]),
            ]
            for c in fetch:
                c.start()
            for c in fetch:
                c.wait()
            for s in range(seqs):
                xt_ref[:, s * span : (s + 1) * span] = dx_ref[s].T

            def output_rows(j, carry):
                cols = pl.ds(pl.multiple_of(j * GROUP, GROUP), GROUP)
                value = dot(att_ref[:, cols].T, db_ref[...].reshape(rows, width)).astype(bf16)
                for d in range(GROUP // depth):
                    go_ref[lay.place(j * (GROUP // depth) + d)] = value[d * depth : (d + 1) * depth]
                return carry

            lax.fori_loop(0, groups, output_rows, 0)

        do_ref[...] = dot_t(db_ref[...].reshape(rows, width), wo_ref[...]).astype(bf16)

        def pair_step(i, carry):
            s, pair = i // (GROUP // 128), lax.rem(i, GROUP // 128)
            at = (pl.ds(pl.multiple_of(s * span, span), span), pl.ds(pl.multiple_of(pair * 128, 128), 128))
            length = len_ref[base + s]
            qs, ks, vs, dos = q_ref[at], k_ref[at], v_ref[at], do_ref[at]
            lane = lax.broadcasted_iota(jnp.int32, (span, 128), 1)
            keep = lax.broadcasted_iota(jnp.int32, (span, 1), 0) < length
            kt = ks.T
            dqs, dks, dvs = [], [], []
            for h in range(2):
                mine = (lane < DH) if h == 0 else (lane >= DH)
                zero = jnp.zeros_like(ks)
                st = dot_t(jnp.where(mine, ks, zero), qs) * scale
                p = jnp.where(keep, jnp.exp2(st - lse_ref[0, pl.ds(i * 2 + h, 1)]), 0.0)
                dp = dot_t(jnp.where(mine, vs, zero), dos)
                delta = jnp.sum(p * dp, axis=0, keepdims=True)
                ds = (p * (dp - delta)).astype(bf16)
                dvs.append(dot(p.astype(bf16), dos))
                dks.append(dot(ds, qs))
                dqs.append(dot(kt[h * DH : (h + 1) * DH], ds))
            low_half = lane < DH
            unit = 1.0 / math.sqrt(DH)
            dv_ref[at] = jnp.where(low_half, dvs[0], dvs[1]).astype(bf16)
            dk_ref[at] = (jnp.where(low_half, dks[0], dks[1]) * unit).astype(bf16)
            dq_ref[at] = (jnp.concatenate(dqs, axis=0).T * unit).astype(bf16)

            @pl.when(pair == GROUP // 128 - 1)
            def _():
                mine = at[0]
                acc_ref[mine] += (
                    dot_t(dq_ref[mine], wq_ref[...]) + dot_t(dk_ref[mine], wk_ref[...]) + dot_t(dv_ref[mine], wv_ref[...])
                )

            for n in range(seqs):
                @pl.when((g == groups - 1) & (i == (n + 1) * (GROUP // 128) - 1))
                def _():
                    dx_ref[n] = acc_ref[n * span : (n + 1) * span].astype(bf16)
                    splits[n].start()

            hooks.at(g * steps + i, [k for k in range(groups * steps) if k % steps < pairs])
            return carry

        lax.fori_loop(0, pairs, pair_step, 0)
        xt = xt_ref[...]
        cols = (slice(None),) * 5 + (pl.ds(pl.multiple_of(g * GROUP, GROUP), GROUP),)
        for grad, low in ((gq_ref, dq_ref), (gk_ref, dk_ref), (gv_ref, dv_ref)):
            grad[cols] = dot(xt, low[...]).astype(bf16).reshape(lay.dims + (depth, GROUP))
        hooks.at(g * steps + pairs, [k for k in range(groups * steps) if k % steps == pairs])

        @pl.when(g == groups - 1)
        def _():
            for p, stage in finals:
                p.stage(stage)
            for p in made:
                p.drain()
            for split in splits:
                split.finish()

    col = pl.BlockSpec((width, GROUP), lambda g, *_: (0, g))
    row = pl.BlockSpec((GROUP, width), lambda g, *_: (g, 0))
    act = pl.BlockSpec((rows, GROUP), lambda g, *_: (0, g))
    vmem = pl.BlockSpec(memory_space=pltpu.VMEM)
    grad = pltpu.VMEM(lay.dims + (depth, width), bf16)
    no_core = tuple(lay.size[n] for n in lay.order if n != "c")
    shard = jax.ShapeDtypeStruct((depth, width), f32)
    return pl.pallas_call(
        kernel,
        grid_spec=pltpu.PrefetchScalarGridSpec(
            num_scalar_prefetch=0,
            grid=(groups,),
            in_specs=[pl.BlockSpec(memory_space=pltpu.SMEM), ANY, col, col, col, row, act, act, act, once((rows, width)),
                      pl.BlockSpec((1, heads, span), lambda g, *_: (g, 0, 0)), once((seqs, span, width)), ANY, ANY, ANY],
            out_specs=[once((depth, width))] * 4 + [once((share, deep) if wide else (deep, share)), once((8, 128)), ANY],
            scratch_shapes=[grad] * 4
            + [pltpu.VMEM((width, rows), bf16)] + [pltpu.VMEM((rows, GROUP), bf16)] * 4
            + [pltpu.VMEM((rows, width), f32), pltpu.VMEM((seqs, span, width), bf16)]
            + [pltpu.VMEM(no_core + (8, 128), f32)] + [pltpu.VMEM((lag + 1,) + no_core + (deep // pieces, share), bf16)]
            + sems(lay, count, 0)[:3]
            + sems(lay, 0, seqs)[3:] + [pltpu.SemaphoreType.DMA((2,))]
            + [b for bs in bufs for b in bs],
        ),
        out_shape=[shard] * 4
        + [jax.ShapeDtypeStruct((share, deep) if wide else (deep, share), f32), jax.ShapeDtypeStruct((8, 128), f32),
           jax.ShapeDtypeStruct((seqs * lay.blk, span // lay.blk, width), bf16)],
        compiler_params=pltpu.CompilerParams(
            collective_id=3, has_side_effects=True, vmem_limit_bytes=63 << 20),
        name="attention_backward",
    )(lengths, x, wq, wk, wv, wo, q, k, v, att, lse, d_branch, d_one, outer, small)


TILE = 512
CHUNK = 512


def feed_forward(lay, h1, teacher, out_grad, lengths, vecs, bias_inner, w1, w2, orders):
    rows, width = h1.shape
    hidden = w1.shape[1]
    seqs = teacher.shape[0] // lay.blk
    span = rows // seqs
    devices = lay.devices
    tiles = hidden // TILE
    share, share1 = hidden // devices, width // devices
    per_tile = TILE // share
    wide = share % 128 == 0
    pieces, depth, lag, kept = tiles, width // devices, 2, 4
    columns = hidden // pieces
    bufs = Scatter.buffers(lay, (0, depth, 0, columns), bf16, orders)

    def kernel(
        len_ref, h1_ref, teach_in, og_in, vec_ref, b1_ref, w1_ref, w2_ref,
        layer_out, d1_ref, db_out, gw1_out, gw2_ref, small_ref,
        low_ref, lowt_ref, act_ref, slope_ref, acc_ref, do_ref, dot_ref, inv1_ref, di_ref, db_ref, gw1_ref, sums_ref, gb1_ref,
        rsend, rrecv, rown, send, recv, own, *held,
    ):
        t = pl.program_id(0)
        here = lay.here()
        base = lax.axis_index("blk") * seqs
        rows_in = [
            Resplit(lay, src, dst.at[pl.ds(n, 1)], rsend.at[2 * n + i], rrecv.at[2 * n + i], rown.at[2 * n + i], first=n)
            for n in range(seqs) for i, (src, dst) in enumerate(((teach_in, do_ref), (og_in, db_ref)))
        ]
        rows_out = Resplit(lay, low_ref, layer_out, rsend.at[2 * seqs], rrecv.at[2 * seqs], rown.at[2 * seqs], True)
        sums = [
            Scatter(
                lay, here, gw1_ref.at[i % kept], (0, depth, 0, columns), gw1_out.at[:, pl.ds(i * columns, columns)],
                held[4 * i : 4 * i + 4], send.at[i], recv.at[i], own.at[i], orders)
            for i in range(pieces)
        ]
        hooks = Hooks()
        for slot in range(pieces + 4 * lag):
            for i in range(pieces):
                stage, rest = divmod(slot - i, lag)
                if rest == 0 and 0 <= stage < 5:
                    hooks.put(slot, (sums[i], stage))
        last = max(hooks.slots)
        span_of = lambda row: (row // span, pl.ds(row % span, CHUNK))
        gain1, shift1 = vec_ref[0:1], vec_ref[1:2]
        bias2, gain2, shift2 = vec_ref[2:3], vec_ref[3:4], vec_ref[4:5]

        @pl.when(t == 0)
        def _():
            lay.greet(here)
            for split in rows_in[:2]:
                split.start()
            fetch = pltpu.make_async_copy(h1_ref, d1_ref, own.at[pieces])
            fetch.start()
            fetch.wait()
            sums_ref[...] = jnp.zeros_like(sums_ref)

            def norm(i, carry):
                at = pl.ds(pl.multiple_of(i * 128, 128), 128)
                seq = (i * 128) // span
                there = (seq, pl.ds(pl.multiple_of(i * 128 - seq * span, 128), 128))
                h = d1_ref[at]
                centred = h - jnp.mean(h, axis=-1, keepdims=True)
                inverse = lax.rsqrt(jnp.mean(centred * centred, axis=-1, keepdims=True) + 1e-12)
                normal = centred * inverse
                d1_ref[at] = normal
                inv1_ref[at] = inverse
                low = (normal * gain1 + shift1).astype(bf16)
                low_ref[there] = low
                lowt_ref[:, at] = low.T
                return carry

            lax.fori_loop(0, rows // 128, norm, 0)
            acc_ref[...] = jnp.zeros_like(acc_ref)

        for n in range(1, seqs):
            @pl.when(t == n * tiles // seqs)
            def _():
                for split in rows_in[2 * n : 2 * n + 2]:
                    split.start()

        @pl.when(t < tiles)
        def _():
            for i in range(rows // CHUNK):
                at = slice(i * CHUNK, (i + 1) * CHUNK)
                inner = dot(low_ref[span_of(i * CHUNK)], w1_ref[...]) + b1_ref[...]
                cum = 0.5 * (1.0 + lax.erf(inner * (1.0 / math.sqrt(2.0))))
                density = jnp.exp(-0.5 * inner * inner) * (1.0 / math.sqrt(2.0 * math.pi))
                active = (inner * cum).astype(bf16)
                act_ref[t, at] = active
                slope_ref[t, at] = (cum + inner * density).astype(bf16)
                acc_ref[at] += dot(active, w2_ref[...])

        @pl.when(t == tiles)
        def _():
            inv = vec_ref[5:6]

            def middle(i, carry):
                at = pl.ds(pl.multiple_of(i * 128, 128), 128)
                normed = d1_ref[at] * gain1 + shift1
                h2 = normed + acc_ref[at] + bias2
                centred = h2 - jnp.mean(h2, axis=-1, keepdims=True)
                inverse = lax.rsqrt(jnp.mean(centred * centred, axis=-1, keepdims=True) + 1e-12)
                normal = centred * inverse
                result = normal * gain2 + shift2
                seq = (i * 128) // span
                first = i * 128 - seq * span
                there = (seq, pl.ds(pl.multiple_of(first, 128), 128))
                low_ref[there] = result.astype(bf16)
                pos = first + lax.broadcasted_iota(jnp.int32, (128, 1), 0)
                valid = (pos < len_ref[base + seq]).astype(f32)
                deviation = (result - do_ref[there].astype(f32)) * valid
                grad = db_ref[there].astype(f32) * valid + (2.0 * inv) * deviation
                sums_ref[0:1] += jnp.sum(deviation * deviation, axis=0, keepdims=True)
                sums_ref[1:2] += jnp.sum(grad * normal, axis=0, keepdims=True)
                sums_ref[2:3] += jnp.sum(grad, axis=0, keepdims=True)
                scaled = grad * gain2
                mean = jnp.mean(scaled, axis=-1, keepdims=True)
                along = jnp.mean(scaled * normal, axis=-1, keepdims=True)
                d_two = inverse * (scaled - mean - normal * along)
                acc_ref[at] = d_two
                low = d_two.astype(bf16)
                sums_ref[3:4] += jnp.sum(low.astype(f32), axis=0, keepdims=True)
                do_ref[there] = low
                dot_ref[:, at] = low.T
                return carry

            for n in range(seqs):
                for split in rows_in[2 * n : 2 * n + 2]:
                    split.finish()
                lax.fori_loop(n * span // 128, (n + 1) * span // 128, middle, 0)
            rows_out.start()

        @pl.when((t > tiles) & (t <= 2 * tiles))
        def _():
            j = t - tiles - 1
            total = jnp.zeros((1, TILE), f32)
            for i in range(rows // CHUNK):
                at = slice(i * CHUNK, (i + 1) * CHUNK)
                d_act = dot_t(do_ref[span_of(i * CHUNK)], w2_ref[...])
                d_in = (d_act * slope_ref[j, at].astype(f32)).astype(bf16)
                total += jnp.sum(d_in.astype(f32), axis=0, keepdims=True)
                di_ref[at] = d_in
                acc_ref[at] += dot_t(d_in, w1_ref[...])
            gb1_ref[:, pl.ds(pl.multiple_of(j * TILE, TILE), TILE)] = total
            value = dot(lowt_ref[...], di_ref[...]).astype(bf16)
            gw1_ref[lax.rem(j, kept)] = value.reshape(lay.dims + (depth, TILE))
            hooks.at(j, range(tiles))

        @pl.when(t == 2 * tiles)
        def _():
            def back(i, carry):
                at = pl.ds(pl.multiple_of(i * 128, 128), 128)
                seq = (i * 128) // span
                there = (seq, pl.ds(pl.multiple_of(i * 128 - seq * span, 128), 128))
                grad, normal = acc_ref[at], d1_ref[at]
                sums_ref[4:5] += jnp.sum(grad * normal, axis=0, keepdims=True)
                sums_ref[5:6] += jnp.sum(grad, axis=0, keepdims=True)
                scaled = grad * gain1
                mean = jnp.mean(scaled, axis=-1, keepdims=True)
                along = jnp.mean(scaled * normal, axis=-1, keepdims=True)
                d_one = inv1_ref[at] * (scaled - mean - normal * along)
                d1_ref[at] = d_one
                db_ref[there] = d_one.astype(bf16)
                return carry

            lax.fori_loop(0, rows // 128, back, 0)

        @pl.when(t > 2 * tiles)
        def _():
            j = t - 2 * tiles - 1
            gw2 = dot(dot_ref[...], act_ref[j]).astype(bf16)
            if wide:
                for d in range(per_tile):
                    gw2_ref[d] = gw2[:, d * share : (d + 1) * share]
            else:
                gw2_ref[...] = gw2
            hooks.at(t - tiles - 1, range(tiles, 2 * tiles))

        @pl.when(t == 2 * tiles + 1)
        def _():
            small_ref[...] = jnp.zeros_like(small_ref)
            loss = jnp.broadcast_to(jnp.sum(sums_ref[0:1], axis=-1, keepdims=True), (1, 128))
            for d in range(devices):
                at = lay.place(d)
                small_ref[at + (slice(0, 5), slice(0, share1))] = sums_ref[1:6, d * share1 : (d + 1) * share1]
                small_ref[at + (slice(5, 6), slice(0, share))] = gb1_ref[:, d * share : (d + 1) * share]
                small_ref[at + (slice(6, 7),)] = loss

        @pl.when(t == 3 * tiles)
        def _():
            save = pltpu.make_async_copy(db_ref, db_out, own.at[pieces])
            save.start()
            for k in range(2 * tiles, last + 1):
                hooks.run(k)
            for part in sums:
                part.drain()
            rows_out.finish()
            save.wait()

    def tile(t, *_):
        return jnp.where(t < tiles, t, jnp.clip(t - tiles - 1, 0, tiles - 1))

    def outer_tile(t, *_):
        return jnp.maximum(t - 2 * tiles - 1, 0)

    full = once((rows, width))
    vec = pl.BlockSpec((1, TILE), lambda t, *_: (0, tile(t)))
    low = pltpu.VMEM((seqs, span, width), bf16)
    return pl.pallas_call(
        kernel,
        grid_spec=pltpu.PrefetchScalarGridSpec(
            num_scalar_prefetch=0,
            grid=(3 * tiles + 1,),
            in_specs=[
                pl.BlockSpec(memory_space=pltpu.SMEM), ANY, ANY, ANY, once((8, width)), vec,
                pl.BlockSpec((width, TILE), lambda t, *_: (0, tile(t))),
                pl.BlockSpec((TILE, width), lambda t, *_: (tile(t), 0)),
            ],
            out_specs=[
                ANY, full, ANY, once((depth, hidden)),
                pl.BlockSpec((per_tile, width, share), lambda t, *_: (outer_tile(t), 0, 0))
                if wide else pl.BlockSpec((width, TILE), lambda t, *_: (0, outer_tile(t))),
                once(lay.dims + (8, 128)),
            ],
            scratch_shapes=[
                low, pltpu.VMEM((width, rows), bf16),
                pltpu.VMEM((tiles, rows, TILE), bf16), pltpu.VMEM((tiles, rows, TILE), bf16),
                pltpu.VMEM((rows, width), f32), low, pltpu.VMEM((width, rows), bf16),
                pltpu.VMEM((rows, 1), f32), pltpu.VMEM((rows, TILE), bf16), low,
                pltpu.VMEM((kept,) + lay.dims + (depth, columns), bf16),
                pltpu.VMEM((8, width), f32), pltpu.VMEM((1, hidden), f32),
            ]
            + sems(lay, 0, 2 * seqs + 1)[3:]
            + sems(lay, pieces + 1, 0)[:3]
            + bufs * pieces,
        ),
        out_shape=[
            jax.ShapeDtypeStruct(teacher.shape, bf16),
            jax.ShapeDtypeStruct((rows, width), f32),
            jax.ShapeDtypeStruct((seqs, span, width), bf16),
            jax.ShapeDtypeStruct((depth, hidden), f32),
            jax.ShapeDtypeStruct((devices, width, share) if wide else (width, hidden), bf16),
            jax.ShapeDtypeStruct(lay.dims + (8, 128), f32),
        ],
        compiler_params=pltpu.CompilerParams(
            collective_id=2, has_side_effects=True, vmem_limit_bytes=63 << 20),
        name="feed_forward",
    )(lengths, h1, teacher, out_grad, vecs, bias_inner, w1, w2)


def finish(d_tokens, small, vecs, share, deep, whole):
    seqs, span, width = d_tokens.shape
    n, steps = len(whole), 4

    def kernel(dx_ref, small_ref, vec_ref, *refs):
        ins, refs = refs[:n], refs[n:]
        dx_out, loss_ref, bias_ref = refs[:3]
        for a, b in zip(ins, refs[3:]):
            b[...] = a[...]
        loss_ref[...] = small_ref[6:7, :1] * vec_ref[5:6, :1]
        bias_ref[...] = small_ref[5:6, :deep]
        dx_out[...] = dx_ref[...].astype(f32)

    def block(a):
        if a.ndim == 3:
            return pl.BlockSpec((a.shape[0] // steps,) + a.shape[1:], lambda i: (i, 0, 0))
        return pl.BlockSpec((a.shape[0], a.shape[1] // steps), lambda i: (0, i))

    like = lambda a, dtype: jax.ShapeDtypeStruct(a.shape, dtype)
    blocks = [block(a) for a in whole]
    out = pl.pallas_call(
        kernel,
        grid=(steps,),
        in_specs=[block(d_tokens), once((8, 128)), once((8, width))] + blocks,
        out_specs=[block(d_tokens), once((1, 1)), once((1, deep))] + blocks,
        out_shape=[like(d_tokens, f32), jax.ShapeDtypeStruct((1, 1), f32), jax.ShapeDtypeStruct((1, deep), f32)]
        + [like(a, a.dtype) for a in whole],
        compiler_params=pltpu.CompilerParams(vmem_limit_bytes=63 << 20),
        name="finish",
    )(d_tokens, small, vecs, *whole)
    return out[0], out[1], out[2], out[3:]


def cut(shape, which, pieces, orders, columns=False):
    rows, wide = shape
    if columns:
        step = wide // pieces
        return [(which, (0, rows, i * step, step), orders) for i in range(pieces)]
    while pieces > 1 and rows % (pieces * 16):
        pieces -= 1
    step = rows // pieces
    return [(which, (i * step, step), orders) for i in range(pieces)]


def shards(
    lay, tokens, lengths, teacher, out_grad, w_query, w_key, w_value, w_output, gain_one, shift_one,
    w_inner, bias_inner, w_outer, bias_outer, gain_two, shift_two,
):
    width = tokens.shape[2]
    hidden = w_inner.shape[1]
    devices = lay.devices
    there = (("z", "x", "y"), ("z", "y", "x"))
    back = (("y", "x", "z"), ("x", "y", "z"))
    aside = (("x", "y", "z"),) * 2
    share, deep = gain_one.shape[0], bias_inner.shape[0]
    ins = [w_query, w_key, w_value, w_output, w_inner, w_outer]
    parts = [(6, (0, 8), there)]
    for i in range(4):
        parts += cut(ins[i].shape, i, 1, there)
    early = len(parts)
    parts += cut(w_inner.shape, 4, 8, there, True) + cut(w_outer.shape, 5, 8, there)
    vectors = [gain_one, shift_one, bias_outer, gain_two, shift_two, bias_inner]
    wq, wk, wv, wo, w1, w2, x, q, k, v, att, lse, h1, vecs, bias1 = attention_forward(
        lay, tokens, lengths, vectors, ins, parts, early
    )
    wq, wk, wv, wo = (w.reshape(width, width) for w in (wq, wk, wv, wo))
    w1, w2 = w1.reshape(width, hidden), w2.reshape(hidden, width)
    layer_out, d_one, d_branch, g_inner, gw2, small = feed_forward(
        lay, h1, teacher, out_grad, lengths, vecs, bias1, w1, w2, back
    )
    if gw2.ndim == 2:
        gw2 = gw2.T.reshape(devices, hidden // devices, width)
    g_query, g_key, g_value, g_output, g_outer, small, d_tokens = attention_backward(
        lay, x, lengths, wq, wk, wv, wo, q, k, v, att, lse, d_branch, d_one, gw2, small, back, aside
    )
    d_tokens, loss, g_bias, copied = finish(
        d_tokens, small, vecs, share, deep, [layer_out, g_query, g_key, g_value, g_output, g_inner, g_outer]
    )
    layer_out, g_query, g_key, g_value, g_output, g_inner, g_outer = copied
    vec = lambda i: small[i, :share]
    return (
        loss[0, 0],
        layer_out,
        d_tokens,
        g_query,
        g_key,
        g_value,
        g_output,
        vec(3),
        vec(4),
        g_inner,
        g_bias[0],
        g_outer,
        vec(2),
        vec(0),
        vec(1),
    )


def solution(mesh):
    lay = Layout(mesh)
    rows = P("dp", "blk", None)
    weight = P(("dp", "blk"), None)
    vector = P(("dp", "blk"))
    return jax.shard_map(
        lambda *args: shards(lay, *args),
        mesh=mesh,
        in_specs=(
            rows, P("dp"), rows, rows, weight, weight, weight, weight, vector, vector,
            weight, vector, weight, vector, vector, vector,
        ),
        out_specs=(
            P(), rows, rows, weight, weight, weight, weight, vector, vector,
            weight, vector, weight, vector, vector, vector,
        ),
        check_vma=False,
    )
```

```python
import math

import jax
import jax.numpy as jnp
from jax import lax
from jax.experimental import pallas as pl
from jax.experimental.pallas import tpu as pltpu
from jax.sharding import PartitionSpec as P

ANY = pl.BlockSpec(memory_space=pl.ANY)
MESH = pl.DeviceIdType.MESH
f32 = jnp.float32
bf16 = jnp.bfloat16


class Layout:
    def __init__(self, mesh):
        dp, blk = mesh.shape["dp"], mesh.shape["blk"]
        if dp == 8 and blk == 4:
            dims = [("z", "dp", 2, 4), ("x", "dp", 1, 2), ("y", "blk", 2, 2), ("c", "blk", 1, 2)]
        else:
            dims = [("z", "dp", dp // 4, 4), ("x", "dp", 2, dp // 8), ("c", "dp", 1, 2), ("y", "blk", 1, blk)]
        self.order = [d[0] for d in dims]
        self.axis = {d[0]: d[1] for d in dims}
        self.stride = {d[0]: d[2] for d in dims}
        self.size = {d[0]: d[3] for d in dims}
        self.dims = tuple(d[3] for d in dims)
        self.blk = blk
        self.devices = dp * blk
        self.slot = {}
        count = 0
        for name in self.order:
            self.slot[name] = count
            count += self.size[name] - 1
        self.slots = count

    def here(self):
        return {
            name: lax.rem(lax.axis_index(self.axis[name]) // self.stride[name], self.size[name])
            for name in self.order
        }

    def step_to(self, here, name, distance):
        there = lax.rem(here[name] + distance, self.size[name])
        index = lax.axis_index(self.axis[name]) + (there - here[name]) * self.stride[name]
        return there, {self.axis[name]: index}

    def at(self, here, whole, changed=(), names=None):
        changed = dict(changed)
        return tuple(
            slice(None) if name in whole else changed.get(name, here[name])
            for name in (names or self.order)
        )

    def place(self, device):
        index = []
        for size in reversed(self.dims):
            index.append(lax.rem(device, size))
            device = device // size
        return tuple(reversed(index))

    def greet(self, here):
        barrier = pltpu.get_barrier_semaphore()
        count = 0
        for name in self.order:
            if self.axis[name] == "blk":
                continue
            for distance in range(1, self.size[name]):
                _, device = self.step_to(here, name, distance)
                pl.semaphore_signal(barrier, inc=1, device_id=device, device_id_type=MESH)
                count += 1
        me = lax.axis_index("blk")
        for distance in range(1, self.blk):
            pl.semaphore_signal(
                barrier, inc=1, device_id={"blk": lax.rem(me + distance, self.blk)}, device_id_type=MESH
            )
            count += 1
        pl.semaphore_wait(barrier, count)


def window(cut):
    if len(cut) == 2:
        return (pl.ds(*cut),)
    return (pl.ds(cut[0], cut[1]), pl.ds(cut[2], cut[3]))


def by_core(here, orders, make):
    if orders[0] == orders[1]:
        make(orders[0])
        return
    for core in range(2):
        @pl.when(here["c"] == core)
        def _():
            make(orders[core])


class Gather:
    stages = 5

    def __init__(self, lay, here, src, full, rows, send, recv, own, orders):
        self.lay, self.here = lay, here
        self.rows = window(rows)
        self.src, self.full = src.at[self.rows], full
        self.send, self.recv, self.own = send, recv, own
        self.orders = orders

    def line(self, name, whole):
        copies = []
        place = self.full.at[self.lay.at(self.here, whole) + self.rows]
        source = self.src if not whole else place
        for distance in range(1, self.lay.size[name]):
            _, device = self.lay.step_to(self.here, name, distance)
            slot = self.lay.slot[name] + distance - 1
            copies.append(
                pltpu.make_async_remote_copy(
                    src_ref=source, dst_ref=place, send_sem=self.send.at[slot], recv_sem=self.recv.at[slot],
                    device_id=device, device_id_type=MESH,
                )
            )
        return copies

    def local(self):
        return pltpu.make_async_copy(self.src, self.full.at[self.lay.at(self.here, ()) + self.rows], self.own)

    def stage(self, k):
        if k == 1:
            self.local().wait()

        def make(order):
            lines = tuple(order) + ("c",)
            if k > 0:
                for c in self.line(lines[k - 1], lines[: k - 1]):
                    c.wait_recv()
            if k < 4:
                for c in self.line(lines[k], lines[:k]):
                    c.start()

        if k == 0:
            self.local().start()
        by_core(self.here, self.orders, make)

    def drain(self):
        def make(order):
            lines = tuple(order) + ("c",)
            for k in range(4):
                for c in self.line(lines[k], lines[:k]):
                    c.wait_send()
        by_core(self.here, self.orders, make)


class Resplit:
    def __init__(self, lay, src, dst, send, recv, own, back=False, first=0):
        self.lay, self.src, self.dst = lay, src, dst
        self.first = first
        self.send, self.recv, self.own = send, recv, own
        self.me = lax.axis_index("blk")
        self.back = back
        self.seqs = (src if back else dst).shape[0]
        self.total = (dst if back else src).shape[0] // lay.blk
        self.span = (dst if back else src).shape[1]

    def ends(self, there):
        if self.back:
            return (self.src.at[:, pl.ds(there * self.span, self.span)],
                    self.dst.at[pl.ds(self.me * self.total + self.first, self.seqs)])
        return (self.src.at[pl.ds(there * self.total + self.first, self.seqs)],
                self.dst.at[:, pl.ds(self.me * self.span, self.span)])

    def copies(self):
        out = []
        for distance in range(1, self.lay.blk):
            there = lax.rem(self.me + distance, self.lay.blk)
            src, dst = self.ends(there)
            out.append(
                pltpu.make_async_remote_copy(
                    src_ref=src, dst_ref=dst,
                    send_sem=self.send.at[distance - 1], recv_sem=self.recv.at[distance - 1],
                    device_id={"blk": there}, device_id_type=MESH,
                )
            )
        return out

    def local(self):
        src, dst = self.ends(self.me)
        return pltpu.make_async_copy(src, dst, self.own)

    def start(self):
        self.local().start()
        for c in self.copies():
            c.start()

    def finish(self):
        self.local().wait()
        for c in self.copies():
            c.wait()


class Scatter:
    stages = 5

    def __init__(self, lay, here, grad, cut, out, bufs, send, recv, own, orders, staged=None, turn=False):
        self.turn = turn
        self.lay, self.here, self.grad, self.cut = lay, here, grad, window(cut)
        self.out, self.held, self.recvs, self.staged = out, bufs[0], bufs[1:], staged
        self.send, self.recv, self.own = send, recv, own
        self.orders = orders
        self.names = [n for n in lay.order if n != "c"]

    @staticmethod
    def buffers(lay, cut, dtype, orders):
        shape = (cut[1], cut[3])
        names = [n for n in lay.order if n != "c"]
        out = [pltpu.VMEM(tuple(lay.size[n] for n in names) + shape, dtype)]
        for k in range(3):
            lines = orders[0][k + 1 :]
            left = tuple(lay.size[n] for n in names if n in lines)
            out.append(pltpu.VMEM((lay.size[orders[0][k]] - 1,) + left + shape, dtype))
        return out

    def local(self):
        return pltpu.make_async_copy(
            self.grad.at[self.lay.at(self.here, self.names) + self.cut], self.staged, self.own)

    def core(self):
        there, device = self.lay.step_to(self.here, "c", 1)
        slot = self.lay.slot["c"]
        return pltpu.make_async_remote_copy(
            src_ref=self.grad.at[self.lay.at(self.here, self.names, {"c": there}) + self.cut], dst_ref=self.held,
            send_sem=self.send.at[slot], recv_sem=self.recv.at[slot], device_id=device, device_id_type=MESH)

    def line(self, order, k):
        name, left = order[k], order[k + 1 :]
        copies = []
        for distance in range(1, self.lay.size[name]):
            there, device = self.lay.step_to(self.here, name, distance)
            slot = self.lay.slot[name] + distance - 1
            copies.append(
                pltpu.make_async_remote_copy(
                    src_ref=self.held.at[self.lay.at(self.here, left, {name: there}, self.names)],
                    dst_ref=self.recvs[k].at[distance - 1],
                    send_sem=self.send.at[slot], recv_sem=self.recv.at[slot],
                    device_id=device, device_id_type=MESH,
                )
            )
        return copies

    def add(self, order, k):
        left = [n for n in self.names if k < 0 or n in order[k + 1 :]]
        steps = self.lay.size[left[0]] if left else 1

        def one(i, carry):
            index = {n: slice(None) for n in left}
            if left:
                index[left[0]] = i
            mine = tuple(index.get(n, self.here[n]) for n in self.names)
            alone = k < 0 or (k < 2 and self.lay.size[order[k]] == 2)
            wide = self.held.dtype if alone else f32
            value = self.held[mine].astype(wide)
            if k >= 0:
                theirs = tuple(index[n] for n in left)
                for d in range(self.lay.size[order[k]] - 1):
                    value = value + self.recvs[k][(d,) + theirs].astype(wide)
            elif self.staged is not None:
                value = value + self.staged[mine].astype(wide)
            else:
                value = value + self.grad[self.lay.at({**self.here, **index}, ()) + self.cut].astype(wide)
            if k == 2:
                self.out[...] = value.T if self.turn else value
            else:
                self.held[mine] = value.astype(self.held.dtype)
            return carry

        lax.fori_loop(0, steps, one, 0)

    def stage(self, k):
        if k == 0:
            self.core().start()
            if self.staged is not None:
                self.local().start()
            return
        if k == 1:
            if self.staged is not None:
                self.local().wait()
            self.core().wait()
            self.add(None, -1)

        def make(order):
            if k > 1:
                for c in self.line(order, k - 2):
                    c.wait_recv()
                self.add(order, k - 2)
            if k < 4:
                for c in self.line(order, k - 1):
                    c.start()

        by_core(self.here, self.orders, make)

    def drain(self):
        def make(order):
            for k in range(3):
                for c in self.line(order, k):
                    c.wait_send()

        by_core(self.here, self.orders, make)


def skewed(parts, lag=1, stages=5):
    events = []
    for t in range(len(parts) + lag * (stages - 1)):
        for i, part in enumerate(parts):
            stage, rest = divmod(t - i, lag)
            if rest == 0 and 0 <= stage < stages:
                events.append((part, stage))
    return events


class Hooks:
    def __init__(self):
        self.slots = {}

    def put(self, slot, event):
        self.slots.setdefault(slot, []).append(event)

    def spread(self, events, first, last):
        for n, event in enumerate(events):
            self.put(first + n * (last - first) // len(events), event)

    def run(self, slot):
        for part, stage in self.slots.get(slot, ()):
            part.stage(stage)

    def at(self, step, slots):
        for k in slots:
            if k in self.slots:
                pl.when(step == k)(lambda k=k: self.run(k))


def sems(lay, n, m):
    dma = pltpu.SemaphoreType.DMA
    n, m = max(n, 1), max(m, 1)
    return [dma((n, lay.slots)), dma((n, lay.slots)), dma((n,)), dma((m, lay.blk - 1)), dma((m, lay.blk - 1)), dma((m,))]


DH = 64
LOG2E = math.log2(math.e)
GROUP = 256


def dot(a, b):
    return lax.dot_general(a, b, (((1,), (0,)), ((), ())), preferred_element_type=f32)


def dot_t(a, b):
    return lax.dot_general(a, b, (((1,), (1,)), ((), ())), preferred_element_type=f32)


def once(shape):
    return pl.BlockSpec(shape, lambda *_: (0,) * len(shape), pipeline_mode=pl.Buffered(1))


def attention_forward(lay, tokens, lengths, vectors, shards, parts, early):
    width = tokens.shape[2]
    seqs, span = tokens.shape[0] // lay.blk, tokens.shape[1] * lay.blk
    rows = seqs * span
    groups = width // GROUP
    scale = LOG2E / math.sqrt(DH)
    heads = seqs * GROUP // DH
    pairs = seqs * GROUP // 128
    n, p, m = len(shards), len(parts), len(vectors)
    share, deep = vectors[0].shape[0], vectors[-1].shape[0]
    slots = pairs + 3

    def kernel(len_ref, *refs):
        vecs, refs = refs[:m], refs[m:]
        tok_ref, refs = refs[0], refs[1:]
        ins, refs = refs[:n], refs[n:]
        fulls, refs = refs[:n], refs[n:]
        xt_out, q_out, k_out, v_out, att_out, lse_ref, h1_out, vec_out, bias_out = refs[:9]
        x_ref, wq_ref, wk_ref, wv_ref, wo_ref, q_ref, k_ref, v_ref, att_ref, h1_ref, pack_ref, packs_ref, low_ref, xt_ref = refs[9:23]
        load, send, recv, own, rsend, rrecv, rown = refs[23:]
        ins, fulls = list(ins) + [pack_ref], list(fulls) + [packs_ref]
        here = lay.here()
        pack_ref[...] = jnp.zeros_like(pack_ref)
        for i, vec in enumerate(vecs):
            pack_ref[i : i + 1, : vec.shape[0]] = vec[...].astype(f32).reshape(1, vec.shape[0])
        tokens_here = len_ref[0]
        for i in range(1, lengths.shape[0]):
            tokens_here = tokens_here + len_ref[i]
        pack_ref[m : m + 1] = jnp.full((1, 128), tokens_here.astype(f32))
        lay.greet(here)
        split = Resplit(lay, tok_ref, x_ref, rsend, rrecv, rown)
        split.start()
        gathers = [
            Gather(lay, here, ins[a], fulls[a], cut, send.at[i], recv.at[i], own.at[i], orders)
            for i, (a, cut, orders) in enumerate(parts)
        ]
        events = skewed(gathers, 3)
        last = max(i for i, (part, stage) in enumerate(events) if part in gathers[:early] and stage == 4)
        for part, stage in events[: last + 1]:
            part.stage(stage)
        split.finish()
        loads = [
            pltpu.make_async_copy(src, dst, load.at[i])
            for i, (src, dst) in enumerate(
                zip(fulls[:4], [wq_ref, wk_ref, wv_ref, wo_ref]))
        ]
        for c in loads:
            c.start()
        for c in loads:
            c.wait()
        hooks = Hooks()
        hooks.spread(events[last + 1 :], 0, groups * slots * 6 // 5)
        base = lax.axis_index("blk") * seqs

        def columns(ref, g):
            block = ref[(slice(None),) * 5 + (pl.ds(pl.multiple_of(g * GROUP, GROUP), GROUP),)]
            return block.reshape(width, GROUP)

        def features(ref, g):
            per = GROUP // ref.shape[-2]
            return jnp.concatenate([ref[lay.place(g * per + j)] for j in range(per)], axis=0)

        def step(i, carry):
            g, r = i // pairs, lax.rem(i, pairs)
            cols = pl.ds(pl.multiple_of(g * GROUP, GROUP), GROUP)

            @pl.when(r == 0)
            def _():
                xv = x_ref[...].reshape(rows, width)
                for j, (low, weight) in enumerate(((q_ref, wq_ref), (k_ref, wk_ref), (v_ref, wv_ref))):
                    low[:, cols] = dot(xv, columns(weight, g)).astype(bf16)
                    hooks.at(g * slots + j, range(j, groups * slots, slots))

            @pl.when(i == groups * pairs // 4)
            def _():
                for n in range(seqs):
                    xt_ref[:, n * span : (n + 1) * span] = x_ref[n].T

            @pl.when(i == groups * pairs // 2)
            def _():
                total = jnp.zeros((1, 128), f32)
                for d in range(lay.devices):
                    tile = packs_ref[lay.place(d)]
                    vec_out[0 : m - 1, d * share : (d + 1) * share] = tile[0 : m - 1, :share]
                    bias_out[:, d * deep : (d + 1) * deep] = tile[m - 1 : m, :deep]
                    total = total + tile[m : m + 1]
                inverse = 1.0 / (total / lay.blk * width)
                for d in range(width // 128):
                    vec_out[m - 1 : m, d * 128 : (d + 1) * 128] = inverse

            s, pair = r // (GROUP // 128), lax.rem(r, GROUP // 128)
            at = (pl.ds(pl.multiple_of(s * span, span), span),
                  pl.ds(pl.multiple_of(g * GROUP + pair * 128, 128), 128))
            qs, ks, vs = q_ref[at], k_ref[at], v_ref[at]
            lane = lax.broadcasted_iota(jnp.int32, (span, 128), 1)
            keep = lax.broadcasted_iota(jnp.int32, (span, 1), 0) < len_ref[base + s]
            vt = vs.T
            outs = []
            for h in range(2):
                km = jnp.where((lane < DH) if h == 0 else (lane >= DH), ks, jnp.zeros_like(ks))
                st = dot_t(km, qs) * scale
                st = jnp.where(keep, st, -1e30)
                top = jnp.max(st, axis=0, keepdims=True)
                e = jnp.exp2(st - top)
                den = jnp.sum(e, axis=0, keepdims=True)
                ot = dot(vt[h * DH : (h + 1) * DH], e.astype(bf16))
                outs.append(ot * (1.0 / den))
                lse_ref[g, pl.ds(r * 2 + h, 1)] = top + jnp.log2(den)
            turned = jnp.concatenate(outs, axis=0)
            att_ref[at[1], at[0]] = turned.astype(bf16)
            low_ref[at[0], pl.ds(pl.multiple_of(pair * 128, 128), 128)] = turned.T.astype(bf16)

            @pl.when(r == pairs - 1)
            def _():
                add = dot(low_ref[...], features(wo_ref, g))

                @pl.when(g == 0)
                def _():
                    h1_ref[...] = x_ref[...].reshape(rows, width).astype(f32) + add

                @pl.when(g > 0)
                def _():
                    h1_ref[...] += add

            hooks.at(g * slots + 3 + r, [k for k in range(groups * slots) if k % slots >= 3])
            return carry

        lax.fori_loop(0, groups * pairs, step, 0)
        saves = [
            pltpu.make_async_copy(src, dst, load.at[i])
            for i, (src, dst) in enumerate(
                zip([xt_ref, q_ref, k_ref, v_ref, att_ref, h1_ref], [xt_out, q_out, k_out, v_out, att_out, h1_out]))
        ]
        for c in saves:
            c.start()
        for k in sorted(hooks.slots):
            if k >= groups * slots:
                hooks.run(k)
        for g in gathers:
            g.drain()
        for c in saves:
            c.wait()

    whole = [jax.ShapeDtypeStruct(lay.dims + s.shape, s.dtype) for s in shards]
    vmem = pl.BlockSpec(memory_space=pltpu.VMEM)
    act, turned = jax.ShapeDtypeStruct((rows, width), bf16), jax.ShapeDtypeStruct((width, rows), bf16)
    return pl.pallas_call(
        kernel,
        in_specs=[pl.BlockSpec(memory_space=pltpu.SMEM)] + [vmem] * m + [ANY] + [vmem] * n,
        out_specs=[ANY] * (n + 5) + [vmem, ANY, vmem, vmem],
        out_shape=whole
        + [turned, act, act, act, turned,
           jax.ShapeDtypeStruct((groups, heads, span), f32), jax.ShapeDtypeStruct((rows, width), f32),
           jax.ShapeDtypeStruct((8, width), f32), jax.ShapeDtypeStruct((1, deep * lay.devices), f32)],
        scratch_shapes=[pltpu.VMEM((seqs, span, width), bf16)]
        + [pltpu.VMEM(lay.dims + s.shape, bf16) for s in shards[:4]]
        + [pltpu.VMEM((rows, width), bf16)] * 3 + [pltpu.VMEM((width, rows), bf16)]
        + [pltpu.VMEM((rows, width), f32), pltpu.VMEM((8, 128), f32), pltpu.VMEM(lay.dims + (8, 128), f32),
           pltpu.VMEM((rows, GROUP), bf16), pltpu.VMEM((width, rows), bf16),
           pltpu.SemaphoreType.DMA((6,))]
        + sems(lay, p, 0)[:3]
        + [pltpu.SemaphoreType.DMA((lay.blk - 1,)), pltpu.SemaphoreType.DMA((lay.blk - 1,)),
           pltpu.SemaphoreType.DMA],
        compiler_params=pltpu.CompilerParams(collective_id=1, has_side_effects=True, vmem_limit_bytes=60 << 20),
        name="attention_forward",
    )(lengths, *vectors, tokens, *shards)


def attention_backward(lay, xt, lengths, wq, wk, wv, wo, q, k, v, att, lse, d_branch, d_one, outer, small, orders, aside):
    seqs, span, width = d_branch.shape
    rows = seqs * span
    heads = lse.shape[1]
    groups = width // GROUP
    pairs = seqs * GROUP // 128
    steps = pairs + 1
    depth = width // lay.devices
    scale = LOG2E / math.sqrt(DH)
    deep, share = outer.shape[1:]
    pieces, lag = 8, 3
    while deep % (pieces * 16):
        pieces //= 2
    outer_cuts = [(i * deep // pieces, deep // pieces, 0, share) for i in range(pieces)]
    small_cut = (0, 8, 0, 128)
    wo_cuts = [(0, depth, i * width // 2, width // 2) for i in range(2)]
    late_cuts = [((0, depth, c * GROUP, GROUP), c) for c in range(groups)]
    bufs = [Scatter.buffers(lay, c, bf16, orders) for c in outer_cuts + wo_cuts]
    bufs += [Scatter.buffers(lay, small_cut, f32, orders)]
    bufs += [Scatter.buffers(lay, c, bf16, aside) for c, _ in late_cuts for _ in range(3)]
    count = len(bufs)
    wide = deep == width
    outer = outer.reshape(lay.dims + outer.shape[1:])

    def kernel(
        len_ref, xt_ref, wq_ref, wk_ref, wv_ref, wo_ref, q_ref, k_ref, v_ref, att_ref, lse_ref, db_ref, d1_in, outer_in, small_in,
        gq_out, gk_out, gv_out, go_out, outer_out, small_out, dx_out,
        gq_ref, gk_ref, gv_ref, go_ref, do_ref, dq_ref, dk_ref, dv_ref, acc_ref, dx_ref,
        stage_small, stage_ref, send, recv, own, rsend, rrecv, rown, fetch_sem, *held,
    ):
        g = pl.program_id(0)
        here = lay.here()
        base = lax.axis_index("blk") * seqs
        made = []

        def part(grad, cut, out, way, staged=None, turn=False):
            i = len(made)
            made.append(Scatter(
                lay, here, grad, cut, out, held[4 * i : 4 * i + 4], send.at[i], recv.at[i], own.at[i], way, staged, turn))
            return made[-1]

        first = [
            part(outer_in, c, outer_out.at[:, pl.ds(c[0], c[1])] if wide else outer_out.at[pl.ds(c[0], c[1])], orders,
                 stage_ref.at[i % (lag + 1)], wide)
            for i, c in enumerate(outer_cuts)
        ]
        first += [part(go_ref, c, go_out.at[:, pl.ds(c[2], c[3])], orders) for c in wo_cuts]
        first += [part(small_in, small_cut, small_out, orders, stage_small)]
        hooks = Hooks()
        events = skewed(first, lag)
        hooks.spread(events[lag:], 0, groups * steps - 1)
        finals = []
        for c, group in late_cuts:
            parts = [
                part(ref, c, out.at[:, pl.ds(c[2], c[3])], aside)
                for ref, out in ((gq_ref, gq_out), (gk_ref, gk_out), (gv_ref, gv_out))
            ]
            ready = (group + 1) * steps - 1
            for stage in range(5):
                for i, p in enumerate(parts):
                    hooks.put(ready + i + 3 * stage, (p, stage))
        for k in sorted(hooks.slots):
            if k >= groups * steps - 1:
                finals += hooks.slots.pop(k)
        splits = [
            Resplit(lay, dx_ref.at[pl.ds(s, 1)], dx_out, rsend.at[s], rrecv.at[s], rown.at[s], True, s) for s in range(seqs)
        ]

        @pl.when(g == 0)
        def _():
            lay.greet(here)
            for p, stage in events[:lag]:
                p.stage(stage)
            fetch = pltpu.make_async_copy(d1_in, acc_ref, fetch_sem)
            fetch.start()

            def output_rows(j, carry):
                value = dot(att_ref[pl.ds(pl.multiple_of(j * GROUP, GROUP), GROUP)], db_ref[...].reshape(rows, width)).astype(bf16)
                for d in range(GROUP // depth):
                    go_ref[lay.place(j * (GROUP // depth) + d)] = value[d * depth : (d + 1) * depth]
                return carry

            lax.fori_loop(0, groups, output_rows, 0)
            fetch.wait()

        do_ref[...] = dot_t(db_ref[...].reshape(rows, width), wo_ref[...]).astype(bf16)

        def pair_step(i, carry):
            s, pair = i // (GROUP // 128), lax.rem(i, GROUP // 128)
            at = (pl.ds(pl.multiple_of(s * span, span), span), pl.ds(pl.multiple_of(pair * 128, 128), 128))
            length = len_ref[base + s]
            qs, ks, vs, dos = q_ref[at], k_ref[at], v_ref[at], do_ref[at]
            lane = lax.broadcasted_iota(jnp.int32, (span, 128), 1)
            keep = lax.broadcasted_iota(jnp.int32, (span, 1), 0) < length
            kt = ks.T
            dqs, dks, dvs = [], [], []
            for h in range(2):
                mine = (lane < DH) if h == 0 else (lane >= DH)
                zero = jnp.zeros_like(ks)
                st = dot_t(jnp.where(mine, ks, zero), qs) * scale
                p = jnp.where(keep, jnp.exp2(st - lse_ref[0, pl.ds(i * 2 + h, 1)]), 0.0)
                dp = dot_t(jnp.where(mine, vs, zero), dos)
                delta = jnp.sum(p * dp, axis=0, keepdims=True)
                ds = (p * (dp - delta)).astype(bf16)
                dvs.append(dot(p.astype(bf16), dos))
                dks.append(dot(ds, qs))
                dqs.append(dot(kt[h * DH : (h + 1) * DH], ds))
            low_half = lane < DH
            unit = 1.0 / math.sqrt(DH)
            dv_ref[at] = jnp.where(low_half, dvs[0], dvs[1]).astype(bf16)
            dk_ref[at] = (jnp.where(low_half, dks[0], dks[1]) * unit).astype(bf16)
            dq_ref[at] = (jnp.concatenate(dqs, axis=0).T * unit).astype(bf16)

            @pl.when(pair == GROUP // 128 - 1)
            def _():
                mine = at[0]
                acc_ref[mine] += (
                    dot_t(dq_ref[mine], wq_ref[...]) + dot_t(dk_ref[mine], wk_ref[...]) + dot_t(dv_ref[mine], wv_ref[...])
                )

            for n in range(seqs):
                @pl.when((g == groups - 1) & (i == (n + 1) * (GROUP // 128) - 1))
                def _():
                    dx_ref[n] = acc_ref[n * span : (n + 1) * span].astype(bf16)
                    splits[n].start()

            hooks.at(g * steps + i, [k for k in range(groups * steps) if k % steps < pairs])
            return carry

        lax.fori_loop(0, pairs, pair_step, 0)
        xt = xt_ref[...]
        cols = (slice(None),) * 5 + (pl.ds(pl.multiple_of(g * GROUP, GROUP), GROUP),)
        for grad, low in ((gq_ref, dq_ref), (gk_ref, dk_ref), (gv_ref, dv_ref)):
            grad[cols] = dot(xt, low[...]).astype(bf16).reshape(lay.dims + (depth, GROUP))
        hooks.at(g * steps + pairs, [k for k in range(groups * steps) if k % steps == pairs])

        @pl.when(g == groups - 1)
        def _():
            for p, stage in finals:
                p.stage(stage)
            for p in made:
                p.drain()
            for split in splits:
                split.finish()

    col = pl.BlockSpec((width, GROUP), lambda g, *_: (0, g))
    row = pl.BlockSpec((GROUP, width), lambda g, *_: (g, 0))
    act = pl.BlockSpec((rows, GROUP), lambda g, *_: (0, g))
    vmem = pl.BlockSpec(memory_space=pltpu.VMEM)
    grad = pltpu.VMEM(lay.dims + (depth, width), bf16)
    no_core = tuple(lay.size[n] for n in lay.order if n != "c")
    shard = jax.ShapeDtypeStruct((depth, width), f32)
    return pl.pallas_call(
        kernel,
        grid_spec=pltpu.PrefetchScalarGridSpec(
            num_scalar_prefetch=0,
            grid=(groups,),
            in_specs=[pl.BlockSpec(memory_space=pltpu.SMEM), once((width, rows)), col, col, col, row, act, act, act, once((width, rows)),
                      pl.BlockSpec((1, heads, span), lambda g, *_: (g, 0, 0)), once((seqs, span, width)), ANY, ANY, ANY],
            out_specs=[once((depth, width))] * 4 + [once((share, deep) if wide else (deep, share)), once((8, 128)), ANY],
            scratch_shapes=[grad] * 4
            + [pltpu.VMEM((rows, GROUP), bf16)] * 4
            + [pltpu.VMEM((rows, width), f32), pltpu.VMEM((seqs, span, width), bf16)]
            + [pltpu.VMEM(no_core + (8, 128), f32)] + [pltpu.VMEM((lag + 1,) + no_core + (deep // pieces, share), bf16)]
            + sems(lay, count, 0)[:3]
            + sems(lay, 0, seqs)[3:] + [pltpu.SemaphoreType.DMA]
            + [b for bs in bufs for b in bs],
        ),
        out_shape=[shard] * 4
        + [jax.ShapeDtypeStruct((share, deep) if wide else (deep, share), f32), jax.ShapeDtypeStruct((8, 128), f32),
           jax.ShapeDtypeStruct((seqs * lay.blk, span // lay.blk, width), bf16)],
        compiler_params=pltpu.CompilerParams(
            collective_id=3, has_side_effects=True, vmem_limit_bytes=63 << 20),
        name="attention_backward",
    )(lengths, xt, wq, wk, wv, wo, q, k, v, att, lse, d_branch, d_one, outer, small)


TILE = 512
CHUNK = 512


def feed_forward(lay, h1, teacher, out_grad, lengths, vecs, bias_inner, w1, w2, orders, aside):
    rows, width = h1.shape
    hidden = w1.shape[1]
    seqs = teacher.shape[0] // lay.blk
    span = rows // seqs
    devices = lay.devices
    tiles = hidden // TILE
    share, share1 = hidden // devices, width // devices
    per_tile = TILE // share
    wide = share % 128 == 0
    pieces, depth, lag, kept = tiles, width // devices, 2, 4
    columns = hidden // pieces
    ways = [aside if i % 3 < 2 else orders for i in range(pieces)]

    def kernel(
        len_ref, h1_ref, teach_in, og_in, vec_ref, b1_ref, w1_ref, w2_ref,
        layer_out, d1_ref, db_out, gw1_out, gw2_ref, small_ref,
        low_ref, lowt_ref, act_ref, slope_ref, acc_ref, do_ref, dot_ref, inv1_ref, di_ref, db_ref, gw1_ref, sums_ref, gb1_ref,
        rsend, rrecv, rown, send, recv, own, *held,
    ):
        t = pl.program_id(0)
        here = lay.here()
        base = lax.axis_index("blk") * seqs
        rows_in = [
            Resplit(lay, src, dst.at[pl.ds(n, 1)], rsend.at[2 * n + i], rrecv.at[2 * n + i], rown.at[2 * n + i], first=n)
            for n in range(seqs) for i, (src, dst) in enumerate(((teach_in, do_ref), (og_in, db_ref)))
        ]
        rows_out = Resplit(lay, low_ref, layer_out, rsend.at[2 * seqs], rrecv.at[2 * seqs], rown.at[2 * seqs], True)
        sums = [
            Scatter(
                lay, here, gw1_ref.at[i % kept], (0, depth, 0, columns), gw1_out.at[:, pl.ds(i * columns, columns)],
                held[4 * i : 4 * i + 4], send.at[i], recv.at[i], own.at[i], ways[i])
            for i in range(pieces)
        ]
        hooks = Hooks()
        for slot in range(pieces + 4 * lag):
            for i in range(pieces):
                stage, rest = divmod(slot - i, lag)
                if rest == 0 and 0 <= stage < 5:
                    hooks.put(slot, (sums[i], stage))
        last = max(hooks.slots)
        span_of = lambda row: (row // span, pl.ds(row % span, CHUNK))
        gain1, shift1 = vec_ref[0:1], vec_ref[1:2]
        bias2, gain2, shift2 = vec_ref[2:3], vec_ref[3:4], vec_ref[4:5]

        @pl.when(t == 0)
        def _():
            lay.greet(here)
            for split in rows_in[:2]:
                split.start()
            fetch = pltpu.make_async_copy(h1_ref, d1_ref, own.at[pieces])
            fetch.start()
            fetch.wait()
            sums_ref[...] = jnp.zeros_like(sums_ref)

            def norm(i, carry):
                at = pl.ds(pl.multiple_of(i * 128, 128), 128)
                seq = (i * 128) // span
                there = (seq, pl.ds(pl.multiple_of(i * 128 - seq * span, 128), 128))
                h = d1_ref[at]
                centred = h - jnp.mean(h, axis=-1, keepdims=True)
                inverse = lax.rsqrt(jnp.mean(centred * centred, axis=-1, keepdims=True) + 1e-12)
                normal = centred * inverse
                d1_ref[at] = normal
                inv1_ref[at] = inverse
                low = (normal * gain1 + shift1).astype(bf16)
                low_ref[there] = low
                lowt_ref[:, at] = low.T
                return carry

            lax.fori_loop(0, rows // 128, norm, 0)
            acc_ref[...] = jnp.zeros_like(acc_ref)

        for n in range(1, seqs):
            @pl.when(t == n * tiles // seqs)
            def _():
                for split in rows_in[2 * n : 2 * n + 2]:
                    split.start()

        @pl.when(t < tiles)
        def _():
            for i in range(rows // CHUNK):
                at = slice(i * CHUNK, (i + 1) * CHUNK)
                inner = dot(low_ref[span_of(i * CHUNK)], w1_ref[...]) + b1_ref[...]
                cum = 0.5 * (1.0 + lax.erf(inner * (1.0 / math.sqrt(2.0))))
                density = jnp.exp(-0.5 * inner * inner) * (1.0 / math.sqrt(2.0 * math.pi))
                active = (inner * cum).astype(bf16)
                act_ref[t, at] = active
                slope_ref[t, at] = (cum + inner * density).astype(bf16)
                acc_ref[at] += dot(active, w2_ref[...])

        @pl.when(t == tiles)
        def _():
            inv = vec_ref[5:6]

            def middle(i, carry):
                at = pl.ds(pl.multiple_of(i * 128, 128), 128)
                normed = d1_ref[at] * gain1 + shift1
                h2 = normed + acc_ref[at] + bias2
                centred = h2 - jnp.mean(h2, axis=-1, keepdims=True)
                inverse = lax.rsqrt(jnp.mean(centred * centred, axis=-1, keepdims=True) + 1e-12)
                normal = centred * inverse
                result = normal * gain2 + shift2
                seq = (i * 128) // span
                first = i * 128 - seq * span
                there = (seq, pl.ds(pl.multiple_of(first, 128), 128))
                low_ref[there] = result.astype(bf16)
                pos = first + lax.broadcasted_iota(jnp.int32, (128, 1), 0)
                valid = (pos < len_ref[base + seq]).astype(f32)
                deviation = (result - do_ref[there].astype(f32)) * valid
                grad = db_ref[there].astype(f32) * valid + (2.0 * inv) * deviation
                sums_ref[0:1] += jnp.sum(deviation * deviation, axis=0, keepdims=True)
                sums_ref[1:2] += jnp.sum(grad * normal, axis=0, keepdims=True)
                sums_ref[2:3] += jnp.sum(grad, axis=0, keepdims=True)
                scaled = grad * gain2
                mean = jnp.mean(scaled, axis=-1, keepdims=True)
                along = jnp.mean(scaled * normal, axis=-1, keepdims=True)
                d_two = inverse * (scaled - mean - normal * along)
                acc_ref[at] = d_two
                low = d_two.astype(bf16)
                sums_ref[3:4] += jnp.sum(low.astype(f32), axis=0, keepdims=True)
                do_ref[there] = low
                dot_ref[:, at] = low.T
                return carry

            for n in range(seqs):
                for split in rows_in[2 * n : 2 * n + 2]:
                    split.finish()
                lax.fori_loop(n * span // 128, (n + 1) * span // 128, middle, 0)
            rows_out.start()

        @pl.when((t > tiles) & (t <= 2 * tiles))
        def _():
            j = t - tiles - 1
            total = jnp.zeros((1, TILE), f32)
            for i in range(rows // CHUNK):
                at = slice(i * CHUNK, (i + 1) * CHUNK)
                d_act = dot_t(do_ref[span_of(i * CHUNK)], w2_ref[...])
                d_in = (d_act * slope_ref[j, at].astype(f32)).astype(bf16)
                total += jnp.sum(d_in.astype(f32), axis=0, keepdims=True)
                di_ref[at] = d_in
                acc_ref[at] += dot_t(d_in, w1_ref[...])
            gb1_ref[:, pl.ds(pl.multiple_of(j * TILE, TILE), TILE)] = total
            value = dot(lowt_ref[...], di_ref[...]).astype(bf16)
            gw1_ref[lax.rem(j, kept)] = value.reshape(lay.dims + (depth, TILE))
            hooks.at(j, range(tiles))

        @pl.when(t == 2 * tiles)
        def _():
            def back(i, carry):
                at = pl.ds(pl.multiple_of(i * 128, 128), 128)
                seq = (i * 128) // span
                there = (seq, pl.ds(pl.multiple_of(i * 128 - seq * span, 128), 128))
                grad, normal = acc_ref[at], d1_ref[at]
                sums_ref[4:5] += jnp.sum(grad * normal, axis=0, keepdims=True)
                sums_ref[5:6] += jnp.sum(grad, axis=0, keepdims=True)
                scaled = grad * gain1
                mean = jnp.mean(scaled, axis=-1, keepdims=True)
                along = jnp.mean(scaled * normal, axis=-1, keepdims=True)
                d_one = inv1_ref[at] * (scaled - mean - normal * along)
                d1_ref[at] = d_one
                db_ref[there] = d_one.astype(bf16)
                return carry

            lax.fori_loop(0, rows // 128, back, 0)

        @pl.when(t > 2 * tiles)
        def _():
            j = t - 2 * tiles - 1
            gw2 = dot(dot_ref[...], act_ref[j]).astype(bf16)
            if wide:
                for d in range(per_tile):
                    gw2_ref[d] = gw2[:, d * share : (d + 1) * share]
            else:
                gw2_ref[...] = gw2
            hooks.at(t - tiles - 1, range(tiles, 2 * tiles))

        @pl.when(t == 2 * tiles + 1)
        def _():
            small_ref[...] = jnp.zeros_like(small_ref)
            loss = jnp.broadcast_to(jnp.sum(sums_ref[0:1], axis=-1, keepdims=True), (1, 128))
            for d in range(devices):
                at = lay.place(d)
                small_ref[at + (slice(0, 5), slice(0, share1))] = sums_ref[1:6, d * share1 : (d + 1) * share1]
                small_ref[at + (slice(5, 6), slice(0, share))] = gb1_ref[:, d * share : (d + 1) * share]
                small_ref[at + (slice(6, 7),)] = loss

        @pl.when(t == 3 * tiles)
        def _():
            save = pltpu.make_async_copy(db_ref, db_out, own.at[pieces])
            save.start()
            for k in range(2 * tiles, last + 1):
                hooks.run(k)
            for part in sums:
                part.drain()
            rows_out.finish()
            save.wait()

    def tile(t, *_):
        return jnp.where(t < tiles, t, jnp.clip(t - tiles - 1, 0, tiles - 1))

    def outer_tile(t, *_):
        return jnp.maximum(t - 2 * tiles - 1, 0)

    full = once((rows, width))
    vec = pl.BlockSpec((1, TILE), lambda t, *_: (0, tile(t)))
    low = pltpu.VMEM((seqs, span, width), bf16)
    return pl.pallas_call(
        kernel,
        grid_spec=pltpu.PrefetchScalarGridSpec(
            num_scalar_prefetch=0,
            grid=(3 * tiles + 1,),
            in_specs=[
                pl.BlockSpec(memory_space=pltpu.SMEM), ANY, ANY, ANY, once((8, width)), vec,
                pl.BlockSpec((width, TILE), lambda t, *_: (0, tile(t))),
                pl.BlockSpec((TILE, width), lambda t, *_: (tile(t), 0)),
            ],
            out_specs=[
                ANY, full, ANY, once((depth, hidden)),
                pl.BlockSpec((per_tile, width, share), lambda t, *_: (outer_tile(t), 0, 0))
                if wide else pl.BlockSpec((width, TILE), lambda t, *_: (0, outer_tile(t))),
                once(lay.dims + (8, 128)),
            ],
            scratch_shapes=[
                low, pltpu.VMEM((width, rows), bf16),
                pltpu.VMEM((tiles, rows, TILE), bf16), pltpu.VMEM((tiles, rows, TILE), bf16),
                pltpu.VMEM((rows, width), f32), low, pltpu.VMEM((width, rows), bf16),
                pltpu.VMEM((rows, 1), f32), pltpu.VMEM((rows, TILE), bf16), low,
                pltpu.VMEM((kept,) + lay.dims + (depth, columns), bf16),
                pltpu.VMEM((8, width), f32), pltpu.VMEM((1, hidden), f32),
            ]
            + sems(lay, 0, 2 * seqs + 1)[3:]
            + sems(lay, pieces + 1, 0)[:3]
            + [b for way in ways for b in Scatter.buffers(lay, (0, depth, 0, columns), bf16, way)],
        ),
        out_shape=[
            jax.ShapeDtypeStruct(teacher.shape, bf16),
            jax.ShapeDtypeStruct((rows, width), f32),
            jax.ShapeDtypeStruct((seqs, span, width), bf16),
            jax.ShapeDtypeStruct((depth, hidden), f32),
            jax.ShapeDtypeStruct((devices, width, share) if wide else (width, hidden), bf16),
            jax.ShapeDtypeStruct(lay.dims + (8, 128), f32),
        ],
        compiler_params=pltpu.CompilerParams(
            collective_id=2, has_side_effects=True, vmem_limit_bytes=63 << 20),
        name="feed_forward",
    )(lengths, h1, teacher, out_grad, vecs, bias_inner, w1, w2)


def finish(d_tokens, small, vecs, share, deep, whole):
    seqs, span, width = d_tokens.shape
    n, steps = len(whole), 4

    def kernel(dx_ref, small_ref, vec_ref, *refs):
        ins, refs = refs[:n], refs[n:]
        dx_out, loss_ref, bias_ref = refs[:3]
        for i, vec in enumerate(refs[3:8]):
            vec[...] = small_ref[i : i + 1, :share]
        for a, b in zip(ins, refs[8:]):
            if a.ndim == 3:
                b[...] = a[...]
            else:
                pl.when(pl.program_id(0) == 0)(lambda a=a, b=b: b.__setitem__(Ellipsis, a[...]))
        loss_ref[...] = small_ref[6:7, :1] * vec_ref[5:6, :1]
        bias_ref[...] = small_ref[5:6, :deep]
        dx_out[...] = dx_ref[...].astype(f32)

    def block(a):
        if a.ndim == 3:
            return pl.BlockSpec((a.shape[0] // steps,) + a.shape[1:], lambda i: (i, 0, 0))
        return once(a.shape)

    like = lambda a, dtype: jax.ShapeDtypeStruct(a.shape, dtype)
    blocks = [block(a) for a in whole]
    out = pl.pallas_call(
        kernel,
        grid=(steps,),
        in_specs=[block(d_tokens), once((8, 128)), once((8, width))] + blocks,
        out_specs=[block(d_tokens), once((1, 1)), once((1, deep))] + [once((1, share))] * 5 + blocks,
        out_shape=[like(d_tokens, f32), jax.ShapeDtypeStruct((1, 1), f32), jax.ShapeDtypeStruct((1, deep), f32)]
        + [jax.ShapeDtypeStruct((1, share), f32)] * 5
        + [like(a, a.dtype) for a in whole],
        compiler_params=pltpu.CompilerParams(vmem_limit_bytes=63 << 20),
        name="finish",
    )(d_tokens, small, vecs, *whole)
    return out[0], out[1], out[2], out[3:8], out[8:]


def cut(shape, which, pieces, orders, columns=False):
    rows, wide = shape
    if columns:
        step = wide // pieces
        return [(which, (0, rows, i * step, step), orders) for i in range(pieces)]
    while pieces > 1 and rows % (pieces * 16):
        pieces -= 1
    step = rows // pieces
    return [(which, (i * step, step), orders) for i in range(pieces)]


def shards(
    lay, tokens, lengths, teacher, out_grad, w_query, w_key, w_value, w_output, gain_one, shift_one,
    w_inner, bias_inner, w_outer, bias_outer, gain_two, shift_two,
):
    width = tokens.shape[2]
    hidden = w_inner.shape[1]
    devices = lay.devices
    there = (("z", "x", "y"), ("z", "y", "x"))
    back = (("y", "x", "z"), ("x", "y", "z"))
    aside = (("x", "y", "z"),) * 2
    share, deep = gain_one.shape[0], bias_inner.shape[0]
    ins = [w_query, w_key, w_value, w_output, w_inner, w_outer]
    parts = [(6, (0, 8), there)]
    for i in range(4):
        parts += cut(ins[i].shape, i, 1, there)
    early = len(parts)
    parts += cut(w_inner.shape, 4, 8, there, True) + cut(w_outer.shape, 5, 8, there)
    vectors = [gain_one, shift_one, bias_outer, gain_two, shift_two, bias_inner]
    wq, wk, wv, wo, w1, w2, xt, q, k, v, att, lse, h1, vecs, bias1 = attention_forward(
        lay, tokens, lengths, vectors, ins, parts, early
    )
    wq, wk, wv, wo = (w.reshape(width, width) for w in (wq, wk, wv, wo))
    w1, w2 = w1.reshape(width, hidden), w2.reshape(hidden, width)
    layer_out, d_one, d_branch, g_inner, gw2, small = feed_forward(
        lay, h1, teacher, out_grad, lengths, vecs, bias1, w1, w2, back, aside
    )
    if gw2.ndim == 2:
        gw2 = gw2.T.reshape(devices, hidden // devices, width)
    g_query, g_key, g_value, g_output, g_outer, small, d_tokens = attention_backward(
        lay, xt, lengths, wq, wk, wv, wo, q, k, v, att, lse, d_branch, d_one, gw2, small, back, aside
    )
    d_tokens, loss, g_bias, vec_grads, copied = finish(
        d_tokens, small, vecs, share, deep, [layer_out, g_query, g_key, g_value, g_output, g_inner, g_outer]
    )
    layer_out, g_query, g_key, g_value, g_output, g_inner, g_outer = copied
    vec = lambda i: vec_grads[i][0]
    return (
        loss[0, 0],
        layer_out,
        d_tokens,
        g_query,
        g_key,
        g_value,
        g_output,
        vec(3),
        vec(4),
        g_inner,
        g_bias[0],
        g_outer,
        vec(2),
        vec(0),
        vec(1),
    )


def solution(mesh):
    lay = Layout(mesh)
    rows = P("dp", "blk", None)
    weight = P(("dp", "blk"), None)
    vector = P(("dp", "blk"))
    return jax.shard_map(
        lambda *args: shards(lay, *args),
        mesh=mesh,
        in_specs=(
            rows, P("dp"), rows, rows, weight, weight, weight, weight, vector, vector,
            weight, vector, weight, vector, vector, vector,
        ),
        out_specs=(
            P(), rows, rows, weight, weight, weight, weight, vector, vector,
            weight, vector, weight, vector, vector, vector,
        ),
        check_vma=False,
    )
```

```python
import math

import jax
import jax.numpy as jnp
from jax import lax
from jax.experimental import pallas as pl
from jax.experimental.pallas import tpu as pltpu
from jax.sharding import PartitionSpec as P

ANY = pl.BlockSpec(memory_space=pl.ANY)
MESH = pl.DeviceIdType.MESH
f32 = jnp.float32
bf16 = jnp.bfloat16


class Layout:
    def __init__(self, mesh):
        dp, blk = mesh.shape["dp"], mesh.shape["blk"]
        if dp == 8 and blk == 4:
            dims = [("z", "dp", 2, 4), ("x", "dp", 1, 2), ("y", "blk", 2, 2), ("c", "blk", 1, 2)]
        else:
            dims = [("z", "dp", dp // 4, 4), ("x", "dp", 2, dp // 8), ("c", "dp", 1, 2), ("y", "blk", 1, blk)]
        self.order = [d[0] for d in dims]
        self.axis = {d[0]: d[1] for d in dims}
        self.stride = {d[0]: d[2] for d in dims}
        self.size = {d[0]: d[3] for d in dims}
        self.dims = tuple(d[3] for d in dims)
        self.blk = blk
        self.devices = dp * blk
        self.slot = {}
        count = 0
        for name in self.order:
            self.slot[name] = count
            count += self.size[name] - 1
        self.slots = count

    def here(self):
        return {
            name: lax.rem(lax.axis_index(self.axis[name]) // self.stride[name], self.size[name])
            for name in self.order
        }

    def step_to(self, here, name, distance):
        there = lax.rem(here[name] + distance, self.size[name])
        index = lax.axis_index(self.axis[name]) + (there - here[name]) * self.stride[name]
        return there, {self.axis[name]: index}

    def at(self, here, whole, changed=(), names=None):
        changed = dict(changed)
        return tuple(
            slice(None) if name in whole else changed.get(name, here[name])
            for name in (names or self.order)
        )

    def place(self, device):
        index = []
        for size in reversed(self.dims):
            index.append(lax.rem(device, size))
            device = device // size
        return tuple(reversed(index))

    def greet(self, here):
        barrier = pltpu.get_barrier_semaphore()
        count = 0
        for name in self.order:
            if self.axis[name] == "blk":
                continue
            for distance in range(1, self.size[name]):
                _, device = self.step_to(here, name, distance)
                pl.semaphore_signal(barrier, inc=1, device_id=device, device_id_type=MESH)
                count += 1
        me = lax.axis_index("blk")
        for distance in range(1, self.blk):
            pl.semaphore_signal(
                barrier, inc=1, device_id={"blk": lax.rem(me + distance, self.blk)}, device_id_type=MESH
            )
            count += 1
        pl.semaphore_wait(barrier, count)


def window(cut):
    if len(cut) == 2:
        return (pl.ds(*cut),)
    return (pl.ds(cut[0], cut[1]), pl.ds(cut[2], cut[3]))


def by_core(here, orders, make):
    if orders[0] == orders[1]:
        make(orders[0])
        return
    for core in range(2):
        @pl.when(here["c"] == core)
        def _():
            make(orders[core])


class Gather:
    stages = 5

    def __init__(self, lay, here, src, full, rows, send, recv, own, orders):
        self.lay, self.here = lay, here
        self.rows = window(rows)
        self.src, self.full = src.at[self.rows], full
        self.send, self.recv, self.own = send, recv, own
        self.orders = orders

    def line(self, name, whole):
        copies = []
        place = self.full.at[self.lay.at(self.here, whole) + self.rows]
        source = self.src if not whole else place
        for distance in range(1, self.lay.size[name]):
            _, device = self.lay.step_to(self.here, name, distance)
            slot = self.lay.slot[name] + distance - 1
            copies.append(
                pltpu.make_async_remote_copy(
                    src_ref=source, dst_ref=place, send_sem=self.send.at[slot], recv_sem=self.recv.at[slot],
                    device_id=device, device_id_type=MESH,
                )
            )
        return copies

    def local(self):
        return pltpu.make_async_copy(self.src, self.full.at[self.lay.at(self.here, ()) + self.rows], self.own)

    def stage(self, k):
        if k == 1:
            self.local().wait()

        def make(order):
            lines = tuple(order) + ("c",)
            if k > 0:
                for c in self.line(lines[k - 1], lines[: k - 1]):
                    c.wait_recv()
            if k < 4:
                for c in self.line(lines[k], lines[:k]):
                    c.start()

        if k == 0:
            self.local().start()
        by_core(self.here, self.orders, make)

    def drain(self):
        def make(order):
            lines = tuple(order) + ("c",)
            for k in range(4):
                for c in self.line(lines[k], lines[:k]):
                    c.wait_send()
        by_core(self.here, self.orders, make)


class Resplit:
    def __init__(self, lay, src, dst, send, recv, own, back=False, first=0):
        self.lay, self.src, self.dst = lay, src, dst
        self.first = first
        self.send, self.recv, self.own = send, recv, own
        self.me = lax.axis_index("blk")
        self.back = back
        self.seqs = (src if back else dst).shape[0]
        self.total = (dst if back else src).shape[0] // lay.blk
        self.span = (dst if back else src).shape[1]

    def ends(self, there):
        if self.back:
            return (self.src.at[:, pl.ds(there * self.span, self.span)],
                    self.dst.at[pl.ds(self.me * self.total + self.first, self.seqs)])
        return (self.src.at[pl.ds(there * self.total + self.first, self.seqs)],
                self.dst.at[:, pl.ds(self.me * self.span, self.span)])

    def copies(self):
        out = []
        for distance in range(1, self.lay.blk):
            there = lax.rem(self.me + distance, self.lay.blk)
            src, dst = self.ends(there)
            out.append(
                pltpu.make_async_remote_copy(
                    src_ref=src, dst_ref=dst,
                    send_sem=self.send.at[distance - 1], recv_sem=self.recv.at[distance - 1],
                    device_id={"blk": there}, device_id_type=MESH,
                )
            )
        return out

    def local(self):
        src, dst = self.ends(self.me)
        return pltpu.make_async_copy(src, dst, self.own)

    def start(self):
        self.local().start()
        for c in self.copies():
            c.start()

    def finish(self):
        self.local().wait()
        for c in self.copies():
            c.wait()


class Scatter:
    stages = 5

    def __init__(self, lay, here, grad, cut, out, bufs, send, recv, own, orders, staged=None, turn=False):
        self.turn = turn
        self.lay, self.here, self.grad, self.cut = lay, here, grad, window(cut)
        self.out, self.held, self.recvs, self.staged = out, bufs[0], bufs[1:], staged
        self.send, self.recv, self.own = send, recv, own
        self.orders = orders
        self.names = [n for n in lay.order if n != "c"]

    @staticmethod
    def buffers(lay, cut, dtype, orders):
        shape = (cut[1], cut[3])
        names = [n for n in lay.order if n != "c"]
        out = [pltpu.VMEM(tuple(lay.size[n] for n in names) + shape, dtype)]
        for k in range(3):
            lines = orders[0][k + 1 :]
            left = tuple(lay.size[n] for n in names if n in lines)
            out.append(pltpu.VMEM((lay.size[orders[0][k]] - 1,) + left + shape, dtype))
        return out

    def local(self):
        return pltpu.make_async_copy(
            self.grad.at[self.lay.at(self.here, self.names) + self.cut], self.staged, self.own)

    def core(self):
        there, device = self.lay.step_to(self.here, "c", 1)
        slot = self.lay.slot["c"]
        return pltpu.make_async_remote_copy(
            src_ref=self.grad.at[self.lay.at(self.here, self.names, {"c": there}) + self.cut], dst_ref=self.held,
            send_sem=self.send.at[slot], recv_sem=self.recv.at[slot], device_id=device, device_id_type=MESH)

    def line(self, order, k):
        name, left = order[k], order[k + 1 :]
        copies = []
        for distance in range(1, self.lay.size[name]):
            there, device = self.lay.step_to(self.here, name, distance)
            slot = self.lay.slot[name] + distance - 1
            copies.append(
                pltpu.make_async_remote_copy(
                    src_ref=self.held.at[self.lay.at(self.here, left, {name: there}, self.names)],
                    dst_ref=self.recvs[k].at[distance - 1],
                    send_sem=self.send.at[slot], recv_sem=self.recv.at[slot],
                    device_id=device, device_id_type=MESH,
                )
            )
        return copies

    def add(self, order, k):
        left = [n for n in self.names if k < 0 or n in order[k + 1 :]]
        steps = self.lay.size[left[0]] if left else 1

        def one(i, carry):
            index = {n: slice(None) for n in left}
            if left:
                index[left[0]] = i
            mine = tuple(index.get(n, self.here[n]) for n in self.names)
            alone = k < 0 or (k < 2 and self.lay.size[order[k]] == 2)
            wide = self.held.dtype if alone else f32
            value = self.held[mine].astype(wide)
            if k >= 0:
                theirs = tuple(index[n] for n in left)
                for d in range(self.lay.size[order[k]] - 1):
                    value = value + self.recvs[k][(d,) + theirs].astype(wide)
            elif self.staged is not None:
                value = value + self.staged[mine].astype(wide)
            else:
                value = value + self.grad[self.lay.at({**self.here, **index}, ()) + self.cut].astype(wide)
            if k == 2:
                self.out[...] = value.T if self.turn else value
            else:
                self.held[mine] = value.astype(self.held.dtype)
            return carry

        lax.fori_loop(0, steps, one, 0)

    def stage(self, k):
        if k == 0:
            self.core().start()
            if self.staged is not None:
                self.local().start()
            return
        if k == 1:
            if self.staged is not None:
                self.local().wait()
            self.core().wait()
            self.add(None, -1)

        def make(order):
            if k > 1:
                for c in self.line(order, k - 2):
                    c.wait_recv()
                self.add(order, k - 2)
            if k < 4:
                for c in self.line(order, k - 1):
                    c.start()

        by_core(self.here, self.orders, make)

    def drain(self):
        def make(order):
            for k in range(3):
                for c in self.line(order, k):
                    c.wait_send()

        by_core(self.here, self.orders, make)


def skewed(parts, lag=1, stages=5):
    events = []
    for t in range(len(parts) + lag * (stages - 1)):
        for i, part in enumerate(parts):
            stage, rest = divmod(t - i, lag)
            if rest == 0 and 0 <= stage < stages:
                events.append((part, stage))
    return events


class Hooks:
    def __init__(self):
        self.slots = {}

    def put(self, slot, event):
        self.slots.setdefault(slot, []).append(event)

    def spread(self, events, first, last):
        for n, event in enumerate(events):
            self.put(first + n * (last - first) // len(events), event)

    def run(self, slot):
        for part, stage in self.slots.get(slot, ()):
            part.stage(stage)

    def at(self, step, slots):
        for k in slots:
            if k in self.slots:
                pl.when(step == k)(lambda k=k: self.run(k))


def sems(lay, n, m):
    dma = pltpu.SemaphoreType.DMA
    n, m = max(n, 1), max(m, 1)
    return [dma((n, lay.slots)), dma((n, lay.slots)), dma((n,)), dma((m, lay.blk - 1)), dma((m, lay.blk - 1)), dma((m,))]


DH = 64
LOG2E = math.log2(math.e)
GROUP = 256


def dot(a, b):
    return lax.dot_general(a, b, (((1,), (0,)), ((), ())), preferred_element_type=f32)


def dot_t(a, b):
    return lax.dot_general(a, b, (((1,), (1,)), ((), ())), preferred_element_type=f32)


def once(shape):
    return pl.BlockSpec(shape, lambda *_: (0,) * len(shape), pipeline_mode=pl.Buffered(1))


def attention_forward(lay, tokens, lengths, vectors, shards, parts, early):
    width = tokens.shape[2]
    seqs, span = tokens.shape[0] // lay.blk, tokens.shape[1] * lay.blk
    rows = seqs * span
    groups = width // GROUP
    scale = LOG2E / math.sqrt(DH)
    heads = seqs * GROUP // DH
    pairs = seqs * GROUP // 128
    n, p, m = len(shards), len(parts), len(vectors)
    share, deep = vectors[0].shape[0], vectors[-1].shape[0]
    slots = pairs + 3

    def kernel(len_ref, *refs):
        vecs, refs = refs[:m], refs[m:]
        tok_ref, refs = refs[0], refs[1:]
        ins, refs = refs[:n], refs[n:]
        fulls, refs = refs[:n], refs[n:]
        xt_out, q_out, k_out, v_out, att_out, lse_ref, h1_out, vec_out, bias_out = refs[:9]
        x_ref, wq_ref, wk_ref, wv_ref, wo_ref, q_ref, k_ref, v_ref, att_ref, h1_ref, pack_ref, packs_ref, low_ref, xt_ref = refs[9:23]
        load, send, recv, own, rsend, rrecv, rown = refs[23:]
        ins, fulls = list(ins) + [pack_ref], list(fulls) + [packs_ref]
        here = lay.here()
        pack_ref[...] = jnp.zeros_like(pack_ref)
        for i, vec in enumerate(vecs):
            pack_ref[i : i + 1, : vec.shape[0]] = vec[...].astype(f32).reshape(1, vec.shape[0])
        tokens_here = len_ref[0]
        for i in range(1, lengths.shape[0]):
            tokens_here = tokens_here + len_ref[i]
        pack_ref[m : m + 1] = jnp.full((1, 128), tokens_here.astype(f32))
        lay.greet(here)
        split = Resplit(lay, tok_ref, x_ref, rsend, rrecv, rown)
        split.start()
        gathers = [
            Gather(lay, here, ins[a], fulls[a], cut, send.at[i], recv.at[i], own.at[i], orders)
            for i, (a, cut, orders) in enumerate(parts)
        ]
        events = skewed(gathers, 3)
        last = max(i for i, (part, stage) in enumerate(events) if part in gathers[:early] and stage == 4)
        for part, stage in events[: last + 1]:
            part.stage(stage)
        split.finish()
        loads = [
            pltpu.make_async_copy(src, dst, load.at[i])
            for i, (src, dst) in enumerate(
                zip(fulls[:4], [wq_ref, wk_ref, wv_ref, wo_ref]))
        ]
        for c in loads:
            c.start()
        for c in loads:
            c.wait()
        hooks = Hooks()
        hooks.spread(events[last + 1 :], 0, groups * slots * 6 // 5)
        base = lax.axis_index("blk") * seqs

        def columns(ref, g):
            block = ref[(slice(None),) * 5 + (pl.ds(pl.multiple_of(g * GROUP, GROUP), GROUP),)]
            return block.reshape(width, GROUP)

        def features(ref, g):
            per = GROUP // ref.shape[-2]
            return jnp.concatenate([ref[lay.place(g * per + j)] for j in range(per)], axis=0)

        def step(i, carry):
            g, r = i // pairs, lax.rem(i, pairs)
            cols = pl.ds(pl.multiple_of(g * GROUP, GROUP), GROUP)

            @pl.when(r == 0)
            def _():
                xv = x_ref[...].reshape(rows, width)
                for j, (low, weight) in enumerate(((q_ref, wq_ref), (k_ref, wk_ref), (v_ref, wv_ref))):
                    low[:, cols] = dot(xv, columns(weight, g)).astype(bf16)
                    hooks.at(g * slots + j, range(j, groups * slots, slots))

            @pl.when(i == groups * pairs // 4)
            def _():
                for n in range(seqs):
                    xt_ref[:, n * span : (n + 1) * span] = x_ref[n].T

            @pl.when(i == groups * pairs // 2)
            def _():
                total = jnp.zeros((1, 128), f32)
                for d in range(lay.devices):
                    tile = packs_ref[lay.place(d)]
                    vec_out[0 : m - 1, d * share : (d + 1) * share] = tile[0 : m - 1, :share]
                    bias_out[:, d * deep : (d + 1) * deep] = tile[m - 1 : m, :deep]
                    total = total + tile[m : m + 1]
                inverse = 1.0 / (total / lay.blk * width)
                for d in range(width // 128):
                    vec_out[m - 1 : m, d * 128 : (d + 1) * 128] = inverse

            s, pair = r // (GROUP // 128), lax.rem(r, GROUP // 128)
            at = (pl.ds(pl.multiple_of(s * span, span), span),
                  pl.ds(pl.multiple_of(g * GROUP + pair * 128, 128), 128))
            qs, ks, vs = q_ref[at], k_ref[at], v_ref[at]
            lane = lax.broadcasted_iota(jnp.int32, (span, 128), 1)
            keep = lax.broadcasted_iota(jnp.int32, (span, 1), 0) < len_ref[base + s]
            vt = vs.T
            outs = []
            for h in range(2):
                km = jnp.where((lane < DH) if h == 0 else (lane >= DH), ks, jnp.zeros_like(ks))
                st = dot_t(km, qs) * scale
                st = jnp.where(keep, st, -1e30)
                top = jnp.max(st, axis=0, keepdims=True)
                e = jnp.exp2(st - top)
                den = jnp.sum(e, axis=0, keepdims=True)
                ot = dot(vt[h * DH : (h + 1) * DH], e.astype(bf16))
                outs.append(ot * (1.0 / den))
                lse_ref[g, pl.ds(r * 2 + h, 1)] = top + jnp.log2(den)
            turned = jnp.concatenate(outs, axis=0)
            att_ref[at[1], at[0]] = turned.astype(bf16)
            low_ref[at[0], pl.ds(pl.multiple_of(pair * 128, 128), 128)] = turned.T.astype(bf16)

            @pl.when(r == pairs - 1)
            def _():
                add = dot(low_ref[...], features(wo_ref, g))

                @pl.when(g == 0)
                def _():
                    h1_ref[...] = x_ref[...].reshape(rows, width).astype(f32) + add

                @pl.when(g > 0)
                def _():
                    h1_ref[...] += add

            hooks.at(g * slots + 3 + r, [k for k in range(groups * slots) if k % slots >= 3])
            return carry

        lax.fori_loop(0, groups * pairs, step, 0)
        saves = [
            pltpu.make_async_copy(src, dst, load.at[i])
            for i, (src, dst) in enumerate(
                zip([xt_ref, q_ref, k_ref, v_ref, att_ref, h1_ref], [xt_out, q_out, k_out, v_out, att_out, h1_out]))
        ]
        for c in saves:
            c.start()
        for k in sorted(hooks.slots):
            if k >= groups * slots:
                hooks.run(k)
        for g in gathers:
            g.drain()
        for c in saves:
            c.wait()

    whole = [jax.ShapeDtypeStruct(lay.dims + s.shape, s.dtype) for s in shards]
    vmem = pl.BlockSpec(memory_space=pltpu.VMEM)
    act, turned = jax.ShapeDtypeStruct((rows, width), bf16), jax.ShapeDtypeStruct((width, rows), bf16)
    return pl.pallas_call(
        kernel,
        in_specs=[pl.BlockSpec(memory_space=pltpu.SMEM)] + [vmem] * m + [ANY] + [vmem] * n,
        out_specs=[ANY] * (n + 5) + [vmem, ANY, vmem, vmem],
        out_shape=whole
        + [turned, act, act, act, turned,
           jax.ShapeDtypeStruct((groups, heads, span), f32), jax.ShapeDtypeStruct((rows, width), f32),
           jax.ShapeDtypeStruct((8, width), f32), jax.ShapeDtypeStruct((1, deep * lay.devices), f32)],
        scratch_shapes=[pltpu.VMEM((seqs, span, width), bf16)]
        + [pltpu.VMEM(lay.dims + s.shape, bf16) for s in shards[:4]]
        + [pltpu.VMEM((rows, width), bf16)] * 3 + [pltpu.VMEM((width, rows), bf16)]
        + [pltpu.VMEM((rows, width), f32), pltpu.VMEM((8, 128), f32), pltpu.VMEM(lay.dims + (8, 128), f32),
           pltpu.VMEM((rows, GROUP), bf16), pltpu.VMEM((width, rows), bf16),
           pltpu.SemaphoreType.DMA((6,))]
        + sems(lay, p, 0)[:3]
        + [pltpu.SemaphoreType.DMA((lay.blk - 1,)), pltpu.SemaphoreType.DMA((lay.blk - 1,)),
           pltpu.SemaphoreType.DMA],
        compiler_params=pltpu.CompilerParams(collective_id=1, has_side_effects=True, vmem_limit_bytes=60 << 20),
        name="attention_forward",
    )(lengths, *vectors, tokens, *shards)


def attention_backward(lay, xt, lengths, wq, wk, wv, wo, q, k, v, att, lse, d_branch, d_one, outer, small, orders, aside):
    seqs, span, width = d_branch.shape
    rows = seqs * span
    heads = lse.shape[1]
    groups = width // GROUP
    pairs = seqs * GROUP // 128
    steps = pairs + 1
    depth = width // lay.devices
    scale = LOG2E / math.sqrt(DH)
    deep, share = outer.shape[1:]
    pieces, lag = 8, 3
    while deep % (pieces * 16):
        pieces //= 2
    outer_cuts = [(i * deep // pieces, deep // pieces, 0, share) for i in range(pieces)]
    small_cut = (0, 8, 0, 128)
    wo_cuts = [(0, depth, i * width // 2, width // 2) for i in range(2)]
    late_cuts = [((0, depth, c * GROUP, GROUP), c) for c in range(groups)]
    bufs = [Scatter.buffers(lay, c, bf16, orders) for c in outer_cuts + wo_cuts]
    bufs += [Scatter.buffers(lay, small_cut, f32, orders)]
    bufs += [Scatter.buffers(lay, c, bf16, aside) for c, _ in late_cuts for _ in range(3)]
    count = len(bufs)
    wide = deep == width
    outer = outer.reshape(lay.dims + outer.shape[1:])

    def kernel(
        len_ref, xt_ref, wq_ref, wk_ref, wv_ref, wo_ref, q_ref, k_ref, v_ref, att_ref, lse_ref, db_ref, d1_in, outer_in, small_in,
        gq_out, gk_out, gv_out, go_out, outer_out, small_out, dx_out,
        gq_ref, gk_ref, gv_ref, go_ref, do_ref, dq_ref, dk_ref, dv_ref, acc_ref, dx_ref,
        stage_small, stage_ref, send, recv, own, rsend, rrecv, rown, fetch_sem, *held,
    ):
        g = pl.program_id(0)
        here = lay.here()
        base = lax.axis_index("blk") * seqs
        made = []

        def part(grad, cut, out, way, staged=None, turn=False):
            i = len(made)
            made.append(Scatter(
                lay, here, grad, cut, out, held[4 * i : 4 * i + 4], send.at[i], recv.at[i], own.at[i], way, staged, turn))
            return made[-1]

        first = [
            part(outer_in, c, outer_out.at[:, pl.ds(c[0], c[1])] if wide else outer_out.at[pl.ds(c[0], c[1])], orders,
                 stage_ref.at[i % (lag + 1)], wide)
            for i, c in enumerate(outer_cuts)
        ]
        first += [part(go_ref, c, go_out.at[:, pl.ds(c[2], c[3])], orders) for c in wo_cuts]
        first += [part(small_in, small_cut, small_out, orders, stage_small)]
        hooks = Hooks()
        events = skewed(first, lag)
        hooks.spread(events[lag:], 0, groups * steps - 1)
        finals = []
        for c, group in late_cuts:
            parts = [
                part(ref, c, out.at[:, pl.ds(c[2], c[3])], aside)
                for ref, out in ((gq_ref, gq_out), (gk_ref, gk_out), (gv_ref, gv_out))
            ]
            ready = (group + 1) * steps - 1
            for stage in range(5):
                for i, p in enumerate(parts):
                    hooks.put(ready + i + 3 * stage, (p, stage))
        for k in sorted(hooks.slots):
            if k >= groups * steps - 1:
                finals += hooks.slots.pop(k)
        splits = [
            Resplit(lay, dx_ref.at[pl.ds(s, 1)], dx_out, rsend.at[s], rrecv.at[s], rown.at[s], True, s) for s in range(seqs)
        ]

        @pl.when(g == 0)
        def _():
            lay.greet(here)
            for p, stage in events[:lag]:
                p.stage(stage)
            fetch = pltpu.make_async_copy(d1_in, acc_ref, fetch_sem)
            fetch.start()

            def output_rows(j, carry):
                value = dot(att_ref[pl.ds(pl.multiple_of(j * GROUP, GROUP), GROUP)], db_ref[...].reshape(rows, width)).astype(bf16)
                for d in range(GROUP // depth):
                    go_ref[lay.place(j * (GROUP // depth) + d)] = value[d * depth : (d + 1) * depth]
                return carry

            lax.fori_loop(0, groups, output_rows, 0)
            fetch.wait()

        do_ref[...] = dot_t(db_ref[...].reshape(rows, width), wo_ref[...]).astype(bf16)

        def pair_step(i, carry):
            s, pair = i // (GROUP // 128), lax.rem(i, GROUP // 128)
            at = (pl.ds(pl.multiple_of(s * span, span), span), pl.ds(pl.multiple_of(pair * 128, 128), 128))
            length = len_ref[base + s]
            qs, ks, vs, dos = q_ref[at], k_ref[at], v_ref[at], do_ref[at]
            lane = lax.broadcasted_iota(jnp.int32, (span, 128), 1)
            keep = lax.broadcasted_iota(jnp.int32, (span, 1), 0) < length
            kt = ks.T
            dqs, dks, dvs = [], [], []
            for h in range(2):
                mine = (lane < DH) if h == 0 else (lane >= DH)
                zero = jnp.zeros_like(ks)
                st = dot_t(jnp.where(mine, ks, zero), qs) * scale
                p = jnp.where(keep, jnp.exp2(st - lse_ref[0, pl.ds(i * 2 + h, 1)]), 0.0)
                dp = dot_t(jnp.where(mine, vs, zero), dos)
                delta = jnp.sum(p * dp, axis=0, keepdims=True)
                ds = (p * (dp - delta)).astype(bf16)
                dvs.append(dot(p.astype(bf16), dos))
                dks.append(dot(ds, qs))
                dqs.append(dot(kt[h * DH : (h + 1) * DH], ds))
            low_half = lane < DH
            unit = 1.0 / math.sqrt(DH)
            dv_ref[at] = jnp.where(low_half, dvs[0], dvs[1]).astype(bf16)
            dk_ref[at] = (jnp.where(low_half, dks[0], dks[1]) * unit).astype(bf16)
            dq_ref[at] = (jnp.concatenate(dqs, axis=0).T * unit).astype(bf16)

            @pl.when(pair == GROUP // 128 - 1)
            def _():
                mine = at[0]
                acc_ref[mine] += (
                    dot_t(dq_ref[mine], wq_ref[...]) + dot_t(dk_ref[mine], wk_ref[...]) + dot_t(dv_ref[mine], wv_ref[...])
                )

            for n in range(seqs):
                @pl.when((g == groups - 1) & (i == (n + 1) * (GROUP // 128) - 1))
                def _():
                    dx_ref[n] = acc_ref[n * span : (n + 1) * span].astype(bf16)
                    splits[n].start()

            hooks.at(g * steps + i, [k for k in range(groups * steps) if k % steps < pairs])
            return carry

        lax.fori_loop(0, pairs, pair_step, 0)
        xt = xt_ref[...]
        cols = (slice(None),) * 5 + (pl.ds(pl.multiple_of(g * GROUP, GROUP), GROUP),)
        for grad, low in ((gq_ref, dq_ref), (gk_ref, dk_ref), (gv_ref, dv_ref)):
            grad[cols] = dot(xt, low[...]).astype(bf16).reshape(lay.dims + (depth, GROUP))
        hooks.at(g * steps + pairs, [k for k in range(groups * steps) if k % steps == pairs])

        @pl.when(g == groups - 1)
        def _():
            for p, stage in finals:
                p.stage(stage)
            for p in made:
                p.drain()
            for split in splits:
                split.finish()

    col = pl.BlockSpec((width, GROUP), lambda g, *_: (0, g))
    row = pl.BlockSpec((GROUP, width), lambda g, *_: (g, 0))
    act = pl.BlockSpec((rows, GROUP), lambda g, *_: (0, g))
    vmem = pl.BlockSpec(memory_space=pltpu.VMEM)
    grad = pltpu.VMEM(lay.dims + (depth, width), bf16)
    no_core = tuple(lay.size[n] for n in lay.order if n != "c")
    shard = jax.ShapeDtypeStruct((depth, width), f32)
    return pl.pallas_call(
        kernel,
        grid_spec=pltpu.PrefetchScalarGridSpec(
            num_scalar_prefetch=0,
            grid=(groups,),
            in_specs=[pl.BlockSpec(memory_space=pltpu.SMEM), once((width, rows)), col, col, col, row, act, act, act, once((width, rows)),
                      pl.BlockSpec((1, heads, span), lambda g, *_: (g, 0, 0)), once((seqs, span, width)), ANY, ANY, ANY],
            out_specs=[once((depth, width))] * 4 + [once((share, deep) if wide else (deep, share)), once((8, 128)), ANY],
            scratch_shapes=[grad] * 4
            + [pltpu.VMEM((rows, GROUP), bf16)] * 4
            + [pltpu.VMEM((rows, width), f32), pltpu.VMEM((seqs, span, width), bf16)]
            + [pltpu.VMEM(no_core + (8, 128), f32)] + [pltpu.VMEM((lag + 1,) + no_core + (deep // pieces, share), bf16)]
            + sems(lay, count, 0)[:3]
            + sems(lay, 0, seqs)[3:] + [pltpu.SemaphoreType.DMA]
            + [b for bs in bufs for b in bs],
        ),
        out_shape=[shard] * 4
        + [jax.ShapeDtypeStruct((share, deep) if wide else (deep, share), f32), jax.ShapeDtypeStruct((8, 128), f32),
           jax.ShapeDtypeStruct((seqs * lay.blk, span // lay.blk, width), bf16)],
        compiler_params=pltpu.CompilerParams(
            collective_id=3, has_side_effects=True, vmem_limit_bytes=63 << 20),
        name="attention_backward",
    )(lengths, xt, wq, wk, wv, wo, q, k, v, att, lse, d_branch, d_one, outer, small)


TILE = 512
CHUNK = 512


def feed_forward(lay, h1, teacher, out_grad, lengths, vecs, bias_inner, w1, w2, orders, aside):
    rows, width = h1.shape
    hidden = w1.shape[1]
    seqs = teacher.shape[0] // lay.blk
    span = rows // seqs
    devices = lay.devices
    tiles = hidden // TILE
    share, share1 = hidden // devices, width // devices
    per_tile = TILE // share
    wide = share % 128 == 0
    pieces, depth, lag, kept = tiles, width // devices, 2, 4
    columns = hidden // pieces
    ways = [aside if i % 3 < 2 else orders for i in range(pieces)]

    def kernel(
        len_ref, h1_ref, teach_in, og_in, vec_ref, b1_ref, w1_ref, w2_ref,
        layer_out, d1_ref, db_out, gw1_out, gw2_ref, small_ref,
        low_ref, lowt_ref, act_ref, slope_ref, acc_ref, do_ref, dot_ref, inv1_ref, di_ref, db_ref, gw1_ref, sums_ref, gb1_ref,
        rsend, rrecv, rown, send, recv, own, *held,
    ):
        t = pl.program_id(0)
        here = lay.here()
        base = lax.axis_index("blk") * seqs
        rows_in = [
            Resplit(lay, src, dst.at[pl.ds(n, 1)], rsend.at[2 * n + i], rrecv.at[2 * n + i], rown.at[2 * n + i], first=n)
            for n in range(seqs) for i, (src, dst) in enumerate(((teach_in, do_ref), (og_in, db_ref)))
        ]
        rows_out = Resplit(lay, low_ref, layer_out, rsend.at[2 * seqs], rrecv.at[2 * seqs], rown.at[2 * seqs], True)
        sums = [
            Scatter(
                lay, here, gw1_ref.at[i % kept], (0, depth, 0, columns), gw1_out.at[:, pl.ds(i * columns, columns)],
                held[4 * i : 4 * i + 4], send.at[i], recv.at[i], own.at[i], ways[i])
            for i in range(pieces)
        ]
        hooks = Hooks()
        for slot in range(pieces + 4 * lag):
            for i in range(pieces):
                stage, rest = divmod(slot - i, lag)
                if rest == 0 and 0 <= stage < 5:
                    hooks.put(slot, (sums[i], stage))
        last = max(hooks.slots)
        span_of = lambda row: (row // span, pl.ds(row % span, CHUNK))
        gain1, shift1 = vec_ref[0:1], vec_ref[1:2]
        bias2, gain2, shift2 = vec_ref[2:3], vec_ref[3:4], vec_ref[4:5]

        @pl.when(t == 0)
        def _():
            lay.greet(here)
            for split in rows_in[:2]:
                split.start()
            fetch = pltpu.make_async_copy(h1_ref, d1_ref, own.at[pieces])
            fetch.start()
            fetch.wait()
            sums_ref[...] = jnp.zeros_like(sums_ref)

            def norm(i, carry):
                at = pl.ds(pl.multiple_of(i * 128, 128), 128)
                seq = (i * 128) // span
                there = (seq, pl.ds(pl.multiple_of(i * 128 - seq * span, 128), 128))
                h = d1_ref[at]
                centred = h - jnp.mean(h, axis=-1, keepdims=True)
                inverse = lax.rsqrt(jnp.mean(centred * centred, axis=-1, keepdims=True) + 1e-12)
                normal = centred * inverse
                d1_ref[at] = normal
                inv1_ref[at] = inverse
                low = (normal * gain1 + shift1).astype(bf16)
                low_ref[there] = low
                lowt_ref[:, at] = low.T
                return carry

            lax.fori_loop(0, rows // 128, norm, 0)
            acc_ref[...] = jnp.zeros_like(acc_ref)

        for n in range(1, seqs):
            @pl.when(t == n * tiles // seqs)
            def _():
                for split in rows_in[2 * n : 2 * n + 2]:
                    split.start()

        @pl.when(t < tiles)
        def _():
            for i in range(rows // CHUNK):
                at = slice(i * CHUNK, (i + 1) * CHUNK)
                inner = dot(low_ref[span_of(i * CHUNK)], w1_ref[...]) + b1_ref[...]
                cum = 0.5 * (1.0 + lax.erf(inner * (1.0 / math.sqrt(2.0))))
                density = jnp.exp(-0.5 * inner * inner) * (1.0 / math.sqrt(2.0 * math.pi))
                active = (inner * cum).astype(bf16)
                act_ref[t, at] = active
                slope_ref[t, at] = (cum + inner * density).astype(bf16)
                acc_ref[at] += dot(active, w2_ref[...])

        @pl.when(t == tiles)
        def _():
            inv = vec_ref[5:6]

            def middle(i, carry):
                at = pl.ds(pl.multiple_of(i * 128, 128), 128)
                normed = d1_ref[at] * gain1 + shift1
                h2 = normed + acc_ref[at] + bias2
                centred = h2 - jnp.mean(h2, axis=-1, keepdims=True)
                inverse = lax.rsqrt(jnp.mean(centred * centred, axis=-1, keepdims=True) + 1e-12)
                normal = centred * inverse
                result = normal * gain2 + shift2
                seq = (i * 128) // span
                first = i * 128 - seq * span
                there = (seq, pl.ds(pl.multiple_of(first, 128), 128))
                low_ref[there] = result.astype(bf16)
                pos = first + lax.broadcasted_iota(jnp.int32, (128, 1), 0)
                valid = (pos < len_ref[base + seq]).astype(f32)
                deviation = (result - do_ref[there].astype(f32)) * valid
                grad = db_ref[there].astype(f32) * valid + (2.0 * inv) * deviation
                sums_ref[0:1] += jnp.sum(deviation * deviation, axis=0, keepdims=True)
                sums_ref[1:2] += jnp.sum(grad * normal, axis=0, keepdims=True)
                sums_ref[2:3] += jnp.sum(grad, axis=0, keepdims=True)
                scaled = grad * gain2
                mean = jnp.mean(scaled, axis=-1, keepdims=True)
                along = jnp.mean(scaled * normal, axis=-1, keepdims=True)
                d_two = inverse * (scaled - mean - normal * along)
                acc_ref[at] = d_two
                low = d_two.astype(bf16)
                sums_ref[3:4] += jnp.sum(low.astype(f32), axis=0, keepdims=True)
                do_ref[there] = low
                dot_ref[:, at] = low.T
                return carry

            for n in range(seqs):
                for split in rows_in[2 * n : 2 * n + 2]:
                    split.finish()
                lax.fori_loop(n * span // 128, (n + 1) * span // 128, middle, 0)
            rows_out.start()

        @pl.when((t > tiles) & (t <= 2 * tiles))
        def _():
            j = t - tiles - 1
            total = jnp.zeros((1, TILE), f32)
            for i in range(rows // CHUNK):
                at = slice(i * CHUNK, (i + 1) * CHUNK)
                d_act = dot_t(do_ref[span_of(i * CHUNK)], w2_ref[...])
                d_in = (d_act * slope_ref[j, at].astype(f32)).astype(bf16)
                total += jnp.sum(d_in.astype(f32), axis=0, keepdims=True)
                di_ref[at] = d_in
            gb1_ref[:, pl.ds(pl.multiple_of(j * TILE, TILE), TILE)] = total
            value = dot(lowt_ref[...], di_ref[...]).astype(bf16)
            gw1_ref[lax.rem(j, kept)] = value.reshape(lay.dims + (depth, TILE))
            hooks.at(j, range(tiles))
            for i in range(rows // CHUNK):
                at = slice(i * CHUNK, (i + 1) * CHUNK)
                acc_ref[at] += dot_t(di_ref[at], w1_ref[...])

        @pl.when(t == 2 * tiles)
        def _():
            def back(i, carry):
                at = pl.ds(pl.multiple_of(i * 128, 128), 128)
                seq = (i * 128) // span
                there = (seq, pl.ds(pl.multiple_of(i * 128 - seq * span, 128), 128))
                grad, normal = acc_ref[at], d1_ref[at]
                sums_ref[4:5] += jnp.sum(grad * normal, axis=0, keepdims=True)
                sums_ref[5:6] += jnp.sum(grad, axis=0, keepdims=True)
                scaled = grad * gain1
                mean = jnp.mean(scaled, axis=-1, keepdims=True)
                along = jnp.mean(scaled * normal, axis=-1, keepdims=True)
                d_one = inv1_ref[at] * (scaled - mean - normal * along)
                d1_ref[at] = d_one
                db_ref[there] = d_one.astype(bf16)
                return carry

            lax.fori_loop(0, rows // 128, back, 0)

        @pl.when(t > 2 * tiles)
        def _():
            j = t - 2 * tiles - 1
            gw2 = dot(dot_ref[...], act_ref[j]).astype(bf16)
            if wide:
                for d in range(per_tile):
                    gw2_ref[d] = gw2[:, d * share : (d + 1) * share]
            else:
                gw2_ref[...] = gw2
            hooks.at(t - tiles - 1, range(tiles, 2 * tiles))

        @pl.when(t == 2 * tiles + 1)
        def _():
            small_ref[...] = jnp.zeros_like(small_ref)
            loss = jnp.broadcast_to(jnp.sum(sums_ref[0:1], axis=-1, keepdims=True), (1, 128))
            for d in range(devices):
                at = lay.place(d)
                small_ref[at + (slice(0, 5), slice(0, share1))] = sums_ref[1:6, d * share1 : (d + 1) * share1]
                small_ref[at + (slice(5, 6), slice(0, share))] = gb1_ref[:, d * share : (d + 1) * share]
                small_ref[at + (slice(6, 7),)] = loss

        @pl.when(t == 3 * tiles)
        def _():
            save = pltpu.make_async_copy(db_ref, db_out, own.at[pieces])
            save.start()
            for k in range(2 * tiles, last + 1):
                hooks.run(k)
            for part in sums:
                part.drain()
            rows_out.finish()
            save.wait()

    def tile(t, *_):
        return jnp.where(t < tiles, t, jnp.clip(t - tiles - 1, 0, tiles - 1))

    def outer_tile(t, *_):
        return jnp.maximum(t - 2 * tiles - 1, 0)

    full = once((rows, width))
    vec = pl.BlockSpec((1, TILE), lambda t, *_: (0, tile(t)))
    low = pltpu.VMEM((seqs, span, width), bf16)
    return pl.pallas_call(
        kernel,
        grid_spec=pltpu.PrefetchScalarGridSpec(
            num_scalar_prefetch=0,
            grid=(3 * tiles + 1,),
            in_specs=[
                pl.BlockSpec(memory_space=pltpu.SMEM), ANY, ANY, ANY, once((8, width)), vec,
                pl.BlockSpec((width, TILE), lambda t, *_: (0, tile(t))),
                pl.BlockSpec((TILE, width), lambda t, *_: (tile(t), 0)),
            ],
            out_specs=[
                ANY, full, ANY, once((depth, hidden)),
                pl.BlockSpec((per_tile, width, share), lambda t, *_: (outer_tile(t), 0, 0))
                if wide else pl.BlockSpec((width, TILE), lambda t, *_: (0, outer_tile(t))),
                once(lay.dims + (8, 128)),
            ],
            scratch_shapes=[
                low, pltpu.VMEM((width, rows), bf16),
                pltpu.VMEM((tiles, rows, TILE), bf16), pltpu.VMEM((tiles, rows, TILE), bf16),
                pltpu.VMEM((rows, width), f32), low, pltpu.VMEM((width, rows), bf16),
                pltpu.VMEM((rows, 1), f32), pltpu.VMEM((rows, TILE), bf16), low,
                pltpu.VMEM((kept,) + lay.dims + (depth, columns), bf16),
                pltpu.VMEM((8, width), f32), pltpu.VMEM((1, hidden), f32),
            ]
            + sems(lay, 0, 2 * seqs + 1)[3:]
            + sems(lay, pieces + 1, 0)[:3]
            + [b for way in ways for b in Scatter.buffers(lay, (0, depth, 0, columns), bf16, way)],
        ),
        out_shape=[
            jax.ShapeDtypeStruct(teacher.shape, bf16),
            jax.ShapeDtypeStruct((rows, width), f32),
            jax.ShapeDtypeStruct((seqs, span, width), bf16),
            jax.ShapeDtypeStruct((depth, hidden), f32),
            jax.ShapeDtypeStruct((devices, width, share) if wide else (width, hidden), bf16),
            jax.ShapeDtypeStruct(lay.dims + (8, 128), f32),
        ],
        compiler_params=pltpu.CompilerParams(
            collective_id=2, has_side_effects=True, vmem_limit_bytes=63 << 20),
        name="feed_forward",
    )(lengths, h1, teacher, out_grad, vecs, bias_inner, w1, w2)


def finish(d_tokens, small, vecs, share, deep, whole):
    seqs, span, width = d_tokens.shape
    n, steps = len(whole), 2

    def kernel(dx_ref, small_ref, vec_ref, *refs):
        ins, refs = refs[:n], refs[n:]
        dx_out, loss_ref, bias_ref = refs[:3]
        for i, vec in enumerate(refs[3:8]):
            vec[...] = small_ref[i : i + 1, :share]
        for a, b in zip(ins, refs[8:]):
            if a.ndim == 3:
                b[...] = a[...]
            else:
                pl.when(pl.program_id(0) == 0)(lambda a=a, b=b: b.__setitem__(Ellipsis, a[...]))
        loss_ref[...] = small_ref[6:7, :1] * vec_ref[5:6, :1]
        bias_ref[...] = small_ref[5:6, :deep]
        dx_out[...] = dx_ref[...].astype(f32)

    def block(a):
        if a.ndim == 3:
            return pl.BlockSpec((a.shape[0] // steps,) + a.shape[1:], lambda i: (i, 0, 0))
        return once(a.shape)

    like = lambda a, dtype: jax.ShapeDtypeStruct(a.shape, dtype)
    blocks = [block(a) for a in whole]
    out = pl.pallas_call(
        kernel,
        grid=(steps,),
        in_specs=[block(d_tokens), once((8, 128)), once((8, width))] + blocks,
        out_specs=[block(d_tokens), once((1, 1)), once((1, deep))] + [once((1, share))] * 5 + blocks,
        out_shape=[like(d_tokens, f32), jax.ShapeDtypeStruct((1, 1), f32), jax.ShapeDtypeStruct((1, deep), f32)]
        + [jax.ShapeDtypeStruct((1, share), f32)] * 5
        + [like(a, a.dtype) for a in whole],
        compiler_params=pltpu.CompilerParams(vmem_limit_bytes=63 << 20),
        name="finish",
    )(d_tokens, small, vecs, *whole)
    return out[0], out[1], out[2], out[3:8], out[8:]


def cut(shape, which, pieces, orders, columns=False):
    rows, wide = shape
    if columns:
        step = wide // pieces
        return [(which, (0, rows, i * step, step), orders) for i in range(pieces)]
    while pieces > 1 and rows % (pieces * 16):
        pieces -= 1
    step = rows // pieces
    return [(which, (i * step, step), orders) for i in range(pieces)]


def shards(
    lay, tokens, lengths, teacher, out_grad, w_query, w_key, w_value, w_output, gain_one, shift_one,
    w_inner, bias_inner, w_outer, bias_outer, gain_two, shift_two,
):
    width = tokens.shape[2]
    hidden = w_inner.shape[1]
    devices = lay.devices
    there = (("z", "x", "y"), ("z", "y", "x"))
    back = (("y", "x", "z"), ("x", "y", "z"))
    aside = (("x", "y", "z"),) * 2
    share, deep = gain_one.shape[0], bias_inner.shape[0]
    ins = [w_query, w_key, w_value, w_output, w_inner, w_outer]
    parts = [(6, (0, 8), there)]
    for i in range(4):
        parts += cut(ins[i].shape, i, 1, there)
    early = len(parts)
    parts += cut(w_inner.shape, 4, 8, there, True) + cut(w_outer.shape, 5, 8, there)
    vectors = [gain_one, shift_one, bias_outer, gain_two, shift_two, bias_inner]
    wq, wk, wv, wo, w1, w2, xt, q, k, v, att, lse, h1, vecs, bias1 = attention_forward(
        lay, tokens, lengths, vectors, ins, parts, early
    )
    wq, wk, wv, wo = (w.reshape(width, width) for w in (wq, wk, wv, wo))
    w1, w2 = w1.reshape(width, hidden), w2.reshape(hidden, width)
    layer_out, d_one, d_branch, g_inner, gw2, small = feed_forward(
        lay, h1, teacher, out_grad, lengths, vecs, bias1, w1, w2, back, aside
    )
    if gw2.ndim == 2:
        gw2 = gw2.T.reshape(devices, hidden // devices, width)
    g_query, g_key, g_value, g_output, g_outer, small, d_tokens = attention_backward(
        lay, xt, lengths, wq, wk, wv, wo, q, k, v, att, lse, d_branch, d_one, gw2, small, back, aside
    )
    d_tokens, loss, g_bias, vec_grads, copied = finish(
        d_tokens, small, vecs, share, deep, [layer_out, g_query, g_key, g_value, g_output, g_inner, g_outer]
    )
    layer_out, g_query, g_key, g_value, g_output, g_inner, g_outer = copied
    vec = lambda i: vec_grads[i][0]
    return (
        loss[0, 0],
        layer_out,
        d_tokens,
        g_query,
        g_key,
        g_value,
        g_output,
        vec(3),
        vec(4),
        g_inner,
        g_bias[0],
        g_outer,
        vec(2),
        vec(0),
        vec(1),
    )


def solution(mesh):
    lay = Layout(mesh)
    rows = P("dp", "blk", None)
    weight = P(("dp", "blk"), None)
    vector = P(("dp", "blk"))
    return jax.shard_map(
        lambda *args: shards(lay, *args),
        mesh=mesh,
        in_specs=(
            rows, P("dp"), rows, rows, weight, weight, weight, weight, vector, vector,
            weight, vector, weight, vector, vector, vector,
        ),
        out_specs=(
            P(), rows, rows, weight, weight, weight, weight, vector, vector,
            weight, vector, weight, vector, vector, vector,
        ),
        check_vma=False,
    )
```

```python
import math

import jax
import jax.numpy as jnp
from jax import lax
from jax.experimental import pallas as pl
from jax.experimental.pallas import tpu as pltpu
from jax.sharding import PartitionSpec as P

ANY = pl.BlockSpec(memory_space=pl.ANY)
MESH = pl.DeviceIdType.MESH
f32 = jnp.float32
bf16 = jnp.bfloat16


class Layout:
    def __init__(self, mesh):
        dp, blk = mesh.shape["dp"], mesh.shape["blk"]
        if dp == 8 and blk == 4:
            dims = [("z", "dp", 2, 4), ("x", "dp", 1, 2), ("y", "blk", 2, 2), ("c", "blk", 1, 2)]
        else:
            dims = [("z", "dp", dp // 4, 4), ("x", "dp", 2, dp // 8), ("c", "dp", 1, 2), ("y", "blk", 1, blk)]
        self.order = [d[0] for d in dims]
        self.axis = {d[0]: d[1] for d in dims}
        self.stride = {d[0]: d[2] for d in dims}
        self.size = {d[0]: d[3] for d in dims}
        self.dims = tuple(d[3] for d in dims)
        self.blk = blk
        self.devices = dp * blk
        self.slot = {}
        count = 0
        for name in self.order:
            self.slot[name] = count
            count += self.size[name] - 1
        self.slots = count

    def here(self):
        return {
            name: lax.rem(lax.axis_index(self.axis[name]) // self.stride[name], self.size[name])
            for name in self.order
        }

    def step_to(self, here, name, distance):
        there = lax.rem(here[name] + distance, self.size[name])
        index = lax.axis_index(self.axis[name]) + (there - here[name]) * self.stride[name]
        return there, {self.axis[name]: index}

    def at(self, here, whole, changed=(), names=None):
        changed = dict(changed)
        return tuple(
            slice(None) if name in whole else changed.get(name, here[name])
            for name in (names or self.order)
        )

    def place(self, device):
        index = []
        for size in reversed(self.dims):
            index.append(lax.rem(device, size))
            device = device // size
        return tuple(reversed(index))

    def greet(self, here):
        barrier = pltpu.get_barrier_semaphore()
        count = 0
        for name in self.order:
            if self.axis[name] == "blk":
                continue
            for distance in range(1, self.size[name]):
                _, device = self.step_to(here, name, distance)
                pl.semaphore_signal(barrier, inc=1, device_id=device, device_id_type=MESH)
                count += 1
        me = lax.axis_index("blk")
        for distance in range(1, self.blk):
            pl.semaphore_signal(
                barrier, inc=1, device_id={"blk": lax.rem(me + distance, self.blk)}, device_id_type=MESH
            )
            count += 1
        pl.semaphore_wait(barrier, count)


def window(cut):
    if len(cut) == 2:
        return (pl.ds(*cut),)
    return (pl.ds(cut[0], cut[1]), pl.ds(cut[2], cut[3]))


def by_core(here, orders, make):
    if orders[0] == orders[1]:
        make(orders[0])
        return
    for core in range(2):
        @pl.when(here["c"] == core)
        def _():
            make(orders[core])


class Gather:
    stages = 5

    def __init__(self, lay, here, src, full, rows, send, recv, own, orders):
        self.lay, self.here = lay, here
        self.rows = window(rows)
        self.src, self.full = src.at[self.rows], full
        self.send, self.recv, self.own = send, recv, own
        self.orders = orders

    def line(self, name, whole):
        copies = []
        place = self.full.at[self.lay.at(self.here, whole) + self.rows]
        source = self.src if not whole else place
        for distance in range(1, self.lay.size[name]):
            _, device = self.lay.step_to(self.here, name, distance)
            slot = self.lay.slot[name] + distance - 1
            copies.append(
                pltpu.make_async_remote_copy(
                    src_ref=source, dst_ref=place, send_sem=self.send.at[slot], recv_sem=self.recv.at[slot],
                    device_id=device, device_id_type=MESH,
                )
            )
        return copies

    def local(self):
        return pltpu.make_async_copy(self.src, self.full.at[self.lay.at(self.here, ()) + self.rows], self.own)

    def stage(self, k):
        if k == 1:
            self.local().wait()

        def make(order):
            lines = tuple(order) + ("c",)
            if k > 0:
                for c in self.line(lines[k - 1], lines[: k - 1]):
                    c.wait_recv()
            if k < 4:
                for c in self.line(lines[k], lines[:k]):
                    c.start()

        if k == 0:
            self.local().start()
        by_core(self.here, self.orders, make)

    def drain(self):
        def make(order):
            lines = tuple(order) + ("c",)
            for k in range(4):
                for c in self.line(lines[k], lines[:k]):
                    c.wait_send()
        by_core(self.here, self.orders, make)


class Resplit:
    def __init__(self, lay, src, dst, send, recv, own, back=False, first=0):
        self.lay, self.src, self.dst = lay, src, dst
        self.first = first
        self.send, self.recv, self.own = send, recv, own
        self.me = lax.axis_index("blk")
        self.back = back
        self.seqs = (src if back else dst).shape[0]
        self.total = (dst if back else src).shape[0] // lay.blk
        self.span = (dst if back else src).shape[1]

    def ends(self, there):
        if self.back:
            return (self.src.at[:, pl.ds(there * self.span, self.span)],
                    self.dst.at[pl.ds(self.me * self.total + self.first, self.seqs)])
        return (self.src.at[pl.ds(there * self.total + self.first, self.seqs)],
                self.dst.at[:, pl.ds(self.me * self.span, self.span)])

    def copies(self):
        out = []
        for distance in range(1, self.lay.blk):
            there = lax.rem(self.me + distance, self.lay.blk)
            src, dst = self.ends(there)
            out.append(
                pltpu.make_async_remote_copy(
                    src_ref=src, dst_ref=dst,
                    send_sem=self.send.at[distance - 1], recv_sem=self.recv.at[distance - 1],
                    device_id={"blk": there}, device_id_type=MESH,
                )
            )
        return out

    def local(self):
        src, dst = self.ends(self.me)
        return pltpu.make_async_copy(src, dst, self.own)

    def start(self):
        self.local().start()
        for c in self.copies():
            c.start()

    def finish(self):
        self.local().wait()
        for c in self.copies():
            c.wait()


class Scatter:
    stages = 5

    def __init__(self, lay, here, grad, cut, out, bufs, send, recv, own, orders, staged=None, turn=False):
        self.turn = turn
        self.lay, self.here, self.grad, self.cut = lay, here, grad, window(cut)
        self.out, self.held, self.recvs, self.staged = out, bufs[0], bufs[1:], staged
        self.send, self.recv, self.own = send, recv, own
        self.orders = orders
        self.names = [n for n in lay.order if n != "c"]

    @staticmethod
    def buffers(lay, cut, dtype, orders):
        shape = (cut[1], cut[3])
        names = [n for n in lay.order if n != "c"]
        out = [pltpu.VMEM(tuple(lay.size[n] for n in names) + shape, dtype)]
        for k in range(3):
            lines = orders[0][k + 1 :]
            left = tuple(lay.size[n] for n in names if n in lines)
            out.append(pltpu.VMEM((lay.size[orders[0][k]] - 1,) + left + shape, dtype))
        return out

    def local(self):
        return pltpu.make_async_copy(
            self.grad.at[self.lay.at(self.here, self.names) + self.cut], self.staged, self.own)

    def core(self):
        there, device = self.lay.step_to(self.here, "c", 1)
        slot = self.lay.slot["c"]
        return pltpu.make_async_remote_copy(
            src_ref=self.grad.at[self.lay.at(self.here, self.names, {"c": there}) + self.cut], dst_ref=self.held,
            send_sem=self.send.at[slot], recv_sem=self.recv.at[slot], device_id=device, device_id_type=MESH)

    def line(self, order, k):
        name, left = order[k], order[k + 1 :]
        copies = []
        for distance in range(1, self.lay.size[name]):
            there, device = self.lay.step_to(self.here, name, distance)
            slot = self.lay.slot[name] + distance - 1
            copies.append(
                pltpu.make_async_remote_copy(
                    src_ref=self.held.at[self.lay.at(self.here, left, {name: there}, self.names)],
                    dst_ref=self.recvs[k].at[distance - 1],
                    send_sem=self.send.at[slot], recv_sem=self.recv.at[slot],
                    device_id=device, device_id_type=MESH,
                )
            )
        return copies

    def add(self, order, k):
        left = [n for n in self.names if k < 0 or n in order[k + 1 :]]
        steps = self.lay.size[left[0]] if left else 1

        def one(i, carry):
            index = {n: slice(None) for n in left}
            if left:
                index[left[0]] = i
            mine = tuple(index.get(n, self.here[n]) for n in self.names)
            alone = k < 0 or (k < 2 and self.lay.size[order[k]] == 2)
            wide = self.held.dtype if alone else f32
            value = self.held[mine].astype(wide)
            if k >= 0:
                theirs = tuple(index[n] for n in left)
                for d in range(self.lay.size[order[k]] - 1):
                    value = value + self.recvs[k][(d,) + theirs].astype(wide)
            elif self.staged is not None:
                value = value + self.staged[mine].astype(wide)
            else:
                value = value + self.grad[self.lay.at({**self.here, **index}, ()) + self.cut].astype(wide)
            if k == 2:
                self.out[...] = value.T if self.turn else value
            else:
                self.held[mine] = value.astype(self.held.dtype)
            return carry

        lax.fori_loop(0, steps, one, 0)

    def stage(self, k):
        if k == 0:
            self.core().start()
            if self.staged is not None:
                self.local().start()
            return
        if k == 1:
            if self.staged is not None:
                self.local().wait()
            self.core().wait()
            self.add(None, -1)

        def make(order):
            if k > 1:
                for c in self.line(order, k - 2):
                    c.wait_recv()
                self.add(order, k - 2)
            if k < 4:
                for c in self.line(order, k - 1):
                    c.start()

        by_core(self.here, self.orders, make)

    def drain(self):
        def make(order):
            for k in range(3):
                for c in self.line(order, k):
                    c.wait_send()

        by_core(self.here, self.orders, make)


def skewed(parts, lag=1, stages=5):
    events = []
    for t in range(len(parts) + lag * (stages - 1)):
        for i, part in enumerate(parts):
            stage, rest = divmod(t - i, lag)
            if rest == 0 and 0 <= stage < stages:
                events.append((part, stage))
    return events


class Hooks:
    def __init__(self):
        self.slots = {}

    def put(self, slot, event):
        self.slots.setdefault(slot, []).append(event)

    def spread(self, events, first, last):
        for n, event in enumerate(events):
            self.put(first + n * (last - first) // len(events), event)

    def run(self, slot):
        for part, stage in self.slots.get(slot, ()):
            part.stage(stage)

    def at(self, step, slots):
        for k in slots:
            if k in self.slots:
                pl.when(step == k)(lambda k=k: self.run(k))


def sems(lay, n, m):
    dma = pltpu.SemaphoreType.DMA
    n, m = max(n, 1), max(m, 1)
    return [dma((n, lay.slots)), dma((n, lay.slots)), dma((n,)), dma((m, lay.blk - 1)), dma((m, lay.blk - 1)), dma((m,))]


DH = 64
LOG2E = math.log2(math.e)
GROUP = 256


def dot(a, b):
    return lax.dot_general(a, b, (((1,), (0,)), ((), ())), preferred_element_type=f32)


def dot_t(a, b):
    return lax.dot_general(a, b, (((1,), (1,)), ((), ())), preferred_element_type=f32)


def once(shape):
    return pl.BlockSpec(shape, lambda *_: (0,) * len(shape), pipeline_mode=pl.Buffered(1))


def attention_forward(lay, tokens, lengths, vectors, shards, parts, early):
    width = tokens.shape[2]
    seqs, span = tokens.shape[0] // lay.blk, tokens.shape[1] * lay.blk
    rows = seqs * span
    groups = width // GROUP
    scale = LOG2E / math.sqrt(DH)
    heads = seqs * GROUP // DH
    pairs = seqs * GROUP // 128
    n, p, m = len(shards), len(parts), len(vectors)
    share, deep = vectors[0].shape[0], vectors[-1].shape[0]
    slots = pairs + 3

    def kernel(len_ref, *refs):
        vecs, refs = refs[:m], refs[m:]
        tok_ref, refs = refs[0], refs[1:]
        ins, refs = refs[:n], refs[n:]
        fulls, refs = refs[:n], refs[n:]
        xt_out, q_out, k_out, v_out, att_out, lse_ref, h1_out, vec_out, bias_out = refs[:9]
        x_ref, wq_ref, wk_ref, wv_ref, wo_ref, q_ref, k_ref, v_ref, att_ref, h1_ref, pack_ref, packs_ref, low_ref, xt_ref = refs[9:23]
        load, send, recv, own, rsend, rrecv, rown = refs[23:]
        ins, fulls = list(ins) + [pack_ref], list(fulls) + [packs_ref]
        here = lay.here()
        pack_ref[...] = jnp.zeros_like(pack_ref)
        for i, vec in enumerate(vecs):
            pack_ref[i : i + 1, : vec.shape[0]] = vec[...].astype(f32).reshape(1, vec.shape[0])
        tokens_here = len_ref[0]
        for i in range(1, lengths.shape[0]):
            tokens_here = tokens_here + len_ref[i]
        pack_ref[m : m + 1] = jnp.full((1, 128), tokens_here.astype(f32))
        lay.greet(here)
        split = Resplit(lay, tok_ref, x_ref, rsend, rrecv, rown)
        split.start()
        gathers = [
            Gather(lay, here, ins[a], fulls[a], cut, send.at[i], recv.at[i], own.at[i], orders)
            for i, (a, cut, orders) in enumerate(parts)
        ]
        events = skewed(gathers, 3)
        last = max(i for i, (part, stage) in enumerate(events) if part in gathers[:early] and stage == 4)
        for part, stage in events[: last + 1]:
            part.stage(stage)
        split.finish()
        loads = [
            pltpu.make_async_copy(src, dst, load.at[i])
            for i, (src, dst) in enumerate(
                zip(fulls[:4], [wq_ref, wk_ref, wv_ref, wo_ref]))
        ]
        for c in loads:
            c.start()
        for c in loads:
            c.wait()
        hooks = Hooks()
        hooks.spread(events[last + 1 :], 0, groups * slots * 6 // 5)
        base = lax.axis_index("blk") * seqs

        def columns(ref, g):
            block = ref[(slice(None),) * 5 + (pl.ds(pl.multiple_of(g * GROUP, GROUP), GROUP),)]
            return block.reshape(width, GROUP)

        def features(ref, g):
            per = GROUP // ref.shape[-2]
            return jnp.concatenate([ref[lay.place(g * per + j)] for j in range(per)], axis=0)

        def step(i, carry):
            g, r = i // pairs, lax.rem(i, pairs)
            cols = pl.ds(pl.multiple_of(g * GROUP, GROUP), GROUP)

            @pl.when(r == 0)
            def _():
                xv = x_ref[...].reshape(rows, width)
                for j, (low, weight) in enumerate(((q_ref, wq_ref), (k_ref, wk_ref), (v_ref, wv_ref))):
                    low[:, cols] = dot(xv, columns(weight, g)).astype(bf16)
                    hooks.at(g * slots + j, range(j, groups * slots, slots))

            @pl.when(i == groups * pairs // 4)
            def _():
                for n in range(seqs):
                    xt_ref[:, n * span : (n + 1) * span] = x_ref[n].T

            @pl.when(i == groups * pairs // 2)
            def _():
                total = jnp.zeros((1, 128), f32)
                for d in range(lay.devices):
                    tile = packs_ref[lay.place(d)]
                    vec_out[0 : m - 1, d * share : (d + 1) * share] = tile[0 : m - 1, :share]
                    bias_out[:, d * deep : (d + 1) * deep] = tile[m - 1 : m, :deep]
                    total = total + tile[m : m + 1]
                inverse = 1.0 / (total / lay.blk * width)
                for d in range(width // 128):
                    vec_out[m - 1 : m, d * 128 : (d + 1) * 128] = inverse

            s, pair = r // (GROUP // 128), lax.rem(r, GROUP // 128)
            at = (pl.ds(pl.multiple_of(s * span, span), span),
                  pl.ds(pl.multiple_of(g * GROUP + pair * 128, 128), 128))
            qs, ks, vs = q_ref[at], k_ref[at], v_ref[at]
            lane = lax.broadcasted_iota(jnp.int32, (span, 128), 1)
            keep = lax.broadcasted_iota(jnp.int32, (span, 1), 0) < len_ref[base + s]
            vt = vs.T
            outs = []
            for h in range(2):
                km = jnp.where((lane < DH) if h == 0 else (lane >= DH), ks, jnp.zeros_like(ks))
                st = dot_t(km, qs) * scale
                st = jnp.where(keep, st, -1e30)
                top = jnp.max(st, axis=0, keepdims=True)
                e = jnp.exp2(st - top)
                den = jnp.sum(e, axis=0, keepdims=True)
                ot = dot(vt[h * DH : (h + 1) * DH], e.astype(bf16))
                outs.append(ot * (1.0 / den))
                lse_ref[g, pl.ds(r * 2 + h, 1)] = top + jnp.log2(den)
            turned = jnp.concatenate(outs, axis=0)
            att_ref[at[1], at[0]] = turned.astype(bf16)
            low_ref[at[0], pl.ds(pl.multiple_of(pair * 128, 128), 128)] = turned.T.astype(bf16)

            @pl.when(r == pairs - 1)
            def _():
                add = dot(low_ref[...], features(wo_ref, g))

                @pl.when(g == 0)
                def _():
                    h1_ref[...] = x_ref[...].reshape(rows, width).astype(f32) + add

                @pl.when(g > 0)
                def _():
                    h1_ref[...] += add

            hooks.at(g * slots + 3 + r, [k for k in range(groups * slots) if k % slots >= 3])
            return carry

        lax.fori_loop(0, groups * pairs, step, 0)
        saves = [
            pltpu.make_async_copy(src, dst, load.at[i])
            for i, (src, dst) in enumerate(
                zip([xt_ref, q_ref, k_ref, v_ref, att_ref, h1_ref], [xt_out, q_out, k_out, v_out, att_out, h1_out]))
        ]
        for c in saves:
            c.start()
        for k in sorted(hooks.slots):
            if k >= groups * slots:
                hooks.run(k)
        for g in gathers:
            g.drain()
        for c in saves:
            c.wait()

    whole = [jax.ShapeDtypeStruct(lay.dims + s.shape, s.dtype) for s in shards]
    vmem = pl.BlockSpec(memory_space=pltpu.VMEM)
    act, turned = jax.ShapeDtypeStruct((rows, width), bf16), jax.ShapeDtypeStruct((width, rows), bf16)
    return pl.pallas_call(
        kernel,
        in_specs=[pl.BlockSpec(memory_space=pltpu.SMEM)] + [vmem] * m + [ANY] + [vmem] * n,
        out_specs=[ANY] * (n + 5) + [vmem, ANY, vmem, vmem],
        out_shape=whole
        + [turned, act, act, act, turned,
           jax.ShapeDtypeStruct((groups, heads, span), f32), jax.ShapeDtypeStruct((rows, width), f32),
           jax.ShapeDtypeStruct((8, width), f32), jax.ShapeDtypeStruct((1, deep * lay.devices), f32)],
        scratch_shapes=[pltpu.VMEM((seqs, span, width), bf16)]
        + [pltpu.VMEM(lay.dims + s.shape, bf16) for s in shards[:4]]
        + [pltpu.VMEM((rows, width), bf16)] * 3 + [pltpu.VMEM((width, rows), bf16)]
        + [pltpu.VMEM((rows, width), f32), pltpu.VMEM((8, 128), f32), pltpu.VMEM(lay.dims + (8, 128), f32),
           pltpu.VMEM((rows, GROUP), bf16), pltpu.VMEM((width, rows), bf16),
           pltpu.SemaphoreType.DMA((6,))]
        + sems(lay, p, 0)[:3]
        + [pltpu.SemaphoreType.DMA((lay.blk - 1,)), pltpu.SemaphoreType.DMA((lay.blk - 1,)),
           pltpu.SemaphoreType.DMA],
        compiler_params=pltpu.CompilerParams(collective_id=1, has_side_effects=True, vmem_limit_bytes=60 << 20),
        name="attention_forward",
    )(lengths, *vectors, tokens, *shards)


def attention_backward(lay, xt, lengths, wq, wk, wv, wo, q, k, v, att, lse, d_branch, d_one, outer, small, orders, aside):
    seqs, span, width = d_branch.shape
    rows = seqs * span
    heads = lse.shape[1]
    groups = width // GROUP
    pairs = seqs * GROUP // 128
    steps = pairs + 1
    depth = width // lay.devices
    scale = LOG2E / math.sqrt(DH)
    deep, share = outer.shape[1:]
    pieces, lag = 8, 3
    while deep % (pieces * 16):
        pieces //= 2
    outer_cuts = [(i * deep // pieces, deep // pieces, 0, share) for i in range(pieces)]
    small_cut = (0, 8, 0, 128)
    wo_cuts = [(0, depth, i * width // 2, width // 2) for i in range(2)]
    late_cuts = [((0, depth, c * GROUP, GROUP), c) for c in range(groups)]
    bufs = [Scatter.buffers(lay, c, bf16, orders) for c in outer_cuts + wo_cuts]
    bufs += [Scatter.buffers(lay, small_cut, f32, orders)]
    bufs += [Scatter.buffers(lay, c, bf16, aside) for c, _ in late_cuts for _ in range(3)]
    count = len(bufs)
    wide = deep == width
    outer = outer.reshape(lay.dims + outer.shape[1:])

    def kernel(
        len_ref, xt_ref, wq_ref, wk_ref, wv_ref, wo_ref, q_ref, k_ref, v_ref, att_ref, lse_ref, db_ref, d1_in, outer_in, small_in,
        gq_out, gk_out, gv_out, go_out, outer_out, small_out, dx_out,
        gq_ref, gk_ref, gv_ref, go_ref, do_ref, dq_ref, dk_ref, dv_ref, acc_ref, dx_ref,
        stage_small, stage_ref, send, recv, own, rsend, rrecv, rown, fetch_sem, *held,
    ):
        g = pl.program_id(0)
        here = lay.here()
        base = lax.axis_index("blk") * seqs
        made = []

        def part(grad, cut, out, way, staged=None, turn=False):
            i = len(made)
            made.append(Scatter(
                lay, here, grad, cut, out, held[4 * i : 4 * i + 4], send.at[i], recv.at[i], own.at[i], way, staged, turn))
            return made[-1]

        first = [
            part(outer_in, c, outer_out.at[:, pl.ds(c[0], c[1])] if wide else outer_out.at[pl.ds(c[0], c[1])], orders,
                 stage_ref.at[i % (lag + 1)], wide)
            for i, c in enumerate(outer_cuts)
        ]
        first += [part(go_ref, c, go_out.at[:, pl.ds(c[2], c[3])], orders) for c in wo_cuts]
        first += [part(small_in, small_cut, small_out, orders, stage_small)]
        hooks = Hooks()
        events = skewed(first, lag)
        hooks.spread(events[lag:], 0, groups * steps - 1)
        finals = []
        for c, group in late_cuts:
            parts = [
                part(ref, c, out.at[:, pl.ds(c[2], c[3])], aside)
                for ref, out in ((gq_ref, gq_out), (gk_ref, gk_out), (gv_ref, gv_out))
            ]
            ready = (group + 1) * steps - 1
            for stage in range(5):
                for i, p in enumerate(parts):
                    hooks.put(ready + i + 3 * stage, (p, stage))
        for k in sorted(hooks.slots):
            if k >= groups * steps - 1:
                finals += hooks.slots.pop(k)
        splits = [
            Resplit(lay, dx_ref.at[pl.ds(s, 1)], dx_out, rsend.at[s], rrecv.at[s], rown.at[s], True, s) for s in range(seqs)
        ]

        @pl.when(g == 0)
        def _():
            lay.greet(here)
            for p, stage in events[:lag]:
                p.stage(stage)
            fetch = pltpu.make_async_copy(d1_in, acc_ref, fetch_sem)
            fetch.start()

            def output_rows(j, carry):
                value = dot(att_ref[pl.ds(pl.multiple_of(j * GROUP, GROUP), GROUP)], db_ref[...].reshape(rows, width)).astype(bf16)
                for d in range(GROUP // depth):
                    go_ref[lay.place(j * (GROUP // depth) + d)] = value[d * depth : (d + 1) * depth]
                return carry

            lax.fori_loop(0, groups, output_rows, 0)
            fetch.wait()

        do_ref[...] = dot_t(db_ref[...].reshape(rows, width), wo_ref[...]).astype(bf16)

        def pair_step(i, carry):
            s, pair = i // (GROUP // 128), lax.rem(i, GROUP // 128)
            at = (pl.ds(pl.multiple_of(s * span, span), span), pl.ds(pl.multiple_of(pair * 128, 128), 128))
            length = len_ref[base + s]
            qs, ks, vs, dos = q_ref[at], k_ref[at], v_ref[at], do_ref[at]
            lane = lax.broadcasted_iota(jnp.int32, (span, 128), 1)
            keep = lax.broadcasted_iota(jnp.int32, (span, 1), 0) < length
            kt = ks.T
            dqs, dks, dvs = [], [], []
            for h in range(2):
                mine = (lane < DH) if h == 0 else (lane >= DH)
                zero = jnp.zeros_like(ks)
                st = dot_t(jnp.where(mine, ks, zero), qs) * scale
                p = jnp.where(keep, jnp.exp2(st - lse_ref[0, pl.ds(i * 2 + h, 1)]), 0.0)
                dp = dot_t(jnp.where(mine, vs, zero), dos)
                delta = jnp.sum(p * dp, axis=0, keepdims=True)
                ds = (p * (dp - delta)).astype(bf16)
                dvs.append(dot(p.astype(bf16), dos))
                dks.append(dot(ds, qs))
                dqs.append(dot(kt[h * DH : (h + 1) * DH], ds))
            low_half = lane < DH
            unit = 1.0 / math.sqrt(DH)
            dv_ref[at] = jnp.where(low_half, dvs[0], dvs[1]).astype(bf16)
            dk_ref[at] = (jnp.where(low_half, dks[0], dks[1]) * unit).astype(bf16)
            dq_ref[at] = (jnp.concatenate(dqs, axis=0).T * unit).astype(bf16)

            @pl.when(pair == GROUP // 128 - 1)
            def _():
                mine = at[0]
                acc_ref[mine] += (
                    dot_t(dq_ref[mine], wq_ref[...]) + dot_t(dk_ref[mine], wk_ref[...]) + dot_t(dv_ref[mine], wv_ref[...])
                )

            for n in range(seqs):
                @pl.when((g == groups - 1) & (i == (n + 1) * (GROUP // 128) - 1))
                def _():
                    dx_ref[n] = acc_ref[n * span : (n + 1) * span].astype(bf16)
                    splits[n].start()

            hooks.at(g * steps + i, [k for k in range(groups * steps) if k % steps < pairs])
            return carry

        lax.fori_loop(0, pairs, pair_step, 0)
        xt = xt_ref[...]
        cols = (slice(None),) * 5 + (pl.ds(pl.multiple_of(g * GROUP, GROUP), GROUP),)
        for grad, low in ((gq_ref, dq_ref), (gk_ref, dk_ref), (gv_ref, dv_ref)):
            grad[cols] = dot(xt, low[...]).astype(bf16).reshape(lay.dims + (depth, GROUP))
        hooks.at(g * steps + pairs, [k for k in range(groups * steps) if k % steps == pairs])

        @pl.when(g == groups - 1)
        def _():
            for p, stage in finals:
                p.stage(stage)
            for p in made:
                p.drain()
            for split in splits:
                split.finish()

    col = pl.BlockSpec((width, GROUP), lambda g, *_: (0, g))
    row = pl.BlockSpec((GROUP, width), lambda g, *_: (g, 0))
    act = pl.BlockSpec((rows, GROUP), lambda g, *_: (0, g))
    vmem = pl.BlockSpec(memory_space=pltpu.VMEM)
    grad = pltpu.VMEM(lay.dims + (depth, width), bf16)
    no_core = tuple(lay.size[n] for n in lay.order if n != "c")
    shard = jax.ShapeDtypeStruct((depth, width), f32)
    return pl.pallas_call(
        kernel,
        grid_spec=pltpu.PrefetchScalarGridSpec(
            num_scalar_prefetch=0,
            grid=(groups,),
            in_specs=[pl.BlockSpec(memory_space=pltpu.SMEM), once((width, rows)), col, col, col, row, act, act, act, once((width, rows)),
                      pl.BlockSpec((1, heads, span), lambda g, *_: (g, 0, 0)), once((seqs, span, width)), ANY, ANY, ANY],
            out_specs=[once((depth, width))] * 4 + [once((share, deep) if wide else (deep, share)), once((8, 128)), ANY],
            scratch_shapes=[grad] * 4
            + [pltpu.VMEM((rows, GROUP), bf16)] * 4
            + [pltpu.VMEM((rows, width), f32), pltpu.VMEM((seqs, span, width), bf16)]
            + [pltpu.VMEM(no_core + (8, 128), f32)] + [pltpu.VMEM((lag + 1,) + no_core + (deep // pieces, share), bf16)]
            + sems(lay, count, 0)[:3]
            + sems(lay, 0, seqs)[3:] + [pltpu.SemaphoreType.DMA]
            + [b for bs in bufs for b in bs],
        ),
        out_shape=[shard] * 4
        + [jax.ShapeDtypeStruct((share, deep) if wide else (deep, share), f32), jax.ShapeDtypeStruct((8, 128), f32),
           jax.ShapeDtypeStruct((seqs * lay.blk, span // lay.blk, width), bf16)],
        compiler_params=pltpu.CompilerParams(
            collective_id=3, has_side_effects=True, vmem_limit_bytes=63 << 20),
        name="attention_backward",
    )(lengths, xt, wq, wk, wv, wo, q, k, v, att, lse, d_branch, d_one, outer, small)


TILE = 512
CHUNK = 512


def feed_forward(lay, h1, teacher, out_grad, lengths, vecs, bias_inner, w1, w2, orders, aside):
    rows, width = h1.shape
    hidden = w1.shape[1]
    seqs = teacher.shape[0] // lay.blk
    span = rows // seqs
    devices = lay.devices
    tiles = hidden // TILE
    share, share1 = hidden // devices, width // devices
    per_tile = TILE // share
    wide = share % 128 == 0
    pieces, depth, lag, kept = tiles, width // devices, 2, 4
    columns = hidden // pieces
    ways = [aside if i % 3 < 2 else orders for i in range(pieces)]

    def kernel(
        len_ref, h1_ref, teach_in, og_in, vec_ref, b1_ref, w1_ref, w2_ref,
        layer_out, d1_ref, db_out, gw1_out, gw2_ref, small_ref,
        low_ref, lowt_ref, act_ref, slope_ref, acc_ref, do_ref, dot_ref, inv1_ref, di_ref, db_ref, gw1_ref, sums_ref, gb1_ref,
        rsend, rrecv, rown, send, recv, own, *held,
    ):
        t = pl.program_id(0)
        here = lay.here()
        base = lax.axis_index("blk") * seqs
        rows_in = [
            Resplit(lay, src, dst.at[pl.ds(n, 1)], rsend.at[2 * n + i], rrecv.at[2 * n + i], rown.at[2 * n + i], first=n)
            for n in range(seqs) for i, (src, dst) in enumerate(((teach_in, do_ref), (og_in, db_ref)))
        ]
        rows_out = Resplit(lay, low_ref, layer_out, rsend.at[2 * seqs], rrecv.at[2 * seqs], rown.at[2 * seqs], True)
        sums = [
            Scatter(
                lay, here, gw1_ref.at[i % kept], (0, depth, 0, columns), gw1_out.at[:, pl.ds(i * columns, columns)],
                held[4 * i : 4 * i + 4], send.at[i], recv.at[i], own.at[i], ways[i])
            for i in range(pieces)
        ]
        hooks = Hooks()
        for slot in range(pieces + 4 * lag):
            for i in range(pieces):
                stage, rest = divmod(slot - i, lag)
                if rest == 0 and 0 <= stage < 5:
                    hooks.put(slot, (sums[i], stage))
        last = max(hooks.slots)
        span_of = lambda row: (row // span, pl.ds(row % span, CHUNK))
        gain1, shift1 = vec_ref[0:1], vec_ref[1:2]
        bias2, gain2, shift2 = vec_ref[2:3], vec_ref[3:4], vec_ref[4:5]

        @pl.when(t == 0)
        def _():
            lay.greet(here)
            for split in rows_in[:2]:
                split.start()
            fetch = pltpu.make_async_copy(h1_ref, d1_ref, own.at[pieces])
            fetch.start()
            fetch.wait()
            sums_ref[...] = jnp.zeros_like(sums_ref)

            def norm(i, carry):
                at = pl.ds(pl.multiple_of(i * 128, 128), 128)
                seq = (i * 128) // span
                there = (seq, pl.ds(pl.multiple_of(i * 128 - seq * span, 128), 128))
                h = d1_ref[at]
                centred = h - jnp.mean(h, axis=-1, keepdims=True)
                inverse = lax.rsqrt(jnp.mean(centred * centred, axis=-1, keepdims=True) + 1e-12)
                normal = centred * inverse
                d1_ref[at] = normal
                inv1_ref[at] = inverse
                low = (normal * gain1 + shift1).astype(bf16)
                low_ref[there] = low
                lowt_ref[:, at] = low.T
                return carry

            lax.fori_loop(0, rows // 128, norm, 0)
            acc_ref[...] = jnp.zeros_like(acc_ref)

        for n in range(1, seqs):
            @pl.when(t == n * tiles // seqs)
            def _():
                for split in rows_in[2 * n : 2 * n + 2]:
                    split.start()

        @pl.when(t < tiles)
        def _():
            for i in range(rows // CHUNK):
                at = slice(i * CHUNK, (i + 1) * CHUNK)
                inner = dot(low_ref[span_of(i * CHUNK)], w1_ref[...]) + b1_ref[...]
                cum = 0.5 * (1.0 + lax.erf(inner * (1.0 / math.sqrt(2.0))))
                density = jnp.exp(-0.5 * inner * inner) * (1.0 / math.sqrt(2.0 * math.pi))
                active = (inner * cum).astype(bf16)
                act_ref[t, at] = active
                slope_ref[t, at] = (cum + inner * density).astype(bf16)
                acc_ref[at] += dot(active, w2_ref[...])

        @pl.when(t == tiles)
        def _():
            inv = vec_ref[5:6]

            def middle(i, carry):
                at = pl.ds(pl.multiple_of(i * 128, 128), 128)
                normed = d1_ref[at] * gain1 + shift1
                h2 = normed + acc_ref[at] + bias2
                centred = h2 - jnp.mean(h2, axis=-1, keepdims=True)
                inverse = lax.rsqrt(jnp.mean(centred * centred, axis=-1, keepdims=True) + 1e-12)
                normal = centred * inverse
                result = normal * gain2 + shift2
                seq = (i * 128) // span
                first = i * 128 - seq * span
                there = (seq, pl.ds(pl.multiple_of(first, 128), 128))
                low_ref[there] = result.astype(bf16)
                pos = first + lax.broadcasted_iota(jnp.int32, (128, 1), 0)
                valid = (pos < len_ref[base + seq]).astype(f32)
                deviation = (result - do_ref[there].astype(f32)) * valid
                grad = db_ref[there].astype(f32) * valid + (2.0 * inv) * deviation
                sums_ref[0:1] += jnp.sum(deviation * deviation, axis=0, keepdims=True)
                sums_ref[1:2] += jnp.sum(grad * normal, axis=0, keepdims=True)
                sums_ref[2:3] += jnp.sum(grad, axis=0, keepdims=True)
                scaled = grad * gain2
                mean = jnp.mean(scaled, axis=-1, keepdims=True)
                along = jnp.mean(scaled * normal, axis=-1, keepdims=True)
                d_two = inverse * (scaled - mean - normal * along)
                acc_ref[at] = d_two
                low = d_two.astype(bf16)
                sums_ref[3:4] += jnp.sum(low.astype(f32), axis=0, keepdims=True)
                do_ref[there] = low
                dot_ref[:, at] = low.T
                return carry

            for n in range(seqs):
                for split in rows_in[2 * n : 2 * n + 2]:
                    split.finish()
                lax.fori_loop(n * span // 128, (n + 1) * span // 128, middle, 0)
            rows_out.start()

        @pl.when((t > tiles) & (t <= 2 * tiles))
        def _():
            j = t - tiles - 1
            total = jnp.zeros((1, TILE), f32)
            for i in range(rows // CHUNK):
                at = slice(i * CHUNK, (i + 1) * CHUNK)
                d_act = dot_t(do_ref[span_of(i * CHUNK)], w2_ref[...])
                d_in = (d_act * slope_ref[j, at].astype(f32)).astype(bf16)
                total += jnp.sum(d_in.astype(f32), axis=0, keepdims=True)
                di_ref[at] = d_in
            gb1_ref[:, pl.ds(pl.multiple_of(j * TILE, TILE), TILE)] = total
            value = dot(lowt_ref[...], di_ref[...]).astype(bf16)
            gw1_ref[lax.rem(j, kept)] = value.reshape(lay.dims + (depth, TILE))
            hooks.at(j, range(tiles))
            for i in range(rows // CHUNK):
                at = slice(i * CHUNK, (i + 1) * CHUNK)
                acc_ref[at] += dot_t(di_ref[at], w1_ref[...])

        @pl.when(t == 2 * tiles)
        def _():
            def back(i, carry):
                at = pl.ds(pl.multiple_of(i * 128, 128), 128)
                seq = (i * 128) // span
                there = (seq, pl.ds(pl.multiple_of(i * 128 - seq * span, 128), 128))
                grad, normal = acc_ref[at], d1_ref[at]
                sums_ref[4:5] += jnp.sum(grad * normal, axis=0, keepdims=True)
                sums_ref[5:6] += jnp.sum(grad, axis=0, keepdims=True)
                scaled = grad * gain1
                mean = jnp.mean(scaled, axis=-1, keepdims=True)
                along = jnp.mean(scaled * normal, axis=-1, keepdims=True)
                d_one = inv1_ref[at] * (scaled - mean - normal * along)
                d1_ref[at] = d_one
                db_ref[there] = d_one.astype(bf16)
                return carry

            lax.fori_loop(0, rows // 128, back, 0)

        @pl.when(t > 2 * tiles)
        def _():
            j = t - 2 * tiles - 1
            gw2 = dot(dot_ref[...], act_ref[j]).astype(bf16)
            if wide:
                for d in range(per_tile):
                    gw2_ref[d] = gw2[:, d * share : (d + 1) * share]
            else:
                gw2_ref[...] = gw2
            hooks.at(t - tiles - 1, range(tiles, 2 * tiles))

        @pl.when(t == 2 * tiles + 1)
        def _():
            small_ref[...] = jnp.zeros_like(small_ref)
            loss = jnp.broadcast_to(jnp.sum(sums_ref[0:1], axis=-1, keepdims=True), (1, 128))
            for d in range(devices):
                at = lay.place(d)
                small_ref[at + (slice(0, 5), slice(0, share1))] = sums_ref[1:6, d * share1 : (d + 1) * share1]
                small_ref[at + (slice(5, 6), slice(0, share))] = gb1_ref[:, d * share : (d + 1) * share]
                small_ref[at + (slice(6, 7),)] = loss

        @pl.when(t == 3 * tiles)
        def _():
            save = pltpu.make_async_copy(db_ref, db_out, own.at[pieces])
            save.start()
            for k in range(2 * tiles, last + 1):
                hooks.run(k)
            for part in sums:
                part.drain()
            rows_out.finish()
            save.wait()

    def tile(t, *_):
        return jnp.where(t < tiles, t, jnp.clip(t - tiles - 1, 0, tiles - 1))

    def outer_tile(t, *_):
        return jnp.maximum(t - 2 * tiles - 1, 0)

    full = once((rows, width))
    vec = pl.BlockSpec((1, TILE), lambda t, *_: (0, tile(t)))
    low = pltpu.VMEM((seqs, span, width), bf16)
    return pl.pallas_call(
        kernel,
        grid_spec=pltpu.PrefetchScalarGridSpec(
            num_scalar_prefetch=0,
            grid=(3 * tiles + 1,),
            in_specs=[
                pl.BlockSpec(memory_space=pltpu.SMEM), ANY, ANY, ANY, once((8, width)), vec,
                pl.BlockSpec((width, TILE), lambda t, *_: (0, tile(t))),
                pl.BlockSpec((TILE, width), lambda t, *_: (tile(t), 0)),
            ],
            out_specs=[
                ANY, full, ANY, once((depth, hidden)),
                pl.BlockSpec((per_tile, width, share), lambda t, *_: (outer_tile(t), 0, 0))
                if wide else pl.BlockSpec((width, TILE), lambda t, *_: (0, outer_tile(t))),
                once(lay.dims + (8, 128)),
            ],
            scratch_shapes=[
                low, pltpu.VMEM((width, rows), bf16),
                pltpu.VMEM((tiles, rows, TILE), bf16), pltpu.VMEM((tiles, rows, TILE), bf16),
                pltpu.VMEM((rows, width), f32), low, pltpu.VMEM((width, rows), bf16),
                pltpu.VMEM((rows, 1), f32), pltpu.VMEM((rows, TILE), bf16), low,
                pltpu.VMEM((kept,) + lay.dims + (depth, columns), bf16),
                pltpu.VMEM((8, width), f32), pltpu.VMEM((1, hidden), f32),
            ]
            + sems(lay, 0, 2 * seqs + 1)[3:]
            + sems(lay, pieces + 1, 0)[:3]
            + [b for way in ways for b in Scatter.buffers(lay, (0, depth, 0, columns), bf16, way)],
        ),
        out_shape=[
            jax.ShapeDtypeStruct(teacher.shape, bf16),
            jax.ShapeDtypeStruct((rows, width), f32),
            jax.ShapeDtypeStruct((seqs, span, width), bf16),
            jax.ShapeDtypeStruct((depth, hidden), f32),
            jax.ShapeDtypeStruct((devices, width, share) if wide else (width, hidden), bf16),
            jax.ShapeDtypeStruct(lay.dims + (8, 128), f32),
        ],
        compiler_params=pltpu.CompilerParams(
            collective_id=2, has_side_effects=True, vmem_limit_bytes=63 << 20),
        name="feed_forward",
    )(lengths, h1, teacher, out_grad, vecs, bias_inner, w1, w2)


def finish(d_tokens, small, vecs, share, deep, whole):
    seqs, span, width = d_tokens.shape
    n, steps = len(whole), 2

    def kernel(dx_ref, small_ref, vec_ref, *refs):
        ins, refs = refs[:n], refs[n:]
        dx_out, loss_ref, bias_ref = refs[:3]
        for i, vec in enumerate(refs[3:8]):
            vec[...] = small_ref[i : i + 1, :share]
        for a, b in zip(ins, refs[8:]):
            if a.ndim == 3:
                b[...] = a[...]
            else:
                pl.when(pl.program_id(0) == 0)(lambda a=a, b=b: b.__setitem__(Ellipsis, a[...]))
        loss_ref[...] = small_ref[6:7, :1] * vec_ref[5:6, :1]
        bias_ref[...] = small_ref[5:6, :deep]
        dx_out[...] = dx_ref[...].astype(f32)

    def block(a):
        if a.ndim == 3:
            return pl.BlockSpec((a.shape[0] // steps,) + a.shape[1:], lambda i: (i, 0, 0))
        return once(a.shape)

    like = lambda a, dtype: jax.ShapeDtypeStruct(a.shape, dtype)
    blocks = [block(a) for a in whole]
    out = pl.pallas_call(
        kernel,
        grid=(steps,),
        in_specs=[block(d_tokens), once((8, 128)), once((8, width))] + blocks,
        out_specs=[block(d_tokens), once((1, 1)), once((1, deep))] + [once((1, share))] * 5 + blocks,
        out_shape=[like(d_tokens, f32), jax.ShapeDtypeStruct((1, 1), f32), jax.ShapeDtypeStruct((1, deep), f32)]
        + [jax.ShapeDtypeStruct((1, share), f32)] * 5
        + [like(a, a.dtype) for a in whole],
        compiler_params=pltpu.CompilerParams(vmem_limit_bytes=63 << 20),
        name="finish",
    )(d_tokens, small, vecs, *whole)
    return out[0], out[1], out[2], out[3:8], out[8:]


def cut(shape, which, pieces, orders, columns=False):
    rows, wide = shape
    if columns:
        step = wide // pieces
        return [(which, (0, rows, i * step, step), orders) for i in range(pieces)]
    while pieces > 1 and rows % (pieces * 16):
        pieces -= 1
    step = rows // pieces
    return [(which, (i * step, step), orders) for i in range(pieces)]


def shards(
    lay, tokens, lengths, teacher, out_grad, w_query, w_key, w_value, w_output, gain_one, shift_one,
    w_inner, bias_inner, w_outer, bias_outer, gain_two, shift_two,
):
    width = tokens.shape[2]
    hidden = w_inner.shape[1]
    devices = lay.devices
    there = (("z", "x", "y"), ("z", "y", "x"))
    back = (("y", "x", "z"), ("x", "y", "z"))
    aside = (("x", "y", "z"),) * 2
    share, deep = gain_one.shape[0], bias_inner.shape[0]
    ins = [w_query, w_key, w_value, w_output, w_inner, w_outer]
    parts = [(6, (0, 8), there)]
    for i in range(4):
        parts += cut(ins[i].shape, i, 2, there, True)
    early = len(parts)
    parts += cut(w_inner.shape, 4, 8, there, True) + cut(w_outer.shape, 5, 8, there)
    vectors = [gain_one, shift_one, bias_outer, gain_two, shift_two, bias_inner]
    wq, wk, wv, wo, w1, w2, xt, q, k, v, att, lse, h1, vecs, bias1 = attention_forward(
        lay, tokens, lengths, vectors, ins, parts, early
    )
    wq, wk, wv, wo = (w.reshape(width, width) for w in (wq, wk, wv, wo))
    w1, w2 = w1.reshape(width, hidden), w2.reshape(hidden, width)
    layer_out, d_one, d_branch, g_inner, gw2, small = feed_forward(
        lay, h1, teacher, out_grad, lengths, vecs, bias1, w1, w2, back, aside
    )
    if gw2.ndim == 2:
        gw2 = gw2.T.reshape(devices, hidden // devices, width)
    g_query, g_key, g_value, g_output, g_outer, small, d_tokens = attention_backward(
        lay, xt, lengths, wq, wk, wv, wo, q, k, v, att, lse, d_branch, d_one, gw2, small, back, aside
    )
    d_tokens, loss, g_bias, vec_grads, copied = finish(
        d_tokens, small, vecs, share, deep, [layer_out, g_query, g_key, g_value, g_output, g_inner, g_outer]
    )
    layer_out, g_query, g_key, g_value, g_output, g_inner, g_outer = copied
    vec = lambda i: vec_grads[i][0]
    return (
        loss[0, 0],
        layer_out,
        d_tokens,
        g_query,
        g_key,
        g_value,
        g_output,
        vec(3),
        vec(4),
        g_inner,
        g_bias[0],
        g_outer,
        vec(2),
        vec(0),
        vec(1),
    )


def solution(mesh):
    lay = Layout(mesh)
    rows = P("dp", "blk", None)
    weight = P(("dp", "blk"), None)
    vector = P(("dp", "blk"))
    return jax.shard_map(
        lambda *args: shards(lay, *args),
        mesh=mesh,
        in_specs=(
            rows, P("dp"), rows, rows, weight, weight, weight, weight, vector, vector,
            weight, vector, weight, vector, vector, vector,
        ),
        out_specs=(
            P(), rows, rows, weight, weight, weight, weight, vector, vector,
            weight, vector, weight, vector, vector, vector,
        ),
        check_vma=False,
    )
```
